128 devices in a mesh: dp: 4 (over x), kv: 2 (over core), ctx: 16 (over z, y).
Axes of the slice: x: 4, y: 4, z: 4, core: 2. Of those that a mesh axis runs over, the one named last changes fastest.
Arguments:
- layer_input: bfloat16 [4, 16, 2, 128, 896], P('dp', 'ctx', 'kv'), may hold values from -6 to 6
- cotangent: bfloat16 [4, 16, 2, 128, 896], P('dp', 'ctx', 'kv'), may hold values from -6 to 6
- doc_bounds: int32 [4, 8], P('dp'), may hold values from 0 to 4095, as said below
- w_query: bfloat16 [896, 896], P(None, ('dp', 'kv', 'ctx')), may hold values from -0.1875 to 0.1875
- key_weight: bfloat16 [896, 128], P(None, ('dp', 'kv', 'ctx')), may hold values from -0.1875 to 0.1875
- value_weight: bfloat16 [896, 128], P(None, ('dp', 'kv', 'ctx')), may hold values from -0.1875 to 0.1875
- w_out: bfloat16 [896, 896], P(None, ('dp', 'kv', 'ctx')), may hold values from -0.1875 to 0.1875
- gain_attn_in: float32 [896], replicated, may hold values from 0.5 to 1.5
- gain_attn_out: float32 [896], replicated, may hold values from 0.5 to 1.5
- gain_ffn_in: float32 [896], replicated, may hold values from 0.5 to 1.5
- gain_ffn_out: float32 [896], replicated, may hold values from 0.5 to 1.5
- code_gate: int32 [896, 4864], P(None, 'ctx'), may hold values from -128 to 127
- code_up: int32 [896, 4864], P(None, 'ctx'), may hold values from -128 to 127
- code_down: int32 [4864, 896], P('ctx'), may hold values from -128 to 127
- scale_gate: float32 [4864], P('ctx'), may hold values from 0.00025 to 0.001
- scale_up: float32 [4864], P('ctx'), may hold values from 0.00025 to 0.001
- scale_down: float32 [896], replicated, may hold values from 0.0001 to 0.0004
Outputs:
- block_out: bfloat16 [4, 16, 2, 128, 896], P('dp', 'ctx', 'kv')
- grad_input: float32 [4, 16, 2, 128, 896], P('dp', 'ctx', 'kv')
- grad_query: float32 [896, 896], P(None, ('dp', 'kv', 'ctx'))
- grad_key: float32 [896, 128], P(None, ('dp', 'kv', 'ctx'))
- grad_value: float32 [896, 128], P(None, ('dp', 'kv', 'ctx'))
- grad_out: float32 [896, 896], P(None, ('dp', 'kv', 'ctx'))
- grad_gain_attn_in: float32 [896], replicated
- grad_gain_attn_out: float32 [896], replicated
- grad_gain_ffn_in: float32 [896], replicated
- grad_gain_ffn_out: float32 [896], replicated
- grad_code_gate: float32 [896, 4864], P(None, 'ctx')
- grad_code_up: float32 [896, 4864], P(None, 'ctx')
- grad_code_down: float32 [4864, 896], P('ctx')
- grad_scale_gate: float32 [4864], P('ctx')
- grad_scale_up: float32 [4864], P('ctx')
- grad_scale_down: float32 [896], replicated
The draws below stay inside these ranges and needn't reach their ends.
Inputs may be any that keep to these rules, and one draw needn't show every extreme that they name: In each row the first entry is 0 and the entries rise strictly; document i covers positions doc_bounds[r, i] up to the next entry, or up to 4096. In every row one document starts within the first 256 positions and ends within the last 256.
All inputs are finite; a program needn't handle non-finite values.
Results may differ from the reference program's by a relative error of at most 0.03.
Values may be sent and summed in bfloat16 or wider, within the bound.
No kernel may reach another device: no remote copies, remote signals or barrier semaphores. Data moves between devices by JAX's collectives and lax.ppermute only.
A program may use at most 128 MiB of HBM per device.

```python
import math
import jax
import jax.numpy as jnp
from jax import lax

MODEL_WIDTH = 896
QUERY_HEAD_COUNT = 14
KEY_VALUE_HEADS = 2
HEAD_WIDTH = 64
FF = 4864
DOCS = 8
PACKED_LENGTH = 4096
SPAN = 256
HALF = 128
ROWS = 4
N_KV = 2
N_CTX = 16


def draw_doc_bounds(key, part):
    key = jax.random.fold_in(key, 11)

    def one_row(row_key):
        first_key, second_key, third_key = jax.random.split(row_key, 3)
        left_cuts = jnp.sort(jax.random.permutation(first_key, SPAN - 1)[:DOCS - 1] + 1)
        right_cuts = jnp.sort(jax.random.permutation(second_key, SPAN - 1)[:DOCS - 1] + PACKED_LENGTH - SPAN + 1)
        long_index = jax.random.randint(third_key, (), 1, DOCS)
        token_offsets = jnp.arange(DOCS - 1)
        cuts = jnp.where(token_offsets < long_index, left_cuts, right_cuts)
        return jnp.concatenate([jnp.zeros((1,), jnp.int32), cuts.astype(jnp.int32)])
    return jax.vmap(one_row)(jax.random.split(key, ROWS))


def touch_ends(entries, own_key, least, high):
    extent = entries.shape
    spot = [jax.random.randint(jax.random.fold_in(own_key, axis), (), 0, extent[axis]) for axis in range(len(extent))]
    entries = entries.at[tuple(spot)].set(least)
    longest = extent.index(max(extent))
    spot[longest] = (spot[longest] + 1) % extent[longest]
    return entries.at[tuple(spot)].set(high)


def block_levels(own_key, shape, cuts, low, high):
    factor_of = 1.0
    for dim, blocks in cuts:
        draws = jax.random.uniform(jax.random.fold_in(jax.random.fold_in(own_key, 6), dim), (blocks,), jnp.float32, low / len(cuts), high / len(cuts))
        factor_of = factor_of * jnp.repeat(jnp.exp(draws), shape[dim] // blocks).reshape((-1,) + (1,) * (len(shape) - 1 - dim))
    return factor_of


def normal_values(rng, extent, deviation, most, shards=(), held_as=jnp.bfloat16):
    array = deviation * jax.random.normal(rng, extent, jnp.float32)
    if shards:
        array = array * block_levels(rng, extent, shards, -0.22, 0.18)
    return jnp.clip(array, -most, most).astype(held_as)


def setup_inputs(seed: int = 0) -> dict:
    keys = jax.random.split(jax.random.key(seed), 18)
    return {
        "layer_input": normal_values(keys[0], (ROWS, N_CTX, N_KV, HALF, MODEL_WIDTH), 1.0, 6.0, ((0, 4), (1, 16), (2, 2))),
        "cotangent": normal_values(keys[1], (ROWS, N_CTX, N_KV, HALF, MODEL_WIDTH), 1.0, 6.0, ((0, 4), (1, 16), (2, 2))),
        "doc_bounds": draw_doc_bounds(jax.random.fold_in(keys[17], 71), 0),
        "w_query": normal_values(keys[3], (MODEL_WIDTH, QUERY_HEAD_COUNT * HEAD_WIDTH), MODEL_WIDTH ** -0.5, 0.1875, ((1, 128),)),
        "key_weight": normal_values(keys[4], (MODEL_WIDTH, KEY_VALUE_HEADS * HEAD_WIDTH), MODEL_WIDTH ** -0.5, 0.1875, ((1, 128),)),
        "value_weight": normal_values(keys[5], (MODEL_WIDTH, KEY_VALUE_HEADS * HEAD_WIDTH), MODEL_WIDTH ** -0.5, 0.1875, ((1, 128),)),
        "w_out": normal_values(keys[6], (MODEL_WIDTH, QUERY_HEAD_COUNT * HEAD_WIDTH), (QUERY_HEAD_COUNT * HEAD_WIDTH) ** -0.5, 0.1875, ((1, 128),)),
        "gain_attn_in": jnp.clip(1.0 + 0.1 * jax.random.normal(keys[7], (MODEL_WIDTH,), jnp.float32), 0.5, 1.5),
        "gain_attn_out": jnp.clip(1.0 + 0.1 * jax.random.normal(keys[8], (MODEL_WIDTH,), jnp.float32), 0.5, 1.5),
        "gain_ffn_in": jnp.clip(1.0 + 0.1 * jax.random.normal(keys[9], (MODEL_WIDTH,), jnp.float32), 0.5, 1.5),
        "gain_ffn_out": jnp.clip(1.0 + 0.1 * jax.random.normal(keys[10], (MODEL_WIDTH,), jnp.float32), 0.5, 1.5),
        "code_gate": touch_ends(jax.random.randint(keys[11], (MODEL_WIDTH, FF), -128, 128), jax.random.fold_in(keys[11], 1), -128, 127).astype(jnp.int32),
        "code_up": touch_ends(jax.random.randint(keys[12], (MODEL_WIDTH, FF), -128, 128), jax.random.fold_in(keys[12], 1), -128, 127).astype(jnp.int32),
        "code_down": touch_ends(jax.random.randint(keys[13], (FF, MODEL_WIDTH), -128, 128), jax.random.fold_in(keys[13], 1), -128, 127).astype(jnp.int32),
        "scale_gate": jnp.clip(jnp.exp(math.log(0.001) - 1.3862944 * jax.random.uniform(keys[14], (FF,), jnp.float32) ** block_levels(keys[14], (FF,), ((0, 16),), -0.2, 0.2)), 0.00025, 0.001),
        "scale_up": jnp.clip(jnp.exp(math.log(0.001) - 1.3862944 * jax.random.uniform(keys[15], (FF,), jnp.float32) ** block_levels(keys[15], (FF,), ((0, 16),), -0.2, 0.2)), 0.00025, 0.001),
        "scale_down": jnp.clip(jnp.exp(jax.random.uniform(keys[16], (MODEL_WIDTH,), jnp.float32, math.log(0.0001), math.log(0.0004))), 0.0001, 0.0004),
    }


EPS = 1e-06
CAP = 50.0
NEG = -1e+30
HIGH = lax.Precision.HIGHEST
QSCALE = 0.125

@jax.custom_vjp
def lowered_forward(v):
    return lax.optimization_barrier(v.astype(jnp.bfloat16)).astype(jnp.float32)

@jax.custom_vjp
def lowered_backward(v):
    return v

def low_keep(v):
    return (lowered_forward(v), None)

def low_pass(kept, grad):
    return (grad,)

def back_keep(v):
    return (v, None)

def back_low(kept, grad):
    return (lowered_forward(grad),)
lowered_forward.defvjp(low_keep, low_pass)
lowered_backward.defvjp(back_keep, back_low)

def scores_product(left, right):
    return jnp.dot(left, right, precision=HIGH)

def norm_rows(value_rows, gain):
    return value_rows * lax.rsqrt(lax.optimization_barrier(jnp.mean(value_rows * value_rows, axis=-1, keepdims=True)) + EPS) * gain

def doc_segment(bounds, token_offsets):
    before = bounds[None, :] <= token_offsets[:, None]
    return lax.optimization_barrier(jnp.sum(before.astype(jnp.int32), axis=1))

def doc_position(bounds, token_offsets):
    before = bounds[None, :] <= token_offsets[:, None]
    return token_offsets - lax.optimization_barrier(jnp.max(jnp.where(before, bounds[None, :], 0), axis=1))

def rotary_tables(position):
    half_dim = HEAD_WIDTH // 2
    freq = jnp.exp(jnp.arange(half_dim, dtype=jnp.float32) * (-2.0 * math.log(10000.0) / HEAD_WIDTH))
    angle = position.astype(jnp.float32)[:, None] * freq[None, :]
    return (jnp.cos(angle)[:, None, :], jnp.sin(angle)[:, None, :])

def apply_rotary(value_rows, cosine_table, sine_table):
    half_dim = value_rows.shape[-1] // 2
    first = value_rows[..., :half_dim]
    second = value_rows[..., half_dim:]
    return jnp.concatenate([first * cosine_table - second * sine_table, second * cosine_table + first * sine_table], axis=-1)

def sliced(codes, bits):
    if bits == 8:
        return codes
    step_size = 2 ** (8 - bits)
    return codes // step_size * step_size + step_size // 2

def forward_row(params, x_row, document_ids, token_offsets, position, offsets):
    w_query, key_weight, value_weight, w_out, gain_attn_in, gain_attn_out, gain_ffn_in, gain_ffn_out, code_gate, code_up, code_down, scale_gate, scale_up, scale_down = params
    cosine_table, sine_table = rotary_tables(position)
    normalized_rows = lowered_forward(norm_rows(x_row, gain_attn_in))
    query_rows = lowered_forward(apply_rotary(lowered_backward(scores_product(normalized_rows, w_query)).reshape(PACKED_LENGTH, QUERY_HEAD_COUNT, HEAD_WIDTH), cosine_table, sine_table) * QSCALE)
    key_rows = lowered_forward(apply_rotary(lowered_backward(scores_product(normalized_rows, key_weight)).reshape(PACKED_LENGTH, KEY_VALUE_HEADS, HEAD_WIDTH), cosine_table, sine_table))
    value_rows = lowered_forward(lowered_backward(scores_product(normalized_rows, value_weight))).reshape(PACKED_LENGTH, KEY_VALUE_HEADS, HEAD_WIDTH)
    heads_per_group = QUERY_HEAD_COUNT // KEY_VALUE_HEADS
    block_length = 512 if PACKED_LENGTH % 512 == 0 else PACKED_LENGTH
    block_count = PACKED_LENGTH // block_length

    def attend_heads(block_in):
        query_block, seg_block, place_block = block_in
        scores = lowered_backward(jnp.einsum('tgqd,sgd->gqts', query_block, key_rows, precision=HIGH))
        allowed = (document_ids[None, :] == seg_block[:, None]) & (token_offsets[None, :] <= place_block[:, None])
        capped = jnp.where(allowed[None, None], CAP * jnp.tanh(scores / CAP), NEG)
        probs = lowered_forward(jax.nn.softmax(capped, axis=-1))
        return jnp.einsum('gqts,sgd->tgqd', probs, value_rows, precision=HIGH)
    attended_rows = lax.map(jax.checkpoint(attend_heads), (query_rows.reshape(block_count, block_length, KEY_VALUE_HEADS, heads_per_group, HEAD_WIDTH), document_ids.reshape(block_count, block_length), token_offsets.reshape(block_count, block_length)))
    mixed = lowered_backward(lowered_forward(attended_rows.reshape(PACKED_LENGTH, QUERY_HEAD_COUNT * HEAD_WIDTH)))
    attn_out = lowered_backward(jnp.dot(mixed, w_out.T, precision=HIGH))
    resid = x_row + norm_rows(attn_out, gain_attn_out)
    ffn_in = lowered_forward(norm_rows(resid, gain_ffn_in))
    w_gate = lowered_forward(scale_gate[None, :] * (code_gate + offsets[0]))
    w_up = lowered_forward(scale_up[None, :] * (code_up + offsets[1]))
    w_down = lowered_forward(scale_down[None, :] * (code_down + offsets[2]))
    gate_pre = lowered_backward(scores_product(ffn_in, w_gate))
    up_pre = lowered_backward(scores_product(ffn_in, w_up))
    hidden = lowered_forward(jax.nn.gelu(gate_pre, approximate=True) * up_pre)
    ffn_out = lowered_backward(scores_product(hidden, w_down))
    return resid + norm_rows(ffn_out, gain_ffn_out)

def reference(layer_input, cotangent, doc_bounds, w_query, key_weight, value_weight, w_out, gain_attn_in, gain_attn_out, gain_ffn_in, gain_ffn_out, code_gate, code_up, code_down, scale_gate, scale_up, scale_down):
    rows_in = layer_input.reshape(ROWS, PACKED_LENGTH, MODEL_WIDTH).astype(jnp.float32)
    rows_cot = cotangent.reshape(ROWS, PACKED_LENGTH, MODEL_WIDTH).astype(jnp.float32)
    offsets = ((sliced(code_gate, 8) - code_gate).astype(jnp.float32), (sliced(code_up, 4) - code_up).astype(jnp.float32), (sliced(code_down, 2) - code_down).astype(jnp.float32))
    params = (w_query.astype(jnp.float32), key_weight.astype(jnp.float32), value_weight.astype(jnp.float32), w_out.astype(jnp.float32), gain_attn_in, gain_attn_out, gain_ffn_in, gain_ffn_out, code_gate.astype(jnp.float32), code_up.astype(jnp.float32), code_down.astype(jnp.float32), scale_gate, scale_up, scale_down)
    token_offsets = jnp.arange(PACKED_LENGTH, dtype=jnp.int32)

    def one_row(totals, row_in):
        x_row, cot_row, bounds = row_in
        document_ids = doc_segment(bounds, token_offsets)
        position = doc_position(bounds, token_offsets)
        out_row, pullback = jax.vjp(lambda weights, inputs: forward_row(weights, inputs, document_ids, token_offsets, position, offsets), params, x_row)
        grads, grad_row = pullback(cot_row)
        return (jax.tree.map(jnp.add, totals, grads), (out_row.astype(jnp.bfloat16), grad_row))
    totals, (outputs, grad_rows) = lax.scan(one_row, jax.tree.map(jnp.zeros_like, params), (rows_in, rows_cot, doc_bounds))
    shape_out = (ROWS, N_CTX, N_KV, HALF, MODEL_WIDTH)
    return (outputs.reshape(shape_out), grad_rows.reshape(shape_out), totals[0], totals[1], totals[2], totals[3], totals[4], totals[5], totals[6], totals[7], totals[8], totals[9], totals[10], totals[11], totals[12], totals[13])
```

```python
import math

import jax
import jax.numpy as jnp
from jax import lax
from jax.experimental import pallas as pl
from jax.experimental.pallas import tpu as pltpu
from jax.sharding import PartitionSpec as P

EPS = 1e-06
CAP = 50.0
QSCALE = 0.125
GELU_C = math.sqrt(2.0 / math.pi)
EXP2 = CAP * math.log2(math.e)

TOK = 128
SPAN = 256
WIDTH = 896
HEAD = 64
GROUP = 7
QCOL = 512
KVCOL = 640
SIDE = 4
UNITS = 304
UPAD = 320
HALF_UNITS = 160
HID = 1280
BLOCKS = 16
F32 = jnp.float32
BF16 = jnp.bfloat16
VMEM = pl.BlockSpec(memory_space=pltpu.VMEM)
SMEM = pl.BlockSpec(memory_space=pltpu.SMEM)
ANY = pl.BlockSpec(memory_space=pl.ANY)


def kernel_call(body, out, name, scratch=(), in_specs=None, count=None, us=2.0):
    out = [jax.ShapeDtypeStruct(s, d) for s, d in out]
    return pl.pallas_call(
        body,
        out_shape=out,
        in_specs=in_specs if in_specs is not None else [VMEM] * count,
        out_specs=[VMEM] * len(out),
        scratch_shapes=list(scratch),
        compiler_params=pltpu.CompilerParams(vmem_limit_bytes=48 * 1024 * 1024),
        cost_estimate=pl.CostEstimate(flops=int(us * 1e9), bytes_accessed=0, transcendentals=0),
        name=name,
    )


def dot(left, right):
    return lax.dot_general(left, right, (((1,), (0,)), ((), ())), preferred_element_type=F32)


def dot_right(left, right):
    return lax.dot_general(left, right, (((1,), (1,)), ((), ())), preferred_element_type=F32)


def dot_left(left, right):
    return lax.dot_general(left, right, (((0,), (0,)), ((), ())), preferred_element_type=F32)


def from_core(x):
    return lax.ppermute(x, "kv", [(0, 1), (1, 0)])


def back_x(x, k):
    return lax.ppermute(x, "dp", [(i, (i + k) % SIDE) for i in range(SIDE)])


def back_y(x, k):
    pairs = [(z * SIDE + y, z * SIDE + (y + k) % SIDE) for z in range(SIDE) for y in range(SIDE)]
    return lax.ppermute(x, "ctx", pairs)


def back_z(x, k):
    pairs = [(z * SIDE + y, (z + k) % SIDE * SIDE + y) for z in range(SIDE) for y in range(SIDE)]
    return lax.ppermute(x, "ctx", pairs)


def group_round(x, i, back=False):
    pairs = [(n, 2 * ((n % 4 + i) % SIDE) + n // 4) for n in range(8)]
    if back:
        pairs = [(b, a) for a, b in pairs]
    return lax.ppermute(x, ("dp", "kv"), pairs)


def ring(send, x):
    got = {k: send(x, k) for k in (1, 3, 2)}
    return [x, got[1], got[2], got[3]]


def ring_back(send, parts):
    got = {k: send(parts[k], SIDE - k) for k in (1, 3, 2)}
    return [parts[0], got[1], got[2], got[3]]


def total_all(x):
    x = x + from_core(x)
    for send in (back_x, back_y, back_z):
        a, b, c, d = ring(send, x)
        x = (a + c) + (b + d)
    return x


def norm_rows(rows, gain):
    inverse = lax.rsqrt(jnp.mean(rows * rows, axis=-1, keepdims=True) + EPS)
    return rows * inverse * gain, inverse


def norm_back(rows, gain, incoming):
    inverse = lax.rsqrt(jnp.mean(rows * rows, axis=-1, keepdims=True) + EPS)
    normed = rows * inverse
    scaled = incoming * gain
    grad = inverse * (scaled - normed * jnp.mean(scaled * normed, axis=-1, keepdims=True))
    return grad, jnp.sum(incoming * normed, axis=0, keepdims=True)


def lane(shape):
    return lax.broadcasted_iota(jnp.int32, shape, len(shape) - 1)


def swap_halves(x):
    return jnp.where(lane(x.shape) % HEAD < HEAD // 2, pltpu.roll(x, 96, 1), pltpu.roll(x, 32, 1))


def qkv_kernel(a0, a1, w0, w1, w2, w3, w4, w5, w6, w7, order, cosine, sine, q_out, kv_out, w_out, all_w):
    for j, w in enumerate((w0, w1, w2, w3, w4, w5, w6, w7)):
        all_w[pl.ds(TOK * j, TOK), :] = w[...]
    w_cols = dot(order[...], all_w[...]).astype(BF16)
    w_out[...] = w_cols
    rows = jnp.concatenate([a0[...], a1[...]], axis=0)
    raw = dot_right(rows, w_cols)
    cos, sin = cosine[...], sine[...]
    low = lane((SPAN, 128)) < HEAD
    for j in range(4):
        u = raw[:, 128 * j : 128 * (j + 1)]
        u = (u * cos + swap_halves(u) * sin) * QSCALE
        q_out[2 * j] = jnp.where(low, u, 0.0).astype(BF16)
        if j < 3:
            q_out[2 * j + 1] = jnp.where(low, pltpu.roll(u, HEAD, 1), 0.0).astype(BF16)
    u = raw[:, QCOL:KVCOL]
    kv_out[...] = jnp.where(low, u * cos + swap_halves(u) * sin, u).astype(BF16)


def order_kernel(w0, w1, w2, w3, w4, w5, w6, w7, order, w_out, all_w):
    for j, w in enumerate((w0, w1, w2, w3, w4, w5, w6, w7)):
        all_w[pl.ds(TOK * j, TOK), :] = w[...]
    w_out[...] = dot(order[...], all_w[...]).astype(BF16)


def doc_start(place, p):
    start = jnp.int32(0)
    for i in range(8):
        b = place[4 + i]
        start = jnp.where(b <= p, jnp.maximum(start, b), start)
    return start


def load_blocks(pieces, blocks, sems):
    copies = []
    for j in range(SIDE):
        copies.append(pltpu.make_async_copy(pieces[j], blocks.at[j, :, pl.ds(0, TOK), :], sems.at[j]))
        copies.append(
            pltpu.make_async_copy(pieces[4 + j], blocks.at[:, j, pl.ds(TOK, TOK), :], sems.at[4 + j])
        )
    for c in copies:
        c.start()
    return copies


def block_ranges(place, n):
    kz, ky = n // SIDE, n % SIDE
    source = ((place[1] - kz) & 3) * SIDE + ((place[2] - ky) & 3)
    first = place[0] * SPAN
    low_start, high_start = doc_start(place, first), doc_start(place, first + SPAN - 1)
    active = (source <= place[0]) & (source * SPAN + SPAN - 1 >= low_start)
    full = (source < place[0]) & (source * SPAN >= high_start)
    return kz, ky, source, active, full


def span_places(shape, dim, chip, kv):
    i = lax.broadcasted_iota(jnp.int32, shape, dim)
    half = jnp.where(i < TOK, kv, 1 - kv)
    return chip * SPAN + half * TOK + i % TOK


def query_places(place, pos_ref, start_ref):
    pos = span_places((SPAN, SPAN), 0, place[0], place[3])
    start = jnp.zeros((SPAN, SPAN), jnp.int32)
    for i in range(8):
        b = place[4 + i]
        start = jnp.where(pos >= b, jnp.maximum(start, b), start)
    pos_ref[...] = pos
    start_ref[...] = start


def allowed_keys(place, source, pos_ref, start_ref):
    keys = span_places((SPAN, SPAN), 1, source, place[3])
    return (keys <= pos_ref[...]) & (keys >= start_ref[...])


def attend_kernel(
    place, q, p0, p1, p2, p3, p4, p5, p6, p7, wo, o_out, inv_out, own_out, other_out, blocks, acc, pos_ref, start_ref, sems
):
    copies = load_blocks((p0, p1, p2, p3, p4, p5, p6, p7), blocks, sems)
    query_places(place, pos_ref, start_ref)
    acc[...] = jnp.zeros_like(acc)
    for c in copies:
        c.wait()
    low = lane((SPAN, 128)) < HEAD

    @pl.loop(0, BLOCKS)
    def _(n):
        kz, ky, source, active, full = block_ranges(place, n)

        def step(masked):
            kv = blocks[kz, ky]
            ones_v = jnp.where(low, jnp.ones_like(kv), kv)
            if masked:
                allowed = allowed_keys(place, source, pos_ref, start_ref)
            for h in range(GROUP):
                s = dot_right(q[h], kv)
                p = jnp.exp2(jnp.tanh(s * (1.0 / CAP)) * EXP2)
                if masked:
                    p = jnp.where(allowed, p, 0.0)
                acc[h] += dot(p.astype(BF16), ones_v)

        pl.when(full)(lambda: step(False))
        pl.when(active & jnp.logical_not(full))(lambda: step(True))

    for j in range(4):
        a = acc[2 * j]
        if j < 3:
            b = acc[2 * j + 1]
            total = jnp.where(low, a, pltpu.roll(b, HEAD, 1))
            value = jnp.where(low, pltpu.roll(a, HEAD, 1), b)
        else:
            total = jnp.where(low, a, 1.0)
            value = jnp.where(low, pltpu.roll(a, HEAD, 1), 0.0)
        inv = 1.0 / total
        inv_out[:, 128 * j : 128 * (j + 1)] = inv
        o_out[:, 128 * j : 128 * (j + 1)] = value * inv
    attn = dot(o_out[...].astype(BF16), wo[...])
    own_out[...] = attn[:TOK]
    other_out[...] = attn[TOK:].astype(BF16)


def attend_back_kernel(
    place, q, p0, p1, p2, p3, p4, p5, p6, p7, wo, d0, d1, o, inv, cosine, sine,
    dq_out, k0, k1, k2, k3, k4, k5, k6, k7,
    blocks, grads, dq, do_ext, both_t, pos_ref, start_ref, sems,
):
    copies = load_blocks((p0, p1, p2, p3, p4, p5, p6, p7), blocks, sems)
    query_places(place, pos_ref, start_ref)
    dq[...] = jnp.zeros_like(dq)
    rows = jnp.concatenate([d0[...], d1[...]], axis=0)
    d_o = dot_right(rows, wo[...]).astype(BF16).astype(F32)
    low = lane((SPAN, 128)) < HEAD
    lanes = lane((SPAN, 128))
    for h in range(GROUP):
        j = h // 2
        cols = slice(128 * j, 128 * (j + 1))
        mine = low if h % 2 == 0 else jnp.logical_not(low)
        part, scale = d_o[:, cols], inv[:, cols]
        delta = jnp.sum(jnp.where(mine, part * o[:, cols] * scale, 0.0), axis=1, keepdims=True)
        up = part * scale
        if h % 2 == 0:
            up = pltpu.roll(up, HEAD, 1)
        high = delta.astype(BF16).astype(F32)
        ext = jnp.where(lanes == 0, -high, jnp.where(lanes == 1, high - delta, jnp.where(low, 0.0, up)))
        do_ext[h] = ext.astype(BF16)
        both_t[h] = jnp.transpose(jnp.where(low, q[h].astype(F32), up)).astype(BF16)
    for c in copies:
        c.wait()

    @pl.loop(0, BLOCKS)
    def _(n):
        kz, ky, source, active, full = block_ranges(place, n)

        def step(masked):
            kv = blocks[kz, ky]
            ones_v = jnp.where(low, jnp.ones_like(kv), kv)
            if masked:
                allowed = allowed_keys(place, source, pos_ref, start_ref)
            dk = jnp.zeros((HEAD, SPAN), F32)
            dv = jnp.zeros((HEAD, SPAN), F32)
            for h in range(GROUP):
                s = dot_right(q[h], kv)
                dp = dot_right(do_ext[h], ones_v)
                t = jnp.tanh(s * (1.0 / CAP))
                p = jnp.exp2(t * EXP2)
                if masked:
                    p = jnp.where(allowed, p, 0.0)
                ds = (p * dp * (1.0 - t * t)).astype(BF16)
                dq[h] += dot(ds, kv)
                dk += dot(both_t[h, pl.ds(0, HEAD), :], ds)
                dv += dot(both_t[h, pl.ds(HEAD, HEAD), :], p.astype(BF16))
            grads[kz, ky] = jnp.concatenate([dk, dv], axis=0).astype(BF16)

        pl.when(full)(lambda: step(False))
        pl.when(active & jnp.logical_not(full))(lambda: step(True))

        @pl.when(jnp.logical_not(active))
        def _():
            grads[kz, ky] = jnp.zeros((128, SPAN), BF16)

    for j, out in enumerate((k0, k1, k2, k3)):
        out[...] = grads[j, :, :, pl.ds(0, TOK)]
    for j, out in enumerate((k4, k5, k6, k7)):
        out[...] = grads[:, j, :, pl.ds(TOK, TOK)]
    cos, sin = cosine[...], sine[...]
    for j in range(4):
        u = dq[2 * j]
        if j < 3:
            u = jnp.where(low, u, pltpu.roll(dq[2 * j + 1], HEAD, 1))
        else:
            u = jnp.where(low, u, 0.0)
        u = u * QSCALE
        dq_out[:, 128 * j : 128 * (j + 1)] = (u * cos - swap_halves(u) * sin).astype(BF16)


def project_back_kernel(
    dq, s0, s1, s2, s3, t0, t1, t2, t3, cosine, sine, w, a0, a1, d0, d1, o, order,
    own_out, other_out, g0, g1, g2, g3, g4, g5, g6, g7, left,
):
    first = (s0[...].astype(F32) + s1[...].astype(F32)) + (s2[...].astype(F32) + s3[...].astype(F32))
    second = (t0[...].astype(F32) + t1[...].astype(F32)) + (t2[...].astype(F32) + t3[...].astype(F32))
    u = jnp.concatenate([jnp.transpose(first), jnp.transpose(second)], axis=0)
    low = lane((SPAN, 128)) < HEAD
    dkv = jnp.where(low, u * cosine[...] - swap_halves(u) * sine[...], u).astype(BF16)
    grads = jnp.concatenate([dq[...], dkv], axis=1)
    d_a = dot(grads, w[...])
    own_out[...] = d_a[:TOK]
    other_out[...] = d_a[TOK:].astype(BF16)
    left[pl.ds(0, SPAN), :] = dot(grads, order[pl.ds(0, KVCOL), :]).astype(BF16)
    left[pl.ds(SPAN, SPAN), :] = dot(o[...].astype(BF16), order[pl.ds(KVCOL, QCOL), :]).astype(BF16)
    right = jnp.concatenate([a0[...], a1[...], d0[...], d1[...]], axis=0)
    for j, out in enumerate((g0, g1, g2, g3, g4, g5, g6, g7)):
        out[...] = dot_left(left[:, 128 * j : 128 * (j + 1)], right).astype(BF16)


def attn_norm_kernel(x, own, other, gain_b, gain_c, attn_out, r_out, m_out):
    attn = own[...] + other[...].astype(F32)
    attn_out[...] = attn
    resid = x[...].astype(F32) + norm_rows(attn, gain_b[...])[0]
    r_out[...] = resid
    m_out[...] = norm_rows(resid, gain_c[...])[0].astype(BF16)


def sum_parts(own, b, c, d):
    return (own[...] + b[...].astype(F32)) + (c[...].astype(F32) + d[...].astype(F32))


def ffn_norm_kernel(own, b, c, d, resid, cotangent, gain, out, d_out, gain_out):
    fo = sum_parts(own, b, c, d)
    out[...] = (resid[...] + norm_rows(fo, gain[...])[0]).astype(BF16)
    grad, gain_grad = norm_back(fo, gain[...], cotangent[...].astype(F32))
    d_out[...] = grad.astype(BF16)
    gain_out[...] = gain_grad


def ffn_back_norm_kernel(own, b, c, d, resid, attn, cotangent, gain_c, gain_b, r_out, d_out, gain_c_out, gain_b_out):
    d_m = sum_parts(own, b, c, d)
    grad, gain_grad = norm_back(resid[...], gain_c[...], d_m)
    gain_c_out[...] = gain_grad
    d_resid = cotangent[...].astype(F32) + grad
    r_out[...] = d_resid
    grad, gain_grad = norm_back(attn[...], gain_b[...], d_resid)
    gain_b_out[...] = gain_grad
    d_out[...] = grad.astype(BF16)


def input_norm_kernel(own, other, x, d_resid, gain, out, gain_out):
    d_a = own[...] + other[...].astype(F32)
    grad, gain_grad = norm_back(x[...].astype(F32), gain[...], d_a)
    gain_out[...] = gain_grad
    out[...] = d_resid[...] + grad


def gelu_parts(u):
    t = jnp.tanh(GELU_C * (u + 0.044715 * u * u * u))
    active = 0.5 * u * (1.0 + t)
    slope = 0.5 * (1.0 + t) + 0.5 * u * (1.0 - t * t) * GELU_C * (1.0 + 3.0 * 0.044715 * u * u)
    return active, slope


def weight_copies(pieces, dest, sems, which):
    copies = []
    for j, piece in enumerate(pieces):
        copies.append(
            pltpu.make_async_copy(
                piece.at[pl.ds(which * HALF_UNITS, HALF_UNITS), :],
                dest.at[pl.ds(j * HALF_UNITS, HALF_UNITS), :],
                sems.at[which * 8 + j],
            )
        )
    for c in copies:
        c.start()
    return copies


def ffn_kernel(
    m0, m1, m2, m3, w0, w1, w2, w3, w4, w5, w6, w7, f0, f1, f2, f3, gate_out, up_out,
    m, gate_w, up_w, down_w, acc, sems,
):
    pieces = (w0, w1, w2, w3, w4, w5, w6, w7)
    gates = weight_copies(pieces, gate_w, sems, 0)
    ups = weight_copies(pieces, up_w, sems, 1)
    downs = weight_copies(pieces, down_w, sems, 2)
    for j, part in enumerate((m0, m1, m2, m3)):
        m[pl.ds(TOK * j, TOK), :] = part[...]
    for c in gates + ups + downs:
        c.wait()
    for n in range(HID // 256):
        units = pl.ds(256 * n, 256)
        gate = dot_right(m[...], gate_w[units, :])
        up = dot_right(m[...], up_w[units, :])
        gate_out[:, 256 * n : 256 * (n + 1)] = gate.astype(BF16)
        up_out[:, 256 * n : 256 * (n + 1)] = up.astype(BF16)
        hidden = (gelu_parts(gate)[0] * up).astype(BF16)
        part = dot(hidden, down_w[units, :])
        if n == 0:
            acc[...] = part
        else:
            acc[...] += part
    f0[...] = acc[pl.ds(0, TOK), :]
    for j, out in enumerate((f1, f2, f3)):
        out[...] = acc[pl.ds(TOK * (j + 1), TOK), :].astype(BF16)


def ffn_back_kernel(
    e0, e1, e2, e3, gate_in, up_in, w0, w1, w2, w3, w4, w5, w6, w7, f0, f1, f2, f3, hidden_out, gate_out, up_out,
    e, gate_w, up_w, down_w, acc, sems,
):
    pieces = (w0, w1, w2, w3, w4, w5, w6, w7)
    downs = weight_copies(pieces, down_w, sems, 2)
    gates = weight_copies(pieces, gate_w, sems, 0)
    ups = weight_copies(pieces, up_w, sems, 1)
    for j, part in enumerate((e0, e1, e2, e3)):
        e[pl.ds(TOK * j, TOK), :] = part[...]
    for c in downs + gates + ups:
        c.wait()
    for n in range(HID // 256):
        units = pl.ds(256 * n, 256)
        cols = slice(256 * n, 256 * (n + 1))
        d_hidden = dot_right(e[...], down_w[units, :])
        active, slope = gelu_parts(gate_in[:, cols].astype(F32))
        up = up_in[:, cols].astype(F32)
        hidden_out[:, cols] = (active * up).astype(BF16)
        d_gate = (d_hidden * up * slope).astype(BF16)
        d_up = (d_hidden * active).astype(BF16)
        gate_out[:, cols] = d_gate
        up_out[:, cols] = d_up
        part = dot(d_gate, gate_w[units, :]) + dot(d_up, up_w[units, :])
        if n == 0:
            acc[...] = part
        else:
            acc[...] += part
    f0[...] = acc[pl.ds(0, TOK), :]
    for j, out in enumerate((f1, f2, f3)):
        out[...] = acc[pl.ds(TOK * (j + 1), TOK), :].astype(BF16)


def ffn_weight_kernel(
    m0, m1, m2, m3, e0, e1, e2, e3, hidden, d_gate, d_up, own0, own1, own2, own3, other0, other1, other2, other3, m, e
):
    for j, (a, b) in enumerate(zip((m0, m1, m2, m3), (e0, e1, e2, e3))):
        m[pl.ds(TOK * j, TOK), :] = a[...]
        e[pl.ds(TOK * j, TOK), :] = b[...]
    outs = (own0, own1, own2, own3, other0, other1, other2, other3)
    for which, (left, right) in enumerate(((d_gate, m), (d_up, m), (hidden, e))):
        for n in range(HID // 256):
            part = dot_left(left[:, 256 * n : 256 * (n + 1)], right[...]).astype(BF16)
            at = 256 * n
            while at < 256 * (n + 1):
                piece, row = at // HALF_UNITS, at % HALF_UNITS
                count = min(HALF_UNITS - row, 256 * (n + 1) - at)
                outs[piece][pl.ds(which * HALF_UNITS + row, count), :] = part[at - 256 * n : at - 256 * n + count]
                at += count


def slices(codes, bits):
    if bits == 8:
        return codes
    step = 2 ** (8 - bits)
    return codes // step * step + step // 2


def shards(
    layer_input, cotangent, doc_bounds, w_query, key_weight, value_weight, w_out,
    gain_attn_in, gain_attn_out, gain_ffn_in, gain_ffn_out,
    code_gate, code_up, code_down, scale_gate, scale_up, scale_down,
):
    ctx, kv, dp = lax.axis_index("ctx"), lax.axis_index("kv"), lax.axis_index("dp")
    z, y = ctx // SIDE, ctx % SIDE
    place = jnp.concatenate([jnp.stack([ctx, z, y, kv]).astype(jnp.int32), doc_bounds[0]])
    x = layer_input.reshape(TOK, WIDTH)
    cot = cotangent.reshape(TOK, WIDTH)
    gain_1, gain_2, gain_3, gain_4 = (
        g.reshape(1, WIDTH) for g in (gain_attn_in, gain_attn_out, gain_ffn_in, gain_ffn_out)
    )

    shard = jnp.concatenate([w_query.T, key_weight.T, value_weight.T, w_out.T], axis=0)
    rounds = [group_round(shard, i) for i in range(4)]
    first = jnp.concatenate(rounds[:2], axis=0)
    second = jnp.concatenate(rounds[2:], axis=0)
    first = jnp.concatenate(ring(back_y, first), axis=0)
    second = jnp.concatenate(ring(back_z, second), axis=0)
    pieces = ring(back_z, first) + ring(back_y, second)

    row = jnp.arange(1024, dtype=jnp.int32)
    piece, outer, inner, kind = row // 128, row // 32 % 4, row // 16 % 2, row % 16
    by_z = piece < 4
    kz = jnp.where(by_z, piece, outer)
    ky = jnp.where(by_z, outer, piece - 4)
    i = jnp.where(by_z, inner, inner + 2)
    col = ((dp - i) & 3) * 16 + ((z - kz) & 3) * SIDE + ((y - ky) & 3)
    target = jnp.where(
        kind < 7,
        7 * col + kind,
        jnp.where(kind == 7, QCOL + col, jnp.where(kind == 8, QCOL + HEAD + col, KVCOL + 7 * col + kind - 9)),
    )
    order = (target[None, :] == jnp.arange(KVCOL + QCOL, dtype=jnp.int32)[:, None]).astype(BF16)

    spot = jnp.arange(SPAN, dtype=jnp.int32)
    spot = ctx * SPAN + jnp.where(spot < TOK, kv, 1 - kv) * TOK + spot % TOK
    before = doc_bounds[0][None, :] <= spot[:, None]
    position = spot - jnp.max(jnp.where(before, doc_bounds[0][None, :], 0), axis=1)
    freq = jnp.exp(jnp.arange(HEAD // 2, dtype=F32) * (-2.0 * math.log(10000.0) / HEAD))
    angle = position.astype(F32)[:, None] * freq[None, :]
    cos, sin = jnp.cos(angle), jnp.sin(angle)
    cosine = jnp.concatenate([cos] * 4, axis=1)
    sine = jnp.concatenate([-sin, sin] * 2, axis=1)

    a_own = norm_rows(x.astype(F32), gain_1)[0].astype(BF16)
    a_other = from_core(a_own)
    q, kv_own, w_qkv = kernel_call(
        qkv_kernel,
        [((8, SPAN, 128), BF16), ((SPAN, 128), BF16), ((KVCOL, WIDTH), BF16)],
        "qkv",
        [pltpu.VMEM((1024, WIDTH), BF16)],
        count=13,
        us=4,
    )(a_own, a_other, *pieces, order[:KVCOL], cosine, sine)
    (wo,) = kernel_call(
        order_kernel, [((QCOL, WIDTH), BF16)], "order", [pltpu.VMEM((1024, WIDTH), BF16)], count=9, us=2
    )(*pieces, order[KVCOL:])

    keys_a = jnp.concatenate([p[None] for p in ring(back_y, kv_own[:TOK])], axis=0)
    keys_b = jnp.concatenate([p[None] for p in ring(back_z, kv_own[TOK:])], axis=0)
    keys = ring(back_z, keys_a) + ring(back_y, keys_b)

    halves = []
    for codes, scale, bits in (
        (code_gate.T, scale_gate[:, None], 8),
        (code_up.T, scale_up[:, None], 4),
        (code_down, scale_down[None, :], 2),
    ):
        weight = (scale * slices(codes, bits).astype(F32)).astype(BF16)
        weight = jnp.pad(weight, ((0, UPAD - UNITS), (0, 0)))
        halves.append(lax.dynamic_slice_in_dim(weight, kv * HALF_UNITS, HALF_UNITS, 0))
    ffn_w = ring(back_y, jnp.concatenate(halves, axis=0))
    ffn_w = ffn_w + [from_core(p) for p in ffn_w]

    attend_scratch = [
        pltpu.VMEM((SIDE, SIDE, SPAN, 128), BF16),
        pltpu.VMEM((8, SPAN, 128), F32),
        pltpu.VMEM((SPAN, SPAN), jnp.int32),
        pltpu.VMEM((SPAN, SPAN), jnp.int32),
        pltpu.SemaphoreType.DMA((8,)),
    ]
    o, inv, attn_own, attn_other = kernel_call(
        attend_kernel,
        [((SPAN, QCOL), F32), ((SPAN, QCOL), F32), ((TOK, WIDTH), F32), ((TOK, WIDTH), BF16)],
        "attend",
        attend_scratch,
        in_specs=[SMEM, VMEM] + [ANY] * 8 + [VMEM],
        us=20,
    )(place, q, *keys, wo)

    attn, resid, m_own = kernel_call(
        attn_norm_kernel,
        [((TOK, WIDTH), F32), ((TOK, WIDTH), F32), ((TOK, WIDTH), BF16)],
        "attn_norm",
        count=5,
    )(x, attn_own, from_core(attn_other), gain_2, gain_3)

    m_parts = ring(back_z, m_own)
    part_shapes = [((TOK, WIDTH), F32)] + [((TOK, WIDTH), BF16)] * 3
    wide = ((SIDE * TOK, HID), BF16)
    ffn_scratch = [
        pltpu.VMEM((SIDE * TOK, WIDTH), BF16),
        pltpu.VMEM((HID, WIDTH), BF16),
        pltpu.VMEM((HID, WIDTH), BF16),
        pltpu.VMEM((HID, WIDTH), BF16),
        pltpu.VMEM((SIDE * TOK, WIDTH), F32),
        pltpu.SemaphoreType.DMA((24,)),
    ]
    *fo_parts, gate, up = kernel_call(
        ffn_kernel, part_shapes + [wide, wide], "ffn", ffn_scratch, in_specs=[VMEM] * 4 + [ANY] * 8, us=8
    )(*m_parts, *ffn_w)
    fo_parts = ring_back(back_z, fo_parts)
    block_out, d_fo, g_gain_4 = kernel_call(
        ffn_norm_kernel,
        [((TOK, WIDTH), BF16), ((TOK, WIDTH), BF16), ((1, WIDTH), F32)],
        "ffn_norm",
        count=7,
    )(*fo_parts, resid, cot, gain_4)

    d_parts = ring(back_z, d_fo)
    *dm_parts, hidden, d_gate, d_up = kernel_call(
        ffn_back_kernel, part_shapes + [wide] * 3, "ffn_back", ffn_scratch, in_specs=[VMEM] * 6 + [ANY] * 8, us=10
    )(*d_parts, gate, up, *ffn_w)
    dm_parts = ring_back(back_z, dm_parts)
    weight_parts = kernel_call(
        ffn_weight_kernel,
        [((3 * HALF_UNITS, WIDTH), BF16)] * 8,
        "ffn_weight",
        [pltpu.VMEM((SIDE * TOK, WIDTH), BF16), pltpu.VMEM((SIDE * TOK, WIDTH), BF16)],
        count=11,
        us=8,
    )(*m_parts, *d_parts, hidden, d_gate, d_up)
    d_resid, d_attn, g_gain_3, g_gain_2 = kernel_call(
        ffn_back_norm_kernel,
        [((TOK, WIDTH), F32), ((TOK, WIDTH), BF16), ((1, WIDTH), F32), ((1, WIDTH), F32)],
        "ffn_back_norm",
        count=9,
    )(*dm_parts, resid, attn, cot, gain_3, gain_2)

    got = [from_core(p) for p in weight_parts[4:]]
    sums = [(a.astype(F32) + b.astype(F32)).astype(BF16) for a, b in zip(weight_parts[:4], got)]
    a, b, c, d = ring_back(back_y, sums)
    half = ((a.astype(F32) + b.astype(F32)) + (c.astype(F32) + d.astype(F32))).astype(BF16)
    quarter_rows = 3 * HALF_UNITS // SIDE
    quarter = [
        lax.dynamic_slice_in_dim(half, ((dp - k) & 3) * quarter_rows, quarter_rows, 0) for k in range(SIDE)
    ]
    a, b, c, d = ring_back(back_x, quarter)
    quarter = ((a.astype(F32) + b.astype(F32)) + (c.astype(F32) + d.astype(F32))).astype(BF16)
    half = jnp.zeros((3 * HALF_UNITS, WIDTH), BF16)
    for k, part in enumerate(ring(back_x, quarter)):
        half = lax.dynamic_update_slice_in_dim(half, part, ((dp - k) & 3) * quarter_rows, 0)
    other = from_core(half)
    lower = jnp.where(kv == 0, half, other).reshape(3, HALF_UNITS, WIDTH)
    upper = jnp.where(kv == 0, other, half).reshape(3, HALF_UNITS, WIDTH)
    total = jnp.concatenate([lower, upper], axis=1)[:, :UNITS].astype(F32)
    grad_code_gate = (total[0] * scale_gate[:, None]).T
    grad_code_up = (total[1] * scale_up[:, None]).T
    grad_code_down = total[2] * scale_down[None, :]
    grad_scale_gate = jnp.sum(total[0] * slices(code_gate.T, 8).astype(F32), axis=1)
    grad_scale_up = jnp.sum(total[1] * slices(code_up.T, 4).astype(F32), axis=1)
    part_down = jnp.sum(total[2] * slices(code_down, 2).astype(F32), axis=0, keepdims=True)

    d_attn_other = from_core(d_attn)
    dq, *key_grads = kernel_call(
        attend_back_kernel,
        [((SPAN, QCOL), BF16)] + [((SIDE, 128, TOK), BF16)] * 8,
        "attend_back",
        [
            pltpu.VMEM((SIDE, SIDE, SPAN, 128), BF16),
            pltpu.VMEM((SIDE, SIDE, 128, SPAN), BF16),
            pltpu.VMEM((8, SPAN, 128), F32),
            pltpu.VMEM((8, SPAN, 128), BF16),
            pltpu.VMEM((8, 128, SPAN), BF16),
            pltpu.VMEM((SPAN, SPAN), jnp.int32),
            pltpu.VMEM((SPAN, SPAN), jnp.int32),
            pltpu.SemaphoreType.DMA((8,)),
        ],
        in_specs=[SMEM, VMEM] + [ANY] * 8 + [VMEM] * 7,
        us=35,
    )(place, q, *keys, wo, d_attn, d_attn_other, o, inv, cosine, sine)

    def stage(send, parts):
        a, b, c, d = ring_back(send, parts)
        return ((a.astype(F32) + b.astype(F32)) + (c.astype(F32) + d.astype(F32))).astype(BF16)

    part_a = stage(back_z, key_grads[:4])
    part_b = stage(back_y, key_grads[4:])
    part_a = ring_back(back_y, [part_a[k] for k in range(SIDE)])
    part_b = ring_back(back_z, [part_b[k] for k in range(SIDE)])

    da_own, da_other, *w_grads = kernel_call(
        project_back_kernel,
        [((TOK, WIDTH), F32), ((TOK, WIDTH), BF16)] + [((128, WIDTH), BF16)] * 8,
        "project_back",
        [pltpu.VMEM((2 * SPAN, 1024), BF16)],
        count=18,
        us=5,
    )(dq, *part_a, *part_b, cosine, sine, w_qkv, a_own, a_other, d_attn, d_attn_other, o, order)

    grad_input, g_gain_1 = kernel_call(
        input_norm_kernel, [((TOK, WIDTH), F32), ((1, WIDTH), F32)], "input_norm", count=5
    )(da_own, from_core(da_other), x, d_resid, gain_1)

    part_a = stage(back_z, w_grads[:4])
    part_b = stage(back_y, w_grads[4:])
    part_a = stage(back_y, [part_a[32 * k : 32 * (k + 1)] for k in range(SIDE)])
    part_b = stage(back_z, [part_b[32 * k : 32 * (k + 1)] for k in range(SIDE)])
    parts = [part_a[:16], part_a[16:], part_b[:16], part_b[16:]]
    parts = [group_round(p, i, back=True).astype(F32) for i, p in enumerate(parts)]
    grad_w = (parts[0] + parts[1]) + (parts[2] + parts[3])

    zero = jnp.zeros((1, WIDTH), F32)
    part_down = part_down * 0.125
    small = total_all(
        jnp.concatenate([g_gain_1, g_gain_2, g_gain_3, g_gain_4, part_down, zero, zero, zero], axis=0)
    )

    return (
        block_out.reshape(layer_input.shape),
        grad_input.reshape(layer_input.shape),
        grad_w[:7].T,
        grad_w[7:8].T,
        grad_w[8:9].T,
        grad_w[9:].T,
        small[0],
        small[1],
        small[2],
        small[3],
        grad_code_gate,
        grad_code_up,
        grad_code_down,
        grad_scale_gate,
        grad_scale_up,
        small[4],
    )


def solution(mesh):
    tokens = P("dp", "ctx", "kv", None, None)
    columns = P(None, ("dp", "kv", "ctx"))
    hidden = (P(None, "ctx"), P(None, "ctx"), P("ctx", None), P("ctx"), P("ctx"), P())
    return jax.shard_map(
        shards,
        mesh=mesh,
        in_specs=(tokens, tokens, P("dp", None)) + (columns,) * 4 + (P(),) * 4 + hidden,
        out_specs=(tokens, tokens) + (columns,) * 4 + (P(),) * 4 + hidden,
        check_vma=False,
    )
```

```python
import math

import jax
import jax.numpy as jnp
from jax import lax
from jax.experimental import pallas as pl
from jax.experimental.pallas import tpu as pltpu
from jax.sharding import PartitionSpec as P

EPS = 1e-06
CAP = 50.0
QSCALE = 0.125
GELU_C = math.sqrt(2.0 / math.pi)
EXP2 = CAP * math.log2(math.e)

TOK = 128
SPAN = 256
WIDTH = 896
HEAD = 64
GROUP = 7
QCOL = 512
KVCOL = 640
SIDE = 4
UNITS = 304
UPAD = 320
HALF_UNITS = 160
HID = 1280
HALF_ROWS = 512
BLOCKS = 16
F32 = jnp.float32
BF16 = jnp.bfloat16
VMEM = pl.BlockSpec(memory_space=pltpu.VMEM)
SMEM = pl.BlockSpec(memory_space=pltpu.SMEM)
HBM = pl.BlockSpec(memory_space=pltpu.HBM)


class Fetched:
    def __init__(self, copy, buffer):
        self.copy, self.buffer = copy, buffer

    def __call__(self):
        if self.copy is not None:
            self.copy.wait()
            self.copy = None
        return self.buffer


def kernel_call(body, ins, outs, out, name, args, scratch=(), us=2.0, vmem=16):
    fetched = [i for i, kind in enumerate(ins) if kind == "f"]
    stored = [i for i, kind in enumerate(outs) if kind == "f"]
    count = len(fetched) + len(stored)

    def whole(*refs):
        if not count:
            return body(*refs)
        sems, buffers = refs[-1], refs[len(refs) - 1 - count : -1]
        refs = list(refs[: len(refs) - 1 - count])
        copies = [pltpu.make_async_copy(refs[i], buffers[n], sems.at[n]) for n, i in enumerate(fetched)]
        for c in copies:
            c.start()
        for n, i in enumerate(fetched):
            refs[i] = Fetched(copies[n], buffers[n])
        back = []
        for n, i in enumerate(stored, len(fetched)):
            back.append(pltpu.make_async_copy(buffers[n], refs[len(ins) + i], sems.at[n]))
            refs[len(ins) + i] = buffers[n]
        body(*refs)
        for c in back:
            c.start()
        for c in back:
            c.wait()

    scratch = list(scratch)
    if count:
        scratch += [pltpu.VMEM(args[i].shape, args[i].dtype) for i in fetched]
        scratch += [pltpu.VMEM(*out[i]) for i in stored]
        scratch.append(pltpu.SemaphoreType.DMA((count,)))
    spec = {"s": SMEM, "v": VMEM, "h": HBM, "f": HBM}
    return pl.pallas_call(
        whole,
        out_shape=[jax.ShapeDtypeStruct(shape, dtype) for shape, dtype in out],
        in_specs=[spec[kind] for kind in ins],
        out_specs=[spec[kind] for kind in outs],
        scratch_shapes=scratch,
        compiler_params=pltpu.CompilerParams(vmem_limit_bytes=vmem * 1024 * 1024),
        cost_estimate=pl.CostEstimate(flops=int(us * 1e9), bytes_accessed=0, transcendentals=0),
        name=name,
    )(*args)


def dot(left, right):
    return lax.dot_general(left, right, (((1,), (0,)), ((), ())), preferred_element_type=F32)


def dot_right(left, right):
    return lax.dot_general(left, right, (((1,), (1,)), ((), ())), preferred_element_type=F32)


def dot_left(left, right):
    return lax.dot_general(left, right, (((0,), (0,)), ((), ())), preferred_element_type=F32)


def from_core(x):
    return lax.ppermute(x, "kv", [(0, 1), (1, 0)])


def back_x(x, k):
    return lax.ppermute(x, "dp", [(i, (i + k) % SIDE) for i in range(SIDE)])


def back_y(x, k):
    pairs = [(z * SIDE + y, z * SIDE + (y + k) % SIDE) for z in range(SIDE) for y in range(SIDE)]
    return lax.ppermute(x, "ctx", pairs)


def back_z(x, k):
    pairs = [(z * SIDE + y, (z + k) % SIDE * SIDE + y) for z in range(SIDE) for y in range(SIDE)]
    return lax.ppermute(x, "ctx", pairs)


def group_round(x, i, back=False):
    pairs = [(n, 2 * ((n % 4 + i) % SIDE) + n // 4) for n in range(8)]
    if back:
        pairs = [(b, a) for a, b in pairs]
    return lax.ppermute(x, ("dp", "kv"), pairs)


def all_to_all(x):
    return lax.all_to_all(x, "ctx", split_axis=0, concat_axis=0, tiled=True)


def ring(send, x):
    got = {k: send(x, k) for k in (1, 3, 2)}
    return [x, got[1], got[2], got[3]]


def ring_back(send, parts):
    got = {k: send(parts[k], SIDE - k) for k in (1, 3, 2)}
    return [parts[0], got[1], got[2], got[3]]


def norm_rows(rows, gain):
    inverse = lax.rsqrt(jnp.mean(rows * rows, axis=-1, keepdims=True) + EPS)
    return rows * inverse * gain, inverse


def norm_back(rows, gain, incoming):
    inverse = lax.rsqrt(jnp.mean(rows * rows, axis=-1, keepdims=True) + EPS)
    normed = rows * inverse
    scaled = incoming * gain
    grad = inverse * (scaled - normed * jnp.mean(scaled * normed, axis=-1, keepdims=True))
    return grad, jnp.sum(incoming * normed, axis=0, keepdims=True)


def lane(shape):
    return lax.broadcasted_iota(jnp.int32, shape, len(shape) - 1)


def swap_halves(x):
    return jnp.where(lane(x.shape) % HEAD < HEAD // 2, pltpu.roll(x, 96, 1), pltpu.roll(x, 32, 1))


CTX, DP, KV, STARTS = 0, 1, 2, 3


def doc_start(place, p):
    start = jnp.zeros_like(p)
    for i in range(8):
        b = place[STARTS + i]
        start = jnp.where(p >= b, jnp.maximum(start, b), start)
    return start


def span_places(shape, dim, chip, kv):
    i = lax.broadcasted_iota(jnp.int32, shape, dim)
    half = jnp.where(i < TOK, kv, 1 - kv)
    return chip * SPAN + half * TOK + i % TOK


def rotary(place):
    spot = span_places((SPAN, 128), 0, place[CTX], place[KV])
    index = lane((SPAN, 128)) % HEAD
    freq = jnp.exp((index % (HEAD // 2)).astype(F32) * (-2.0 * math.log(10000.0) / HEAD))
    angle = (spot - doc_start(place, spot)).astype(F32) * freq
    return jnp.cos(angle), jnp.where(index < HEAD // 2, -1.0, 1.0) * jnp.sin(angle)


def order_rows(place, first, count):
    row = lane((1, 1024))
    ctx, turn, kind = row // 64, row // 16 % 4, row % 16
    col = ((place[DP] - turn) & 3) * 16 + ctx
    target = jnp.where(kind == 7, QCOL + col, jnp.where(kind == 8, QCOL + HEAD + col, KVCOL + 7 * col + kind - 9))
    target = jnp.where(kind < 7, 7 * col + kind, target)
    rows = lax.broadcasted_iota(jnp.int32, (count, 1024), 0) + first
    return jnp.where(rows == target, 1.0, 0.0).astype(BF16)


def qkv_kernel(place, x0, x1, gain, w, q_out, kv_out, w_out):
    order = order_rows(place, 0, KVCOL)
    cos, sin = rotary(place)
    rows = jnp.concatenate([x0()[...], x1()[...]], axis=0).astype(F32)
    rows = norm_rows(rows, gain[...])[0].astype(BF16)
    w_cols = dot(order, w()[...]).astype(BF16)
    w_out[...] = w_cols
    raw = dot_right(rows, w_cols)
    low = lane((SPAN, 128)) < HEAD
    for j in range(4):
        u = raw[:, 128 * j : 128 * (j + 1)]
        q_out[:, 128 * j : 128 * (j + 1)] = ((u * cos + swap_halves(u) * sin) * QSCALE).astype(BF16)
    u = raw[:, QCOL:KVCOL]
    kv = jnp.where(low, u * cos + swap_halves(u) * sin, u).astype(BF16)
    for j in range(BLOCKS):
        kv_out[j] = kv


def spread_heads(q, out):
    low = lane((SPAN, 128)) < HEAD
    for j in range(4):
        u = q[:, 128 * j : 128 * (j + 1)].astype(F32)
        out[2 * j] = jnp.where(low, u, 0.0).astype(BF16)
        if j < 3:
            out[2 * j + 1] = jnp.where(low, pltpu.roll(u, HEAD, 1), 0.0).astype(BF16)


def order_kernel(place, w, w_out):
    w_out[...] = dot(order_rows(place, KVCOL, QCOL), w()[...]).astype(BF16)


def block_ranges(place, n):
    first = place[CTX] * SPAN
    low_start, high_start = doc_start(place, first), doc_start(place, first + SPAN - 1)
    active = (n <= place[CTX]) & (n * SPAN + SPAN - 1 >= low_start)
    full = (n < place[CTX]) & (n * SPAN >= high_start)
    return active, full


def query_places(place, pos_ref, start_ref):
    pos = span_places((SPAN, SPAN), 0, place[CTX], place[KV])
    pos_ref[...] = pos
    start_ref[...] = doc_start(place, pos)


def allowed_keys(place, source, pos_ref, start_ref):
    keys = span_places((SPAN, SPAN), 1, source, place[KV])
    return (keys <= pos_ref[...]) & (keys >= start_ref[...])


def attend_kernel(place, q_cols, blocks, wo, o_out, inv_out, own_out, other_out, q, acc, pos_ref, start_ref):
    query_places(place, pos_ref, start_ref)
    acc[...] = jnp.zeros_like(acc)
    spread_heads(q_cols(), q)
    blocks = blocks()
    low = lane((SPAN, 128)) < HEAD

    @pl.loop(0, BLOCKS)
    def _(n):
        active, full = block_ranges(place, n)

        def step(masked):
            kv = blocks[n]
            ones_v = jnp.where(low, jnp.ones_like(kv), kv)
            if masked:
                allowed = allowed_keys(place, n, pos_ref, start_ref)
            for h in range(GROUP):
                s = dot_right(q[h], kv)
                p = jnp.exp2(jnp.tanh(s * (1.0 / CAP)) * EXP2)
                if masked:
                    p = jnp.where(allowed, p, 0.0)
                acc[h] += dot(p.astype(BF16), ones_v)

        pl.when(full)(lambda: step(False))
        pl.when(active & jnp.logical_not(full))(lambda: step(True))

    lanes = lane((SPAN, 128))
    inverse = jnp.ones((SPAN, 128), F32)
    for j in range(4):
        a = acc[2 * j]
        if j < 3:
            b = acc[2 * j + 1]
            total = jnp.where(low, a, pltpu.roll(b, HEAD, 1))
            value = jnp.where(low, pltpu.roll(a, HEAD, 1), b)
            inverse = jnp.where(lanes == 2 * j + 1, 1.0 / b, inverse)
        else:
            total = jnp.where(low, a, 1.0)
            value = jnp.where(low, pltpu.roll(a, HEAD, 1), 0.0)
        inverse = jnp.where(lanes == 2 * j, 1.0 / a, inverse)
        o_out[:, 128 * j : 128 * (j + 1)] = (value / total).astype(BF16)
    inv_out[...] = inverse
    attn = dot(o_out[...], wo()[...])
    own_out[...] = attn[:TOK]
    other_out[...] = attn[TOK:].astype(BF16)


def attend_back_kernel(
    place, d0, d1, wo, q_cols, o, inv, blocks,
    dq_out, grads, q, dq, do_ext, both_t, pos_ref, start_ref,
):
    query_places(place, pos_ref, start_ref)
    dq[...] = jnp.zeros_like(dq)
    rows = jnp.concatenate([d0()[...], d1()[...]], axis=0)
    d_o = dot_right(rows, wo()[...]).astype(BF16).astype(F32)
    low = lane((SPAN, 128)) < HEAD
    lanes = lane((SPAN, 128))
    spread_heads(q_cols(), q)
    o, inv = o(), inv()
    for h in range(GROUP):
        j = h // 2
        cols = slice(128 * j, 128 * (j + 1))
        mine = low if h % 2 == 0 else jnp.logical_not(low)
        scale = inv[:, h : h + 1]
        up = d_o[:, cols] * scale
        delta = jnp.sum(jnp.where(mine, up * o[:, cols].astype(F32), 0.0), axis=1, keepdims=True)
        if h % 2 == 0:
            up = pltpu.roll(up, HEAD, 1)
        high = delta.astype(BF16).astype(F32)
        ext = jnp.where(lanes == 0, -high, jnp.where(lanes == 1, high - delta, jnp.where(low, 0.0, up)))
        do_ext[h] = ext.astype(BF16)
        both_t[h] = jnp.transpose(jnp.where(low, q[h].astype(F32), up)).astype(BF16)
    blocks = blocks()

    @pl.loop(0, BLOCKS)
    def _(n):
        active, full = block_ranges(place, n)

        def step(masked):
            kv = blocks[n]
            ones_v = jnp.where(low, jnp.ones_like(kv), kv)
            if masked:
                allowed = allowed_keys(place, n, pos_ref, start_ref)
            dk = jnp.zeros((HEAD, SPAN), F32)
            dv = jnp.zeros((HEAD, SPAN), F32)
            for h in range(GROUP):
                s = dot_right(q[h], kv)
                dp = dot_right(do_ext[h], ones_v)
                t = jnp.tanh(s * (1.0 / CAP))
                p = jnp.exp2(t * EXP2)
                if masked:
                    p = jnp.where(allowed, p, 0.0)
                ds = (p * dp * (1.0 - t * t)).astype(BF16)
                dq[h] += dot(ds, kv)
                dk += dot(both_t[h, pl.ds(0, HEAD), :], ds)
                dv += dot(both_t[h, pl.ds(HEAD, HEAD), :], p.astype(BF16))
            grads[n] = jnp.concatenate([dk, dv], axis=0).astype(BF16)

        pl.when(full)(lambda: step(False))
        pl.when(active & jnp.logical_not(full))(lambda: step(True))

        @pl.when(jnp.logical_not(active))
        def _():
            grads[n] = jnp.zeros((128, SPAN), BF16)

    cos, sin = rotary(place)
    for j in range(4):
        u = dq[2 * j]
        if j < 3:
            u = jnp.where(low, u, pltpu.roll(dq[2 * j + 1], HEAD, 1))
        else:
            u = jnp.where(low, u, 0.0)
        u = u * QSCALE
        dq_out[:, 128 * j : 128 * (j + 1)] = (u * cos - swap_halves(u) * sin).astype(BF16)


def project_back_kernel(
    place, dkv_parts, dq, w, x0, x1, d0, d1, o, gain, g2, g3, g4, g5,
    own_out, other_out, w_grad, left,
):
    cos, sin = rotary(place)
    dkv_parts = dkv_parts()
    dkv = dkv_parts[0].astype(F32)
    for j in range(1, BLOCKS):
        dkv += dkv_parts[j].astype(F32)
    u = jnp.transpose(dkv)
    low = lane((SPAN, 128)) < HEAD
    dkv = jnp.where(low, u * cos - swap_halves(u) * sin, u).astype(BF16)
    grads = jnp.concatenate([dq()[...], dkv], axis=1)
    d_a = dot(grads, w()[...])
    own_out[...] = d_a[:TOK]
    other_out[...] = d_a[TOK:].astype(BF16)
    rows = jnp.concatenate([x0()[...], x1()[...]], axis=0).astype(F32)
    normed = norm_rows(rows, 1.0)[0]
    g1 = jnp.sum(normed * d_a, axis=0, keepdims=True)
    gains = jnp.concatenate([g1, g2[...], g3[...], g4[...], g5[...], jnp.zeros((3, WIDTH), F32)], axis=0).astype(BF16)
    left[pl.ds(0, SPAN), :] = dot(grads, order_rows(place, 0, KVCOL)).astype(BF16)
    left[pl.ds(SPAN, SPAN), :] = dot(o()[...], order_rows(place, KVCOL, QCOL)).astype(BF16)
    right = jnp.concatenate([(normed * gain[...]).astype(BF16), d0()[...], d1()[...]], axis=0)
    for j in range(4):
        cols = slice(256 * j, 256 * (j + 1))
        part = dot_left(left[:, cols], right).astype(BF16)
        for n in range(4):
            w_grad[4 * j + n, pl.ds(0, 64), :] = part[64 * n : 64 * (n + 1)]
            w_grad[4 * j + n, pl.ds(64, 8), :] = gains


def attn_norm_kernel(x, own, other, gain_b, gain_c, attn_out, r_out, m_out):
    attn = own[...] + other[...].astype(F32)
    attn_out[...] = attn
    resid = x[...].astype(F32) + norm_rows(attn, gain_b[...])[0]
    r_out[...] = resid
    m_out[...] = norm_rows(resid, gain_c[...])[0].astype(BF16)


def sum_parts(own, b, c, d):
    return (own[...] + b[...].astype(F32)) + (c[...].astype(F32) + d[...].astype(F32))


def ffn_norm_kernel(own, b, c, d, resid, cotangent, gain, out, d_out, gain_out):
    fo = sum_parts(own, b, c, d)
    out[...] = (resid[...] + norm_rows(fo, gain[...])[0]).astype(BF16)
    grad, gain_grad = norm_back(fo, gain[...], cotangent[...].astype(F32))
    d_out[...] = grad.astype(BF16)
    gain_out[...] = gain_grad


def ffn_back_norm_kernel(own, b, c, d, resid, attn, cotangent, gain_c, gain_b, r_out, d_out, gain_c_out, gain_b_out):
    d_m = sum_parts(own, b, c, d)
    grad, gain_grad = norm_back(resid[...], gain_c[...], d_m)
    gain_c_out[...] = gain_grad
    d_resid = cotangent[...].astype(F32) + grad
    r_out[...] = d_resid
    grad, gain_grad = norm_back(attn[...], gain_b[...], d_resid)
    gain_b_out[...] = gain_grad
    d_out[...] = grad.astype(BF16)


def input_norm_kernel(own, other, x, d_resid, gain, out):
    d_a = own[...] + other[...].astype(F32)
    out[...] = d_resid[...] + norm_back(x[...].astype(F32), gain[...], d_a)[0]


def gelu_parts(u):
    t = jnp.tanh(GELU_C * (u + 0.044715 * u * u * u))
    active = 0.5 * u * (1.0 + t)
    slope = 0.5 * (1.0 + t) + 0.5 * u * (1.0 - t * t) * GELU_C * (1.0 + 3.0 * 0.044715 * u * u)
    return active, slope


def weight_runs(which):
    runs, at = [], which * HALF_UNITS
    while at < (which + 1) * HALF_UNITS:
        count = min(TOK - at % TOK, (which + 1) * HALF_UNITS - at)
        runs.append((at // TOK, at % TOK, at - which * HALF_UNITS, count))
        at += count
    return runs


def weight_copies(place, pieces, dest, sems, which):
    copies = []
    for core in range(2):
        source = place[KV] if core == 0 else 1 - place[KV]
        for quarter, row, unit, count in weight_runs(which):
            copies.append(
                pltpu.make_async_copy(
                    pieces.at[2 * quarter + source, :, pl.ds(row, count), :],
                    dest.at[pl.ds(core * SIDE, SIDE), pl.ds(unit, count), :],
                    sems.at[which * 4 + len(copies)],
                )
            )
    for c in copies:
        c.start()
    return copies


def dequantise_kernel(place, gate, up, down, gate_scale, up_scale, down_scale, out, codes, sems):
    out[...] = jnp.zeros((TOK, WIDTH), BF16)

    def fill(core, quarter):
        runs = []
        for which in range(3):
            for part, row, unit, count in weight_runs(which):
                first = core * HALF_UNITS + unit
                count = min(count, UNITS - first)
                if part == quarter:
                    runs.append((which, row, first, count))
        copies = [
            pltpu.make_async_copy(
                (gate, up, down)[which].at[pl.ds(first, count), :], codes.at[pl.ds(row, count), :], sems.at[n]
            )
            for n, (which, row, first, count) in enumerate(runs)
        ]
        for c in copies:
            c.start()
        for c in copies:
            c.wait()
        for which, row, first, count in runs:
            c = codes[pl.ds(row, count), :]
            if which == 0:
                weight = c.astype(F32) * gate_scale[pl.ds(first, count), :]
            elif which == 1:
                weight = ((c & -16) + 8).astype(F32) * up_scale[pl.ds(first, count), :]
            else:
                weight = ((c & -64) + 32).astype(F32) * down_scale[...]
            out[pl.ds(row, count), :] = weight.astype(BF16)

    for core in range(2):
        for quarter in range(SIDE):
            pl.when((place[KV] == core) & (place[DP] == quarter))(lambda c=core, q=quarter: fill(c, q))


def ffn_kernel(
    place, m0, m1, m2, m3, pieces, f0, f1, f2, f3, gate_out, up_out,
    m, gate_w3, up_w3, down_w3, acc, sems,
):
    gates = weight_copies(place, pieces, gate_w3, sems, 0)
    ups = weight_copies(place, pieces, up_w3, sems, 1)
    downs = weight_copies(place, pieces, down_w3, sems, 2)
    gate_w, up_w, down_w = (w.reshape(HID, WIDTH) for w in (gate_w3, up_w3, down_w3))
    for j, part in enumerate((m0, m1, m2, m3)):
        m[pl.ds(TOK * j, TOK), :] = part[...]
    for c in gates + ups + downs:
        c.wait()
    for n in range(HID // 256):
        units = pl.ds(256 * n, 256)
        gate = dot_right(m[...], gate_w[units, :])
        up = dot_right(m[...], up_w[units, :])
        gate_out[:, 256 * n : 256 * (n + 1)] = gate.astype(BF16)
        up_out[:, 256 * n : 256 * (n + 1)] = up.astype(BF16)
        hidden = (gelu_parts(gate)[0] * up).astype(BF16)
        part = dot(hidden, down_w[units, :])
        if n == 0:
            acc[...] = part
        else:
            acc[...] += part
    f0[...] = acc[pl.ds(0, TOK), :]
    for j, out in enumerate((f1, f2, f3)):
        out[...] = acc[pl.ds(TOK * (j + 1), TOK), :].astype(BF16)


def ffn_back_kernel(
    place, e0, e1, e2, e3, gate_in, up_in, pieces, f0, f1, f2, f3, hidden_out, gate_out, up_out,
    e, gate_w3, up_w3, down_w3, acc, sems,
):
    downs = weight_copies(place, pieces, down_w3, sems, 2)
    gates = weight_copies(place, pieces, gate_w3, sems, 0)
    ups = weight_copies(place, pieces, up_w3, sems, 1)
    gate_w, up_w, down_w = (w.reshape(HID, WIDTH) for w in (gate_w3, up_w3, down_w3))
    for j, part in enumerate((e0, e1, e2, e3)):
        e[pl.ds(TOK * j, TOK), :] = part[...]
    for c in downs + gates + ups:
        c.wait()
    for n in range(HID // 256):
        units = pl.ds(256 * n, 256)
        cols = slice(256 * n, 256 * (n + 1))
        d_hidden = dot_right(e[...], down_w[units, :])
        active, slope = gelu_parts(gate_in[:, cols].astype(F32))
        up = up_in[:, cols].astype(F32)
        hidden_out[:, cols] = (active * up).astype(BF16)
        d_gate = (d_hidden * up * slope).astype(BF16)
        d_up = (d_hidden * active).astype(BF16)
        gate_out[:, cols] = d_gate
        up_out[:, cols] = d_up
        part = dot(d_gate, gate_w[units, :]) + dot(d_up, up_w[units, :])
        if n == 0:
            acc[...] = part
        else:
            acc[...] += part
    f0[...] = acc[pl.ds(0, TOK), :]
    for j, out in enumerate((f1, f2, f3)):
        out[...] = acc[pl.ds(TOK * (j + 1), TOK), :].astype(BF16)


def ffn_weight_kernel(
    place, m0, m1, m2, m3, e0, e1, e2, e3, hidden, d_gate, d_up, pieces, down_scale, out, scale_out, m, e, down_w3, sems
):
    copies = weight_copies(place, pieces, down_w3, sems, 2)
    for j, (a, b) in enumerate(zip((m0, m1, m2, m3), (e0, e1, e2, e3))):
        m[pl.ds(TOK * j, TOK), :] = a[...]
        e[pl.ds(TOK * j, TOK), :] = b[...]
    empty = SIDE * TOK - 3 * HALF_UNITS
    out[pl.ds(2 * SIDE - 2, 2), :, pl.ds(TOK - empty, empty), :] = jnp.zeros((2, SIDE, empty, WIDTH), BF16)
    for c in copies:
        c.wait()
    down_w = down_w3.reshape(HID, WIDTH)
    per_unit = 1.0 / down_scale[...]
    scale_grad = jnp.zeros((1, WIDTH), F32)
    for which, (left, right) in enumerate(((d_gate, m), (d_up, m), (hidden, e))):
        runs = weight_runs(which)
        for n in range(HID // 256):
            first = 256 * n
            part = dot_left(left[:, first : first + 256], right[...])
            if which == 2:
                level = down_w[pl.ds(first, 256), :].astype(F32) * per_unit
                level = jnp.floor(level * (1.0 / 64.0)) * 64.0 + 32.0
                scale_grad += jnp.sum(part * level, axis=0, keepdims=True)
            part = part.astype(BF16)
            for piece in range(2 * SIDE):
                core = place[KV] if piece < SIDE else 1 - place[KV]
                for quarter, row, unit, count in runs:
                    low = max(piece * HALF_UNITS + unit, first)
                    high = min(piece * HALF_UNITS + unit + count, first + 256)
                    if low < high:
                        at = row + low - piece * HALF_UNITS - unit
                        out[2 * quarter + core, piece % SIDE, pl.ds(at, high - low), :] = part[low - first : high - first]
    scale_out[...] = scale_grad


def finish_kernel(parts, gate, up, gate_scale, up_scale, down_scale, g_gate, g_up, g_down, s_gate, s_up, sums):
    sums[...] = jnp.zeros_like(sums)
    for core in range(2):
        for which in range(3):
            for quarter, row, unit, count in weight_runs(which):
                first = core * HALF_UNITS + unit
                count = min(count, UNITS - first)
                rows = pl.ds(first, count)
                total = parts[2 * quarter + core, pl.ds(row, count), :].astype(F32)
                if which == 0:
                    g_gate[rows, :] = total * gate_scale[rows, :]
                    part = jnp.sum(total * gate[rows, :].astype(F32), axis=1, keepdims=True)
                    sums[0, rows, :] = jnp.broadcast_to(part, (count, 128))
                elif which == 1:
                    g_up[rows, :] = total * up_scale[rows, :]
                    part = jnp.sum(total * ((up[rows, :] & -16) + 8).astype(F32), axis=1, keepdims=True)
                    sums[1, rows, :] = jnp.broadcast_to(part, (count, 128))
                else:
                    g_down[rows, :] = total * down_scale[...]
    s_gate[...] = jnp.transpose(sums[0])[:1, :UNITS]
    s_up[...] = jnp.transpose(sums[1])[:1, :UNITS]


def shards(
    layer_input, cotangent, doc_bounds, w_query, key_weight, value_weight, w_out,
    gain_attn_in, gain_attn_out, gain_ffn_in, gain_ffn_out,
    code_gate, code_up, code_down, scale_gate, scale_up, scale_down,
):
    ctx, kv, dp = lax.axis_index("ctx"), lax.axis_index("kv"), lax.axis_index("dp")
    place = jnp.concatenate([jnp.stack([ctx, dp, kv]).astype(jnp.int32), doc_bounds[0]])
    x = layer_input.reshape(TOK, WIDTH)
    cot = cotangent.reshape(TOK, WIDTH)
    gain_1, gain_2, gain_3, gain_4 = (
        g.reshape(1, WIDTH) for g in (gain_attn_in, gain_attn_out, gain_ffn_in, gain_ffn_out)
    )
    gate_col, up_col, down_row = scale_gate[:, None], scale_up[:, None], scale_down[None, :]
    rows_f32, rows_bf16, row_f32 = ((TOK, WIDTH), F32), ((TOK, WIDTH), BF16), ((1, WIDTH), F32)

    shard = jnp.concatenate([w_query.T, key_weight.T, value_weight.T, w_out.T], axis=0)
    rounds = [group_round(shard, i) for i in range(4)]
    x_other = from_core(x)

    rounds, x_other, place_after = lax.optimization_barrier((jnp.concatenate(rounds, axis=0), x_other, place))
    (quarter,) = kernel_call(
        dequantise_kernel,
        "shhhvvv",
        "v",
        [rows_bf16],
        "dequantise",
        (place_after, code_gate.T, code_up.T, code_down, gate_col, up_col, down_row),
        [pltpu.VMEM((TOK, WIDTH), jnp.int32), pltpu.SemaphoreType.DMA((2,))],
        vmem=58,
    )
    quarters = ring(back_y, quarter)
    w_rows = all_to_all(jnp.broadcast_to(rounds[None], (BLOCKS, 4 * 16, WIDTH))).reshape(1024, WIDTH)
    quarters, w_rows = lax.optimization_barrier((quarters, w_rows))
    ffn_w = lax.all_gather(jnp.stack(quarters), ("dp", "kv"))

    q, keys, w_qkv = kernel_call(
        qkv_kernel,
        "sffvf",
        "fff",
        [((SPAN, QCOL), BF16), ((BLOCKS, SPAN, 128), BF16), ((KVCOL, WIDTH), BF16)],
        "qkv",
        (place, x, x_other, gain_1, w_rows),
        us=4,
        vmem=58,
    )
    w_rows, q = lax.optimization_barrier((w_rows, q))
    keys = all_to_all(keys)
    (wo,) = kernel_call(order_kernel, "sf", "f", [((QCOL, WIDTH), BF16)], "order", (place, w_rows), vmem=58)

    o, inv, attn_own, attn_other = kernel_call(
        attend_kernel,
        "sfff",
        "ffvv",
        [((SPAN, QCOL), BF16), ((SPAN, 128), F32), rows_f32, rows_bf16],
        "attend",
        (place, q, keys, wo),
        [
            pltpu.VMEM((8, SPAN, 128), BF16),
            pltpu.VMEM((8, SPAN, 128), F32),
            pltpu.VMEM((SPAN, SPAN), jnp.int32),
            pltpu.VMEM((SPAN, SPAN), jnp.int32),
        ],
        us=18,
        vmem=58,
    )
    ffn_w, attn_other = lax.optimization_barrier((ffn_w, from_core(attn_other)))
    attn, resid, m_own = kernel_call(
        attn_norm_kernel,
        "vvvvv",
        "vvv",
        [rows_f32, rows_f32, rows_bf16],
        "attn_norm",
        (x, attn_own, attn_other, gain_2, gain_3),
    )

    m_parts = ring(back_z, m_own)
    wide = ((SIDE * TOK, HID), BF16)
    ffn_scratch = [pltpu.VMEM((SIDE * TOK, WIDTH), BF16)]
    ffn_scratch += [pltpu.VMEM((2 * SIDE, HALF_UNITS, WIDTH), BF16)] * 3
    ffn_scratch += [pltpu.VMEM((SIDE * TOK, WIDTH), F32), pltpu.SemaphoreType.DMA((12,))]
    *fo_parts, gate, up = kernel_call(
        ffn_kernel,
        "svvvvh",
        "vvvvvv",
        [rows_f32] + [rows_bf16] * 3 + [wide, wide],
        "ffn",
        (place, *m_parts, ffn_w),
        ffn_scratch,
        us=8,
        vmem=24,
    )
    fo_parts = ring_back(back_z, fo_parts)
    block_out, d_fo, g_gain_4 = kernel_call(
        ffn_norm_kernel, "vvvvvvv", "vvv", [rows_bf16, rows_bf16, row_f32], "ffn_norm", (*fo_parts, resid, cot, gain_4)
    )

    d_parts = ring(back_z, d_fo)
    *dm_parts, hidden, d_gate, d_up = kernel_call(
        ffn_back_kernel,
        "svvvvvvh",
        "vvvvvvv",
        [rows_f32] + [rows_bf16] * 3 + [wide] * 3,
        "ffn_back",
        (place, *d_parts, gate, up, ffn_w),
        ffn_scratch,
        us=10,
        vmem=28,
    )
    dm_parts = ring_back(back_z, dm_parts)
    weight_grads, g_down = kernel_call(
        ffn_weight_kernel,
        "s" + "v" * 11 + "hv",
        "fv",
        [((2 * SIDE, SIDE, TOK, WIDTH), BF16), row_f32],
        "ffn_weight",
        (place, *m_parts, *d_parts, hidden, d_gate, d_up, ffn_w, down_row),
        [
            pltpu.VMEM((SIDE * TOK, WIDTH), BF16),
            pltpu.VMEM((SIDE * TOK, WIDTH), BF16),
            pltpu.VMEM((2 * SIDE, HALF_UNITS, WIDTH), BF16),
            pltpu.SemaphoreType.DMA((12,)),
        ],
        us=8,
        vmem=28,
    )
    dm_parts, weight_grads = lax.optimization_barrier((dm_parts, weight_grads))
    weight_grads = lax.psum_scatter(weight_grads, ("dp", "kv"), scatter_dimension=0)
    d_resid, d_attn, g_gain_3, g_gain_2 = kernel_call(
        ffn_back_norm_kernel,
        "vvvvvvvvv",
        "vvvv",
        [rows_f32, rows_bf16, row_f32, row_f32],
        "ffn_back_norm",
        (*dm_parts, resid, attn, cot, gain_3, gain_2),
    )
    d_attn_other = from_core(d_attn)

    dq, key_grads = kernel_call(
        attend_back_kernel,
        "sfffffff",
        "ff",
        [((SPAN, QCOL), BF16), ((BLOCKS, 128, SPAN), BF16)],
        "attend_back",
        (place, d_attn, d_attn_other, wo, q, o, inv, keys),
        [
            pltpu.VMEM((8, SPAN, 128), BF16),
            pltpu.VMEM((8, SPAN, 128), F32),
            pltpu.VMEM((8, SPAN, 128), BF16),
            pltpu.VMEM((8, 128, SPAN), BF16),
            pltpu.VMEM((SPAN, SPAN), jnp.int32),
            pltpu.VMEM((SPAN, SPAN), jnp.int32),
        ],
        us=35,
        vmem=58,
    )
    key_grads = all_to_all(key_grads)
    da_own, da_other, w_grads = kernel_call(
        project_back_kernel,
        "sffffffffvvvvv",
        "vvv",
        [rows_f32, rows_bf16, ((BLOCKS, 72, WIDTH), BF16)],
        "project_back",
        (place, key_grads, dq, w_qkv, x, x_other, d_attn, d_attn_other, o, gain_1, g_gain_2, g_gain_3, g_gain_4, g_down),
        [pltpu.VMEM((2 * SPAN, 1024), BF16)],
        us=5,
        vmem=58,
    )

    sums = jnp.sum(all_to_all(w_grads).astype(F32), axis=0).astype(BF16)
    sums = [jnp.concatenate([sums[16 * i : 16 * (i + 1)], sums[64:]], axis=0) for i in range(4)]
    sums = [group_round(part, i, back=True).astype(F32) for i, part in enumerate(sums)]
    sums = (sums[0] + sums[1]) + (sums[2] + sums[3])
    grad_w = sums[:16]
    gains = sums[16:] + back_x(sums[16:], 2)

    weight_grads, da_other = lax.optimization_barrier((weight_grads, da_other))
    weight_grads = weight_grads.reshape(SIDE, TOK, WIDTH)
    a, b, c, d = ring_back(back_y, [weight_grads[k] for k in range(SIDE)])
    eighth = ((a.astype(F32) + b.astype(F32)) + (c.astype(F32) + d.astype(F32))).astype(BF16)
    eighths = lax.all_gather(eighth, ("dp", "kv"))

    (grad_input,) = kernel_call(
        input_norm_kernel, "vvvvv", "v", [rows_f32], "input_norm", (da_own, from_core(da_other), x, d_resid, gain_1)
    )

    grad_code_gate, grad_code_up, grad_code_down, grad_scale_gate, grad_scale_up = kernel_call(
        finish_kernel,
        "vvvvvv",
        "vvvvv",
        [((UNITS, WIDTH), F32)] * 3 + [((1, UNITS), F32)] * 2,
        "finish",
        (eighths, code_gate.T, code_up.T, gate_col, up_col, down_row),
        [pltpu.VMEM((2, 384, 128), F32)],
        us=3,
    )

    return (
        block_out.reshape(layer_input.shape),
        grad_input.reshape(layer_input.shape),
        grad_w[:7].T,
        grad_w[7:8].T,
        grad_w[8:9].T,
        grad_w[9:].T,
        gains[0],
        gains[1],
        gains[2],
        gains[3],
        grad_code_gate.T,
        grad_code_up.T,
        grad_code_down,
        grad_scale_gate[0],
        grad_scale_up[0],
        gains[4],
    )


def solution(mesh):
    tokens = P("dp", "ctx", "kv", None, None)
    columns = P(None, ("dp", "kv", "ctx"))
    hidden = (P(None, "ctx"), P(None, "ctx"), P("ctx", None), P("ctx"), P("ctx"), P())
    return jax.shard_map(
        shards,
        mesh=mesh,
        in_specs=(tokens, tokens, P("dp", None)) + (columns,) * 4 + (P(),) * 4 + hidden,
        out_specs=(tokens, tokens) + (columns,) * 4 + (P(),) * 4 + hidden,
        check_vma=False,
    )
```

```python
import math

import jax
import jax.numpy as jnp
from jax import lax
from jax.experimental import pallas as pl
from jax.experimental.pallas import tpu as pltpu
from jax.sharding import PartitionSpec as P

EPS = 1e-06
CAP = 50.0
QSCALE = 0.125
GELU_C = math.sqrt(2.0 / math.pi)
EXP2 = CAP * math.log2(math.e)

TOK = 128
SPAN = 256
WIDTH = 896
HEAD = 64
GROUP = 7
QCOL = 512
SIDE = 4
UNITS = 304
UPAD = 320
HALF_UNITS = 160
HID = 1280
HALF_ROWS = 512
BLOCKS = 16
F32 = jnp.float32
BF16 = jnp.bfloat16
VMEM = pl.BlockSpec(memory_space=pltpu.VMEM)
SMEM = pl.BlockSpec(memory_space=pltpu.SMEM)
HBM = pl.BlockSpec(memory_space=pltpu.HBM)


class Fetched:
    def __init__(self, copy, buffer):
        self.copy, self.buffer = copy, buffer

    def __call__(self):
        if self.copy is not None:
            self.copy.wait()
            self.copy = None
        return self.buffer


def kernel_call(body, ins, outs, out, name, args, scratch=(), us=2.0, vmem=16):
    fetched = [i for i, kind in enumerate(ins) if kind == "f"]
    stored = [i for i, kind in enumerate(outs) if kind == "f"]
    count = len(fetched) + len(stored)

    def whole(*refs):
        if not count:
            return body(*refs)
        sems, buffers = refs[-1], refs[len(refs) - 1 - count : -1]
        refs = list(refs[: len(refs) - 1 - count])
        copies = [pltpu.make_async_copy(refs[i], buffers[n], sems.at[n]) for n, i in enumerate(fetched)]
        for c in copies:
            c.start()
        for n, i in enumerate(fetched):
            refs[i] = Fetched(copies[n], buffers[n])
        back = []
        for n, i in enumerate(stored, len(fetched)):
            back.append(pltpu.make_async_copy(buffers[n], refs[len(ins) + i], sems.at[n]))
            refs[len(ins) + i] = buffers[n]
        body(*refs)
        for c in back:
            c.start()
        for c in back:
            c.wait()

    scratch = list(scratch)
    if count:
        scratch += [pltpu.VMEM(args[i].shape, args[i].dtype) for i in fetched]
        scratch += [pltpu.VMEM(*out[i]) for i in stored]
        scratch.append(pltpu.SemaphoreType.DMA((count,)))
    spec = {"s": SMEM, "v": VMEM, "h": HBM, "f": HBM}
    return pl.pallas_call(
        whole,
        out_shape=[jax.ShapeDtypeStruct(shape, dtype) for shape, dtype in out],
        in_specs=[spec[kind] for kind in ins],
        out_specs=[spec[kind] for kind in outs],
        scratch_shapes=scratch,
        compiler_params=pltpu.CompilerParams(vmem_limit_bytes=vmem * 1024 * 1024),
        cost_estimate=pl.CostEstimate(flops=int(us * 1e9), bytes_accessed=0, transcendentals=0),
        name=name,
    )(*args)


def dot(left, right):
    return lax.dot_general(left, right, (((1,), (0,)), ((), ())), preferred_element_type=F32)


def dot_right(left, right):
    return lax.dot_general(left, right, (((1,), (1,)), ((), ())), preferred_element_type=F32)


def dot_left(left, right):
    return lax.dot_general(left, right, (((0,), (0,)), ((), ())), preferred_element_type=F32)


def from_core(x):
    return lax.ppermute(x, "kv", [(0, 1), (1, 0)])


def back_x(x, k):
    return lax.ppermute(x, "dp", [(i, (i + k) % SIDE) for i in range(SIDE)])


def back_y(x, k):
    pairs = [(z * SIDE + y, z * SIDE + (y + k) % SIDE) for z in range(SIDE) for y in range(SIDE)]
    return lax.ppermute(x, "ctx", pairs)


def back_z(x, k):
    pairs = [(z * SIDE + y, (z + k) % SIDE * SIDE + y) for z in range(SIDE) for y in range(SIDE)]
    return lax.ppermute(x, "ctx", pairs)


def group_round(x, i, back=False):
    pairs = [(n, 2 * ((n % 4 + i) % SIDE) + n // 4) for n in range(8)]
    if back:
        pairs = [(b, a) for a, b in pairs]
    return lax.ppermute(x, ("dp", "kv"), pairs)


def all_to_all(x):
    return lax.all_to_all(x, "ctx", split_axis=0, concat_axis=0, tiled=True)


def ring(send, x):
    got = {k: send(x, k) for k in (1, 3, 2)}
    return [x, got[1], got[2], got[3]]


def ring_back(send, parts):
    got = {k: send(parts[k], SIDE - k) for k in (1, 3, 2)}
    return [parts[0], got[1], got[2], got[3]]


def norm_rows(rows, gain):
    inverse = lax.rsqrt(jnp.mean(rows * rows, axis=-1, keepdims=True) + EPS)
    return rows * inverse * gain, inverse


def norm_back(rows, gain, incoming):
    inverse = lax.rsqrt(jnp.mean(rows * rows, axis=-1, keepdims=True) + EPS)
    normed = rows * inverse
    scaled = incoming * gain
    grad = inverse * (scaled - normed * jnp.mean(scaled * normed, axis=-1, keepdims=True))
    return grad, jnp.sum(incoming * normed, axis=0, keepdims=True)


def lane(shape):
    return lax.broadcasted_iota(jnp.int32, shape, len(shape) - 1)


def swap_halves(x):
    return jnp.where(lane(x.shape) % HEAD < HEAD // 2, pltpu.roll(x, 96, 1), pltpu.roll(x, 32, 1))


CTX, DP, KV, STARTS = 0, 1, 2, 3


def doc_start(place, p):
    start = jnp.zeros_like(p)
    for i in range(8):
        b = place[STARTS + i]
        start = jnp.where(p >= b, jnp.maximum(start, b), start)
    return start


def span_places(shape, dim, chip, kv):
    i = lax.broadcasted_iota(jnp.int32, shape, dim)
    half = jnp.where(i < TOK, kv, 1 - kv)
    return chip * SPAN + half * TOK + i % TOK


def rotary(place):
    spot = span_places((SPAN, 128), 0, place[CTX], place[KV])
    index = lane((SPAN, 128)) % HEAD
    freq = jnp.exp((index % (HEAD // 2)).astype(F32) * (-2.0 * math.log(10000.0) / HEAD))
    angle = (spot - doc_start(place, spot)).astype(F32) * freq
    return jnp.cos(angle), jnp.where(index < HEAD // 2, -1.0, 1.0) * jnp.sin(angle)


def one_hot(target, first, count):
    rows = lax.broadcasted_iota(jnp.int32, (count, target.shape[1]), 0) + first
    return jnp.where(rows == target, 1.0, 0.0).astype(BF16)


def owner_column(place, ctx, turn):
    return ((place[DP] - turn) & 3) * 16 + ctx


def qkv_target(place):
    row = lane((1, 640))
    ctx, inner = row // 40, row % 40
    value = inner >= 32
    turn = jnp.where(value, inner % 8, inner // 8)
    col = owner_column(place, ctx, turn)
    target = jnp.where(inner % 8 < 7, 7 * col + inner % 8, QCOL + col)
    return jnp.where(value, jnp.where(turn < 4, QCOL + HEAD + col, -1), target)


def out_order(place):
    row = lane((1, QCOL))
    kind = row % 8 - 1
    target = 7 * owner_column(place, row // 32, row // 8 % 4) + kind
    return one_hot(jnp.where(kind >= 0, target, -1), 0, QCOL)


def normed_input(x0, x1, gain):
    rows = jnp.concatenate([x0()[...], x1()[...]], axis=0).astype(F32)
    return norm_rows(rows, gain)[0]


def kv_kernel(place, x0, x1, gain, w, kv_out, w_out):
    cos, sin = rotary(place)
    order = one_hot(qkv_target(place), QCOL, 128)
    rows = normed_input(x0, x1, gain[...]).astype(BF16)
    w_cols = dot(order, w()[...]).astype(BF16)
    w_out[...] = w_cols
    u = dot_right(rows, w_cols)
    kv = jnp.where(lane((SPAN, 128)) < HEAD, u * cos + swap_halves(u) * sin, u).astype(BF16)
    for j in range(BLOCKS):
        kv_out[j] = kv


def query_kernel(place, x0, x1, gain, w, after, q_out, w_out):
    cos, sin = rotary(place)
    order = one_hot(qkv_target(place), 0, QCOL)
    rows = normed_input(x0, x1, gain[...]).astype(BF16)
    w_cols = dot(order, w()[...]).astype(BF16)
    w_out[...] = w_cols
    raw = dot_right(rows, w_cols)
    for j in range(4):
        u = raw[:, 128 * j : 128 * (j + 1)]
        q_out[:, 128 * j : 128 * (j + 1)] = ((u * cos + swap_halves(u) * sin) * QSCALE).astype(BF16)


def spread_heads(q, out):
    low = lane((SPAN, 128)) < HEAD
    for j in range(4):
        u = q[:, 128 * j : 128 * (j + 1)].astype(F32)
        out[2 * j] = jnp.where(low, u, 0.0).astype(BF16)
        if j < 3:
            out[2 * j + 1] = jnp.where(low, pltpu.roll(u, HEAD, 1), 0.0).astype(BF16)


def attn_project_kernel(place, w, o, own_out, other_out, w_out):
    wo = dot(out_order(place), w()[...]).astype(BF16)
    w_out[...] = wo
    attn = dot(o()[...], wo)
    own_out[...] = attn[:TOK]
    other_out[...] = attn[TOK:].astype(BF16)


def block_ranges(place, n):
    first = place[CTX] * SPAN
    low_start, high_start = doc_start(place, first), doc_start(place, first + SPAN - 1)
    active = (n <= place[CTX]) & (n * SPAN + SPAN - 1 >= low_start)
    full = (n < place[CTX]) & (n * SPAN >= high_start)
    return active, full


def query_places(place, pos_ref, start_ref):
    pos = span_places((SPAN, SPAN), 0, place[CTX], place[KV])
    pos_ref[...] = pos
    start_ref[...] = doc_start(place, pos)


def allowed_keys(place, source, pos_ref, start_ref):
    keys = span_places((SPAN, SPAN), 1, source, place[KV])
    return (keys <= pos_ref[...]) & (keys >= start_ref[...])


def attend_kernel(place, q_cols, blocks, o_out, inv_out, q, acc, pos_ref, start_ref):
    query_places(place, pos_ref, start_ref)
    acc[...] = jnp.zeros_like(acc)
    spread_heads(q_cols(), q)
    blocks = blocks()
    low = lane((SPAN, 128)) < HEAD

    @pl.loop(0, BLOCKS)
    def _(n):
        active, full = block_ranges(place, n)

        def step(masked):
            kv = blocks[n]
            ones_v = jnp.where(low, jnp.ones_like(kv), kv)
            if masked:
                allowed = allowed_keys(place, n, pos_ref, start_ref)
            s = dot_right(q[...].reshape(GROUP * SPAN, 128), kv)
            p = jnp.exp2(jnp.tanh(s * (1.0 / CAP)) * EXP2)
            if masked:
                p = jnp.where(allowed[None], p.reshape(GROUP, SPAN, SPAN), 0.0).reshape(GROUP * SPAN, SPAN)
            acc[...] += dot(p.astype(BF16), ones_v).reshape(GROUP, SPAN, 128)

        pl.when(full)(lambda: step(False))
        pl.when(active & jnp.logical_not(full))(lambda: step(True))

    lanes = lane((SPAN, 128))
    inverse = jnp.ones((SPAN, 128), F32)
    for j in range(4):
        a = acc[2 * j]
        if j < 3:
            b = acc[2 * j + 1]
            total = jnp.where(low, a, pltpu.roll(b, HEAD, 1))
            value = jnp.where(low, pltpu.roll(a, HEAD, 1), b)
            inverse = jnp.where(lanes == 2 * j + 1, 1.0 / b, inverse)
        else:
            total = jnp.where(low, a, 1.0)
            value = jnp.where(low, pltpu.roll(a, HEAD, 1), 0.0)
        inverse = jnp.where(lanes == 2 * j, 1.0 / a, inverse)
        o_out[:, 128 * j : 128 * (j + 1)] = (value / total).astype(BF16)
    inv_out[...] = inverse


def attend_back_kernel(
    place, d0, d1, wo, q_cols, o, inv, blocks,
    dq_out, grads, q, dq, do_ext, both_t, pos_ref, start_ref,
):
    query_places(place, pos_ref, start_ref)
    dq[...] = jnp.zeros_like(dq)
    rows = jnp.concatenate([d0()[...], d1()[...]], axis=0)
    d_o = dot_right(rows, wo()[...]).astype(BF16).astype(F32)
    low = lane((SPAN, 128)) < HEAD
    lanes = lane((SPAN, 128))
    spread_heads(q_cols(), q)
    o, inv = o(), inv()
    for h in range(GROUP):
        j = h // 2
        cols = slice(128 * j, 128 * (j + 1))
        mine = low if h % 2 == 0 else jnp.logical_not(low)
        scale = inv[:, h : h + 1]
        up = d_o[:, cols] * scale
        delta = jnp.sum(jnp.where(mine, up * o[:, cols].astype(F32), 0.0), axis=1, keepdims=True)
        if h % 2 == 0:
            up = pltpu.roll(up, HEAD, 1)
        high = delta.astype(BF16).astype(F32)
        ext = jnp.where(lanes == 0, -high, jnp.where(lanes == 1, high - delta, jnp.where(low, 0.0, up)))
        do_ext[h] = ext.astype(BF16)
        both_t[:, SPAN * h : SPAN * (h + 1)] = jnp.transpose(jnp.where(low, q[h].astype(F32), up)).astype(BF16)
    blocks = blocks()

    @pl.loop(0, BLOCKS)
    def _(n):
        active, full = block_ranges(place, n)

        def step(masked):
            kv = blocks[n]
            ones_v = jnp.where(low, jnp.ones_like(kv), kv)
            if masked:
                allowed = allowed_keys(place, n, pos_ref, start_ref)
            s = dot_right(q[...].reshape(GROUP * SPAN, 128), kv)
            dp = dot_right(do_ext[...].reshape(GROUP * SPAN, 128), ones_v)
            t = jnp.tanh(s * (1.0 / CAP))
            p = jnp.exp2(t * EXP2)
            if masked:
                p = jnp.where(allowed[None], p.reshape(GROUP, SPAN, SPAN), 0.0).reshape(GROUP * SPAN, SPAN)
            ds = (p * dp * (1.0 - t * t)).astype(BF16)
            dq[...] += dot(ds, kv).reshape(GROUP, SPAN, 128)
            dk = dot(both_t[pl.ds(0, HEAD), :], ds)
            dv = dot(both_t[pl.ds(HEAD, HEAD), :], p.astype(BF16))
            grads[n] = jnp.concatenate([dk, dv], axis=0).astype(BF16)

        pl.when(full)(lambda: step(False))
        pl.when(active & jnp.logical_not(full))(lambda: step(True))

        @pl.when(jnp.logical_not(active))
        def _():
            grads[n] = jnp.zeros((128, SPAN), BF16)

    cos, sin = rotary(place)
    for j in range(4):
        u = dq[2 * j]
        if j < 3:
            u = jnp.where(low, u, pltpu.roll(dq[2 * j + 1], HEAD, 1))
        else:
            u = jnp.where(low, u, 0.0)
        u = u * QSCALE
        dq_out[:, 128 * j : 128 * (j + 1)] = (u * cos - swap_halves(u) * sin).astype(BF16)


def query_grad_kernel(place, dq, o, x0, x1, d0, d1, gain, w_grad, after, left):
    row = lane((1, WIDTH))
    kind = row % 14
    target = 7 * owner_column(place, row // 56, row // 14 % 4) + kind % 7
    after[...] = jnp.zeros_like(after)
    left[pl.ds(0, SPAN), :] = dot(dq()[...], one_hot(jnp.where(kind < 7, target, -1), 0, QCOL)).astype(BF16)
    left[pl.ds(SPAN, SPAN), :] = dot(o()[...], one_hot(jnp.where(kind < 7, -1, target), 0, QCOL)).astype(BF16)
    rows = normed_input(x0, x1, gain[...]).astype(BF16)
    right = jnp.concatenate([rows, d0()[...], d1()[...]], axis=0)
    for j in range(0, WIDTH, 256):
        cols = slice(j, min(j + 256, WIDTH))
        w_grad[cols, :] = dot_left(left[:, cols], right).astype(BF16)


def project_back_kernel(
    place, dkv_parts, dq, w_q, w_kv, x0, x1, gain, g2, g3, g4, g5, after,
    own_out, other_out, w_grad,
):
    cos, sin = rotary(place)
    row = lane((1, SPAN))
    kind = row % 16
    target = kind % 2 * HEAD + owner_column(place, row // 16, kind // 2)
    order = one_hot(jnp.where(kind < 8, target, -1), 0, 128)
    normed = normed_input(x0, x1, 1.0)
    d_a = dot(dq()[...], w_q()[...])
    dkv_parts = dkv_parts()
    dkv = dkv_parts[0].astype(F32)
    for j in range(1, BLOCKS):
        dkv += dkv_parts[j].astype(F32)
    u = jnp.transpose(dkv)
    dkv = jnp.where(lane((SPAN, 128)) < HEAD, u * cos - swap_halves(u) * sin, u).astype(BF16)
    d_a += dot(dkv, w_kv()[...])
    own_out[...] = d_a[:TOK]
    other_out[...] = d_a[TOK:].astype(BF16)
    g1 = jnp.sum(normed * d_a, axis=0, keepdims=True)
    gains = jnp.concatenate([g1, g2[...], g3[...], g4[...], g5[...], jnp.zeros((3, WIDTH), F32)], axis=0)
    part = dot_left(dot(dkv, order).astype(BF16), (normed * gain[...]).astype(BF16))
    part = part.reshape(BLOCKS, 16, WIDTH) + jnp.concatenate([jnp.zeros((8, WIDTH), F32), gains], axis=0)[None]
    w_grad[...] = part.reshape(SPAN, WIDTH).astype(BF16)


def attn_norm_kernel(x, own, other, gain_b, gain_c, attn_out, r_out, m_out):
    attn = own[...] + other[...].astype(F32)
    attn_out[...] = attn
    resid = x[...].astype(F32) + norm_rows(attn, gain_b[...])[0]
    r_out[...] = resid
    m_out[...] = norm_rows(resid, gain_c[...])[0].astype(BF16)


def sum_parts(own, b, c, d):
    return (own[...] + b[...].astype(F32)) + (c[...].astype(F32) + d[...].astype(F32))


def ffn_norm_kernel(own, b, c, d, resid, cotangent, gain, out, d_out, gain_out):
    fo = sum_parts(own, b, c, d)
    out[...] = (resid[...] + norm_rows(fo, gain[...])[0]).astype(BF16)
    grad, gain_grad = norm_back(fo, gain[...], cotangent[...].astype(F32))
    d_out[...] = grad.astype(BF16)
    gain_out[...] = gain_grad


def ffn_back_norm_kernel(own, b, c, d, resid, attn, cotangent, gain_c, gain_b, r_out, d_out, gain_c_out, gain_b_out):
    d_m = sum_parts(own, b, c, d)
    grad, gain_grad = norm_back(resid[...], gain_c[...], d_m)
    gain_c_out[...] = gain_grad
    d_resid = cotangent[...].astype(F32) + grad
    r_out[...] = d_resid
    grad, gain_grad = norm_back(attn[...], gain_b[...], d_resid)
    gain_b_out[...] = gain_grad
    d_out[...] = grad.astype(BF16)


def input_norm_kernel(own, other, x, d_resid, gain, out):
    d_a = own[...] + other[...].astype(F32)
    out[...] = d_resid[...] + norm_back(x[...].astype(F32), gain[...], d_a)[0]


def gelu_parts(u):
    t = jnp.tanh(GELU_C * (u + 0.044715 * u * u * u))
    active = 0.5 * u * (1.0 + t)
    slope = 0.5 * (1.0 + t) + 0.5 * u * (1.0 - t * t) * GELU_C * (1.0 + 3.0 * 0.044715 * u * u)
    return active, slope


def weight_runs(which):
    runs, at = [], which * HALF_UNITS
    while at < (which + 1) * HALF_UNITS:
        count = min(TOK - at % TOK, (which + 1) * HALF_UNITS - at)
        runs.append((at // TOK, at % TOK, at - which * HALF_UNITS, count))
        at += count
    return runs


def arrange_kernel(place, pieces, gate, up, down, sems):
    copies = []
    for which, dest in enumerate((gate, up, down)):
        for core in range(2):
            source = place[KV] if core == 0 else 1 - place[KV]
            for quarter, row, unit, count in weight_runs(which):
                copies.append(
                    pltpu.make_async_copy(
                        pieces.at[2 * quarter + source, :, pl.ds(row, count), :],
                        dest.at[pl.ds(core * SIDE, SIDE), pl.ds(unit, count), :],
                        sems.at[len(copies)],
                    )
                )
    for c in copies:
        c.start()
    for c in copies:
        c.wait()


def dequantise_kernel(place, gate, up, down, gate_scale, up_scale, down_scale, out, codes, sems):
    out[...] = jnp.zeros((TOK, WIDTH), BF16)

    def fill(core, quarter):
        runs = []
        for which in range(3):
            for part, row, unit, count in weight_runs(which):
                first = core * HALF_UNITS + unit
                count = min(count, UNITS - first)
                if part == quarter:
                    runs.append((which, row, first, count))
        copies = [
            pltpu.make_async_copy(
                (gate, up, down)[which].at[pl.ds(first, count), :], codes.at[pl.ds(row, count), :], sems.at[n]
            )
            for n, (which, row, first, count) in enumerate(runs)
        ]
        for c in copies:
            c.start()
        for c in copies:
            c.wait()
        for which, row, first, count in runs:
            c = codes[pl.ds(row, count), :]
            if which == 0:
                weight = c.astype(F32) * gate_scale[pl.ds(first, count), :]
            elif which == 1:
                weight = ((c & -16) + 8).astype(F32) * up_scale[pl.ds(first, count), :]
            else:
                weight = ((c & -64) + 32).astype(F32) * down_scale[...]
            out[pl.ds(row, count), :] = weight.astype(BF16)

    for core in range(2):
        for quarter in range(SIDE):
            pl.when((place[KV] == core) & (place[DP] == quarter))(lambda c=core, q=quarter: fill(c, q))


def ffn_kernel(m0, m1, m2, m3, gate_w, up_w, down_w, f0, f1, f2, f3, gate_out, up_out, m, acc):
    for j, part in enumerate((m0, m1, m2, m3)):
        m[pl.ds(TOK * j, TOK), :] = part[...]
    for n in range(HID // 256):
        units = pl.ds(256 * n, 256)
        gate = dot_right(m[...], gate_w[units, :])
        up = dot_right(m[...], up_w[units, :])
        gate_out[:, 256 * n : 256 * (n + 1)] = gate.astype(BF16)
        up_out[:, 256 * n : 256 * (n + 1)] = up.astype(BF16)
        hidden = (gelu_parts(gate)[0] * up).astype(BF16)
        part = dot(hidden, down_w[units, :])
        if n == 0:
            acc[...] = part
        else:
            acc[...] += part
    f0[...] = acc[pl.ds(0, TOK), :]
    for j, out in enumerate((f1, f2, f3)):
        out[...] = acc[pl.ds(TOK * (j + 1), TOK), :].astype(BF16)


def ffn_back_kernel(
    e0, e1, e2, e3, gate_in, up_in, gate_w, up_w, down_w, f0, f1, f2, f3, hidden_out, gate_out, up_out, e, acc
):
    for j, part in enumerate((e0, e1, e2, e3)):
        e[pl.ds(TOK * j, TOK), :] = part[...]
    for n in range(HID // 256):
        units = pl.ds(256 * n, 256)
        cols = slice(256 * n, 256 * (n + 1))
        d_hidden = dot_right(e[...], down_w[units, :])
        active, slope = gelu_parts(gate_in[:, cols].astype(F32))
        up = up_in[:, cols].astype(F32)
        hidden_out[:, cols] = (active * up).astype(BF16)
        d_gate = (d_hidden * up * slope).astype(BF16)
        d_up = (d_hidden * active).astype(BF16)
        gate_out[:, cols] = d_gate
        up_out[:, cols] = d_up
        part = dot(d_gate, gate_w[units, :]) + dot(d_up, up_w[units, :])
        if n == 0:
            acc[...] = part
        else:
            acc[...] += part
    f0[...] = acc[pl.ds(0, TOK), :]
    for j, out in enumerate((f1, f2, f3)):
        out[...] = acc[pl.ds(TOK * (j + 1), TOK), :].astype(BF16)


def ffn_weight_kernel(
    place, m0, m1, m2, m3, e0, e1, e2, e3, hidden, d_gate, d_up, down_w, down_scale, out, scale_out, m, e
):
    for j, (a, b) in enumerate(zip((m0, m1, m2, m3), (e0, e1, e2, e3))):
        m[pl.ds(TOK * j, TOK), :] = a[...]
        e[pl.ds(TOK * j, TOK), :] = b[...]
    empty = SIDE * TOK - 3 * HALF_UNITS
    out[pl.ds(2 * SIDE - 2, 2), :, pl.ds(TOK - empty, empty), :] = jnp.zeros((2, SIDE, empty, WIDTH), BF16)
    per_unit = 1.0 / down_scale[...]
    scale_grad = jnp.zeros((1, WIDTH), F32)
    for which, (left, right) in enumerate(((d_gate, m), (d_up, m), (hidden, e))):
        runs = weight_runs(which)
        for n in range(HID // 256):
            first = 256 * n
            part = dot_left(left[:, first : first + 256], right[...])
            if which == 2:
                level = down_w[pl.ds(first, 256), :].astype(F32) * per_unit
                level = jnp.floor(level * (1.0 / 64.0)) * 64.0 + 32.0
                scale_grad += jnp.sum(part * level, axis=0, keepdims=True)
            part = part.astype(BF16)
            for piece in range(2 * SIDE):
                core = place[KV] if piece < SIDE else 1 - place[KV]
                for quarter, row, unit, count in runs:
                    low = max(piece * HALF_UNITS + unit, first)
                    high = min(piece * HALF_UNITS + unit + count, first + 256)
                    if low < high:
                        at = row + low - piece * HALF_UNITS - unit
                        out[2 * quarter + core, piece % SIDE, pl.ds(at, high - low), :] = part[low - first : high - first]
    scale_out[...] = scale_grad


def finish_kernel(parts, gate, up, gate_scale, up_scale, down_scale, g_gate, g_up, g_down, s_gate, s_up, sums):
    sums[...] = jnp.zeros_like(sums)
    for core in range(2):
        for which in range(3):
            for quarter, row, unit, count in weight_runs(which):
                first = core * HALF_UNITS + unit
                count = min(count, UNITS - first)
                rows = pl.ds(first, count)
                total = parts[2 * quarter + core, pl.ds(row, count), :].astype(F32)
                if which == 0:
                    g_gate[rows, :] = total * gate_scale[rows, :]
                    part = jnp.sum(total * gate[rows, :].astype(F32), axis=1, keepdims=True)
                    sums[0, rows, :] = jnp.broadcast_to(part, (count, 128))
                elif which == 1:
                    g_up[rows, :] = total * up_scale[rows, :]
                    part = jnp.sum(total * ((up[rows, :] & -16) + 8).astype(F32), axis=1, keepdims=True)
                    sums[1, rows, :] = jnp.broadcast_to(part, (count, 128))
                else:
                    g_down[rows, :] = total * down_scale[...]
    s_gate[...] = jnp.transpose(sums[0])[:1, :UNITS]
    s_up[...] = jnp.transpose(sums[1])[:1, :UNITS]


def shards(
    layer_input, cotangent, doc_bounds, w_query, key_weight, value_weight, w_out,
    gain_attn_in, gain_attn_out, gain_ffn_in, gain_ffn_out,
    code_gate, code_up, code_down, scale_gate, scale_up, scale_down,
):
    ctx, kv, dp = lax.axis_index("ctx"), lax.axis_index("kv"), lax.axis_index("dp")
    place = jnp.concatenate([jnp.stack([ctx, dp, kv]).astype(jnp.int32), doc_bounds[0]])
    x = layer_input.reshape(TOK, WIDTH)
    cot = cotangent.reshape(TOK, WIDTH)
    gain_1, gain_2, gain_3, gain_4 = (
        g.reshape(1, WIDTH) for g in (gain_attn_in, gain_attn_out, gain_ffn_in, gain_ffn_out)
    )
    gate_col, up_col, down_row = scale_gate[:, None], scale_up[:, None], scale_down[None, :]
    rows_f32, rows_bf16, row_f32 = ((TOK, WIDTH), F32), ((TOK, WIDTH), BF16), ((1, WIDTH), F32)

    shard = jnp.concatenate([w_query.T, key_weight.T, value_weight.T, w_out.T], axis=0)
    rounds = [group_round(shard, i) for i in range(4)]
    x_other = from_core(x)

    (quarter,) = kernel_call(
        dequantise_kernel,
        "shhhvvv",
        "v",
        [rows_bf16],
        "dequantise",
        (place, code_gate.T, code_up.T, code_down, gate_col, up_col, down_row),
        [pltpu.VMEM((TOK, WIDTH), jnp.int32), pltpu.SemaphoreType.DMA((2,))],
        vmem=58,
    )
    quarters = ring(back_y, quarter)

    qkv_rows = jnp.concatenate(
        [r[:8] for r in rounds] + [r[8:9] for r in rounds] + [jnp.zeros((4, WIDTH), BF16)], axis=0
    )
    out_rows = jnp.concatenate([r[8:] for r in rounds], axis=0)
    qkv_rows, out_rows, x_other = lax.optimization_barrier((qkv_rows, out_rows, x_other))

    def gathered(rows):
        copies = jnp.broadcast_to(rows[None], (BLOCKS,) + rows.shape)
        return all_to_all(copies).reshape(-1, WIDTH)

    qkv_rows = gathered(qkv_rows)

    keys, w_kv = kernel_call(
        kv_kernel,
        "sffvf",
        "ff",
        [((BLOCKS, SPAN, 128), BF16), ((128, WIDTH), BF16)],
        "keys",
        (place, x, x_other, gain_1, qkv_rows),
        us=4,
        vmem=58,
    )
    out_rows, quarters, after = lax.optimization_barrier((out_rows, quarters, w_kv))
    ffn_w = lax.all_gather(jnp.stack(quarters), ("dp", "kv"))
    out_rows = gathered(out_rows)
    keys = all_to_all(keys)
    q, w_q = kernel_call(
        query_kernel,
        "sffvfh",
        "ff",
        [((SPAN, QCOL), BF16), ((QCOL, WIDTH), BF16)],
        "queries",
        (place, x, x_other, gain_1, qkv_rows, after),
        us=4,
        vmem=58,
    )
    o, inv = kernel_call(
        attend_kernel,
        "sff",
        "ff",
        [((SPAN, QCOL), BF16), ((SPAN, 128), F32)],
        "attend",
        (place, q, keys),
        [
            pltpu.VMEM((GROUP, SPAN, 128), BF16),
            pltpu.VMEM((GROUP, SPAN, 128), F32),
            pltpu.VMEM((SPAN, SPAN), jnp.int32),
            pltpu.VMEM((SPAN, SPAN), jnp.int32),
        ],
        us=16,
        vmem=58,
    )
    attn_own, attn_other, wo = kernel_call(
        attn_project_kernel,
        "sff",
        "vvf",
        [rows_f32, rows_bf16, ((QCOL, WIDTH), BF16)],
        "attn_project",
        (place, out_rows, o),
        vmem=58,
    )
    attn_other = from_core(attn_other)
    attn, resid, m_own = kernel_call(
        attn_norm_kernel,
        "vvvvv",
        "vvv",
        [rows_f32, rows_f32, rows_bf16],
        "attn_norm",
        (x, attn_own, attn_other, gain_2, gain_3),
    )

    m_parts = ring(back_z, m_own)
    m_parts[1], ffn_w = lax.optimization_barrier((m_parts[1], ffn_w))
    wide = ((SIDE * TOK, HID), BF16)
    unit_rows = ((2 * SIDE, HALF_UNITS, WIDTH), BF16)
    ffn_w = kernel_call(
        arrange_kernel,
        "sh",
        "vvv",
        [unit_rows] * 3,
        "arrange",
        (place, ffn_w),
        [pltpu.SemaphoreType.DMA((12,))],
        us=4,
    )
    gate_w, up_w, down_w = (w.reshape(HID, WIDTH) for w in ffn_w)
    ffn_scratch = [pltpu.VMEM((SIDE * TOK, WIDTH), BF16), pltpu.VMEM((SIDE * TOK, WIDTH), F32)]
    *fo_parts, gate, up = kernel_call(
        ffn_kernel,
        "vvvvvvv",
        "vvvvvv",
        [rows_f32] + [rows_bf16] * 3 + [wide, wide],
        "ffn",
        (*m_parts, gate_w, up_w, down_w),
        ffn_scratch,
        us=6,
        vmem=16,
    )
    fo_parts = ring_back(back_z, fo_parts)
    block_out, d_fo, g_gain_4 = kernel_call(
        ffn_norm_kernel, "vvvvvvv", "vvv", [rows_bf16, rows_bf16, row_f32], "ffn_norm", (*fo_parts, resid, cot, gain_4)
    )

    d_parts = ring(back_z, d_fo)
    *dm_parts, hidden, d_gate, d_up = kernel_call(
        ffn_back_kernel,
        "vvvvvvvvv",
        "vvvvvvv",
        [rows_f32] + [rows_bf16] * 3 + [wide] * 3,
        "ffn_back",
        (*d_parts, gate, up, gate_w, up_w, down_w),
        ffn_scratch,
        us=10,
        vmem=20,
    )
    dm_parts = ring_back(back_z, dm_parts)
    weight_grads, g_down = kernel_call(
        ffn_weight_kernel,
        "s" + "v" * 13,
        "fv",
        [((2 * SIDE, SIDE, TOK, WIDTH), BF16), row_f32],
        "ffn_weight",
        (place, *m_parts, *d_parts, hidden, d_gate, d_up, down_w, down_row),
        [
            pltpu.VMEM((SIDE * TOK, WIDTH), BF16),
            pltpu.VMEM((SIDE * TOK, WIDTH), BF16),
        ],
        us=8,
        vmem=20,
    )
    dm_parts, weight_grads = lax.optimization_barrier((dm_parts, weight_grads))
    weight_grads = lax.psum_scatter(weight_grads, ("dp", "kv"), scatter_dimension=0)
    d_resid, d_attn, g_gain_3, g_gain_2 = kernel_call(
        ffn_back_norm_kernel,
        "vvvvvvvvv",
        "vvvv",
        [rows_f32, rows_bf16, row_f32, row_f32],
        "ffn_back_norm",
        (*dm_parts, resid, attn, cot, gain_3, gain_2),
    )
    d_attn_other = from_core(d_attn)

    dq, key_grads = kernel_call(
        attend_back_kernel,
        "sfffffff",
        "ff",
        [((SPAN, QCOL), BF16), ((BLOCKS, 128, SPAN), BF16)],
        "attend_back",
        (place, d_attn, d_attn_other, wo, q, o, inv, keys),
        [
            pltpu.VMEM((GROUP, SPAN, 128), BF16),
            pltpu.VMEM((GROUP, SPAN, 128), F32),
            pltpu.VMEM((GROUP, SPAN, 128), BF16),
            pltpu.VMEM((128, GROUP * SPAN), BF16),
            pltpu.VMEM((SPAN, SPAN), jnp.int32),
            pltpu.VMEM((SPAN, SPAN), jnp.int32),
        ],
        us=26,
        vmem=58,
    )
    key_grads = all_to_all(key_grads)
    q_grads, after = kernel_call(
        query_grad_kernel,
        "sffffffv",
        "fv",
        [((WIDTH, WIDTH), BF16), ((8, 128), F32)],
        "query_grad",
        (place, dq, o, x, x_other, d_attn, d_attn_other, gain_1),
        [pltpu.VMEM((2 * SPAN, WIDTH), BF16)],
        us=5,
        vmem=58,
    )
    q_grads = all_to_all(q_grads.reshape(BLOCKS, 56, WIDTH))
    da_own, da_other, kv_grads = kernel_call(
        project_back_kernel,
        "sffffffvvvvvv",
        "vvf",
        [rows_f32, rows_bf16, ((SPAN, WIDTH), BF16)],
        "project_back",
        (place, key_grads, dq, w_q, w_kv, x, x_other, gain_1, g_gain_2, g_gain_3, g_gain_4, g_down, after),
        us=4,
        vmem=58,
    )
    weight_grads, da_other = lax.optimization_barrier((weight_grads, da_other))
    weight_grads = weight_grads.reshape(SIDE, TOK, WIDTH)
    a, b, c, d = ring_back(back_y, [weight_grads[k] for k in range(SIDE)])
    eighth = ((a.astype(F32) + b.astype(F32)) + (c.astype(F32) + d.astype(F32))).astype(BF16)
    eighths = lax.all_gather(eighth, ("dp", "kv"))

    (grad_input,) = kernel_call(
        input_norm_kernel, "vvvvv", "v", [rows_f32], "input_norm", (da_own, from_core(da_other), x, d_resid, gain_1)
    )

    kv_grads, q_grads, grad_input = lax.optimization_barrier((kv_grads, q_grads, grad_input))
    kv_grads = all_to_all(kv_grads.reshape(BLOCKS, 16, WIDTH))

    grad_code_gate, grad_code_up, grad_code_down, grad_scale_gate, grad_scale_up = kernel_call(
        finish_kernel,
        "vvvvvv",
        "vvvvv",
        [((UNITS, WIDTH), F32)] * 3 + [((1, UNITS), F32)] * 2,
        "finish",
        (eighths, code_gate.T, code_up.T, gate_col, up_col, down_row),
        [pltpu.VMEM((2, 384, 128), F32)],
        us=3,
    )
    grads = (grad_code_gate, grad_code_up, grad_code_down, grad_scale_gate[0], grad_scale_up[0])

    q_grads = jnp.sum(q_grads.astype(F32), axis=0)
    kv_grads = jnp.sum(kv_grads.astype(F32), axis=0)
    gains = kv_grads[8:] + from_core(kv_grads[8:])
    sums = [jnp.concatenate([q_grads[14 * i : 14 * i + 14], kv_grads[2 * i : 2 * i + 2], gains], axis=0) for i in range(4)]
    sums = [group_round(part.astype(BF16), i, back=True).astype(F32) for i, part in enumerate(sums)]
    grad_w = (sums[0] + sums[1]) + (sums[2] + sums[3])
    gains = grad_w[16:]

    return (
        block_out.reshape(layer_input.shape),
        grad_input.reshape(layer_input.shape),
        grad_w[:7].T,
        grad_w[14:15].T,
        grad_w[15:16].T,
        grad_w[7:14].T,
        gains[0],
        gains[1],
        gains[2],
        gains[3],
        grads[0].T,
        grads[1].T,
        *grads[2:],
        gains[4],
    )


def solution(mesh):
    tokens = P("dp", "ctx", "kv", None, None)
    columns = P(None, ("dp", "kv", "ctx"))
    hidden = (P(None, "ctx"), P(None, "ctx"), P("ctx", None), P("ctx"), P("ctx"), P())
    return jax.shard_map(
        shards,
        mesh=mesh,
        in_specs=(tokens, tokens, P("dp", None)) + (columns,) * 4 + (P(),) * 4 + hidden,
        out_specs=(tokens, tokens) + (columns,) * 4 + (P(),) * 4 + hidden,
        check_vma=False,
    )
```

```python
import math

import jax
import jax.numpy as jnp
from jax import lax
from jax.experimental import pallas as pl
from jax.experimental.pallas import tpu as pltpu
from jax.sharding import PartitionSpec as P

EPS = 1e-06
CAP = 50.0
QSCALE = 0.125
GELU_C = math.sqrt(2.0 / math.pi)
EXP2 = CAP * math.log2(math.e)

TOK = 128
SPAN = 256
WIDTH = 896
HEAD = 64
GROUP = 7
QCOL = 512
SIDE = 4
UNITS = 304
UPAD = 320
HALF_UNITS = 160
HID = 1280
HALF_ROWS = 512
BLOCKS = 16
F32 = jnp.float32
BF16 = jnp.bfloat16
VMEM = pl.BlockSpec(memory_space=pltpu.VMEM)
SMEM = pl.BlockSpec(memory_space=pltpu.SMEM)
HBM = pl.BlockSpec(memory_space=pltpu.HBM)


class Fetched:
    def __init__(self, copy, buffer):
        self.copy, self.buffer = copy, buffer

    def __call__(self):
        if self.copy is not None:
            self.copy.wait()
            self.copy = None
        return self.buffer


def kernel_call(body, ins, outs, out, name, args, scratch=(), us=2.0, vmem=16):
    fetched = [i for i, kind in enumerate(ins) if kind == "f"]
    stored = [i for i, kind in enumerate(outs) if kind == "f"]
    count = len(fetched) + len(stored)

    def whole(*refs):
        if not count:
            return body(*refs)
        sems, buffers = refs[-1], refs[len(refs) - 1 - count : -1]
        refs = list(refs[: len(refs) - 1 - count])
        copies = [pltpu.make_async_copy(refs[i], buffers[n], sems.at[n]) for n, i in enumerate(fetched)]
        for c in copies:
            c.start()
        for n, i in enumerate(fetched):
            refs[i] = Fetched(copies[n], buffers[n])
        back = []
        for n, i in enumerate(stored, len(fetched)):
            back.append(pltpu.make_async_copy(buffers[n], refs[len(ins) + i], sems.at[n]))
            refs[len(ins) + i] = buffers[n]
        body(*refs)
        for c in back:
            c.start()
        for c in back:
            c.wait()

    scratch = list(scratch)
    if count:
        scratch += [pltpu.VMEM(args[i].shape, args[i].dtype) for i in fetched]
        scratch += [pltpu.VMEM(*out[i]) for i in stored]
        scratch.append(pltpu.SemaphoreType.DMA((count,)))
    spec = {"s": SMEM, "v": VMEM, "h": HBM, "f": HBM}
    return pl.pallas_call(
        whole,
        out_shape=[jax.ShapeDtypeStruct(shape, dtype) for shape, dtype in out],
        in_specs=[spec[kind] for kind in ins],
        out_specs=[spec[kind] for kind in outs],
        scratch_shapes=scratch,
        compiler_params=pltpu.CompilerParams(vmem_limit_bytes=vmem * 1024 * 1024),
        cost_estimate=pl.CostEstimate(flops=int(us * 1e9), bytes_accessed=0, transcendentals=0),
        name=name,
    )(*args)


def dot(left, right):
    return lax.dot_general(left, right, (((1,), (0,)), ((), ())), preferred_element_type=F32)


def dot_right(left, right):
    return lax.dot_general(left, right, (((1,), (1,)), ((), ())), preferred_element_type=F32)


def dot_left(left, right):
    return lax.dot_general(left, right, (((0,), (0,)), ((), ())), preferred_element_type=F32)


def from_core(x):
    return lax.ppermute(x, "kv", [(0, 1), (1, 0)])


def back_x(x, k):
    return lax.ppermute(x, "dp", [(i, (i + k) % SIDE) for i in range(SIDE)])


def back_y(x, k):
    pairs = [(z * SIDE + y, z * SIDE + (y + k) % SIDE) for z in range(SIDE) for y in range(SIDE)]
    return lax.ppermute(x, "ctx", pairs)


def back_z(x, k):
    pairs = [(z * SIDE + y, (z + k) % SIDE * SIDE + y) for z in range(SIDE) for y in range(SIDE)]
    return lax.ppermute(x, "ctx", pairs)


def group_round(x, i, back=False):
    pairs = [(n, 2 * ((n % 4 + i) % SIDE) + n // 4) for n in range(8)]
    if back:
        pairs = [(b, a) for a, b in pairs]
    return lax.ppermute(x, ("dp", "kv"), pairs)


def all_to_all(x):
    return lax.all_to_all(x, "ctx", split_axis=0, concat_axis=0, tiled=True)


def ring(send, x):
    got = {k: send(x, k) for k in (1, 3, 2)}
    return [x, got[1], got[2], got[3]]


def ring_back(send, parts):
    got = {k: send(parts[k], SIDE - k) for k in (1, 3, 2)}
    return [parts[0], got[1], got[2], got[3]]


def norm_rows(rows, gain):
    inverse = lax.rsqrt(jnp.mean(rows * rows, axis=-1, keepdims=True) + EPS)
    return rows * inverse * gain, inverse


def norm_back(rows, gain, incoming):
    inverse = lax.rsqrt(jnp.mean(rows * rows, axis=-1, keepdims=True) + EPS)
    normed = rows * inverse
    scaled = incoming * gain
    grad = inverse * (scaled - normed * jnp.mean(scaled * normed, axis=-1, keepdims=True))
    return grad, jnp.sum(incoming * normed, axis=0, keepdims=True)


def lane(shape):
    return lax.broadcasted_iota(jnp.int32, shape, len(shape) - 1)


def swap_halves(x):
    return jnp.where(lane(x.shape) % HEAD < HEAD // 2, pltpu.roll(x, 96, 1), pltpu.roll(x, 32, 1))


CTX, DP, KV, STARTS = 0, 1, 2, 3


def doc_start(place, p):
    start = jnp.zeros_like(p)
    for i in range(8):
        b = place[STARTS + i]
        start = jnp.where(p >= b, jnp.maximum(start, b), start)
    return start


def span_places(shape, dim, chip, kv):
    i = lax.broadcasted_iota(jnp.int32, shape, dim)
    half = jnp.where(i < TOK, kv, 1 - kv)
    return chip * SPAN + half * TOK + i % TOK


def rotary(place):
    spot = span_places((SPAN, 128), 0, place[CTX], place[KV])
    index = lane((SPAN, 128)) % HEAD
    freq = jnp.exp((index % (HEAD // 2)).astype(F32) * (-2.0 * math.log(10000.0) / HEAD))
    angle = (spot - doc_start(place, spot)).astype(F32) * freq
    return jnp.cos(angle), jnp.where(index < HEAD // 2, -1.0, 1.0) * jnp.sin(angle)


def one_hot(target, first, count):
    rows = lax.broadcasted_iota(jnp.int32, (count, target.shape[1]), 0) + first
    return jnp.where(rows == target, 1.0, 0.0).astype(BF16)


def owner_column(place, ctx, turn):
    return ((place[DP] - turn) & 3) * 16 + ctx


def qkv_target(place):
    row = lane((1, 640))
    ctx, inner = row // 40, row % 40
    value = inner >= 32
    turn = jnp.where(value, inner % 8, inner // 8)
    col = owner_column(place, ctx, turn)
    target = jnp.where(inner % 8 < 7, 7 * col + inner % 8, QCOL + col)
    return jnp.where(value, jnp.where(turn < 4, QCOL + HEAD + col, -1), target)


def shifted_ctx(place, z_shift, y_shift):
    z, y = place[CTX] // SIDE, place[CTX] % SIDE
    return ((z - z_shift) & 3) * SIDE + ((y - y_shift) & 3)


def out_order(place):
    row = lane((1, QCOL))
    kind = row % 8 - 1
    ctx = shifted_ctx(place, row // 128, row // 32 % 4)
    target = 7 * owner_column(place, ctx, row // 8 % 4) + kind
    return one_hot(jnp.where(kind >= 0, target, -1), 0, QCOL)


def normed_input(x0, x1, gain):
    rows = jnp.concatenate([x0()[...], x1()[...]], axis=0).astype(F32)
    return norm_rows(rows, gain)[0]


def kv_kernel(place, x0, x1, gain, w, kv_out, w_out):
    cos, sin = rotary(place)
    order = one_hot(qkv_target(place), QCOL, 128)
    rows = normed_input(x0, x1, gain[...]).astype(BF16)
    w_cols = dot(order, w[...]).astype(BF16)
    w_out[...] = w_cols
    u = dot_right(rows, w_cols)
    kv = jnp.where(lane((SPAN, 128)) < HEAD, u * cos + swap_halves(u) * sin, u).astype(BF16)
    for j in range(BLOCKS):
        kv_out[j] = kv


def query_kernel(place, x0, x1, gain, w, after, q_out, w_out):
    cos, sin = rotary(place)
    order = one_hot(qkv_target(place), 0, QCOL)
    rows = normed_input(x0, x1, gain[...]).astype(BF16)
    w_cols = dot(order, w()[...]).astype(BF16)
    w_out[...] = w_cols
    raw = dot_right(rows, w_cols)
    for j in range(4):
        u = raw[:, 128 * j : 128 * (j + 1)]
        q_out[:, 128 * j : 128 * (j + 1)] = ((u * cos + swap_halves(u) * sin) * QSCALE).astype(BF16)


def spread_heads(q, out):
    low = lane((SPAN, 128)) < HEAD
    for j in range(4):
        u = q[:, 128 * j : 128 * (j + 1)].astype(F32)
        out[2 * j] = jnp.where(low, u, 0.0).astype(BF16)
        if j < 3:
            out[2 * j + 1] = jnp.where(low, pltpu.roll(u, HEAD, 1), 0.0).astype(BF16)


def attn_project_kernel(place, w0, w1, w2, w3, o, own_out, other_out):
    rows = jnp.concatenate([w0()[...], w1()[...], w2()[...], w3()[...]], axis=0)
    attn = dot(dot(o()[...], out_order(place)).astype(BF16), rows)
    own_out[...] = attn[:TOK]
    other_out[...] = attn[TOK:].astype(BF16)


def block_ranges(place, n):
    first = place[CTX] * SPAN
    low_start, high_start = doc_start(place, first), doc_start(place, first + SPAN - 1)
    active = (n <= place[CTX]) & (n * SPAN + SPAN - 1 >= low_start)
    full = (n < place[CTX]) & (n * SPAN >= high_start)
    return active, full


def query_places(place, pos_ref, start_ref):
    pos = span_places((SPAN, SPAN), 0, place[CTX], place[KV])
    pos_ref[...] = pos
    start_ref[...] = doc_start(place, pos)


def allowed_keys(place, source, pos_ref, start_ref):
    keys = span_places((SPAN, SPAN), 1, source, place[KV])
    return (keys <= pos_ref[...]) & (keys >= start_ref[...])


def attend_kernel(place, q_cols, blocks, o_out, inv_out, q, acc, pos_ref, start_ref):
    query_places(place, pos_ref, start_ref)
    acc[...] = jnp.zeros_like(acc)
    spread_heads(q_cols(), q)
    low = lane((SPAN, 128)) < HEAD

    @pl.loop(0, BLOCKS)
    def _(n):
        active, full = block_ranges(place, n)

        def step(masked):
            kv = blocks[n]
            ones_v = jnp.where(low, jnp.ones_like(kv), kv)
            if masked:
                allowed = allowed_keys(place, n, pos_ref, start_ref)
            s = dot_right(q[...].reshape(GROUP * SPAN, 128), kv)
            p = jnp.exp2(jnp.tanh(s * (1.0 / CAP)) * EXP2)
            if masked:
                p = jnp.where(allowed[None], p.reshape(GROUP, SPAN, SPAN), 0.0).reshape(GROUP * SPAN, SPAN)
            acc[...] += dot(p.astype(BF16), ones_v).reshape(GROUP, SPAN, 128)

        pl.when(full)(lambda: step(False))
        pl.when(active & jnp.logical_not(full))(lambda: step(True))

    lanes = lane((SPAN, 128))
    inverse = jnp.ones((SPAN, 128), F32)
    for j in range(4):
        a = acc[2 * j]
        if j < 3:
            b = acc[2 * j + 1]
            total = jnp.where(low, a, pltpu.roll(b, HEAD, 1))
            value = jnp.where(low, pltpu.roll(a, HEAD, 1), b)
            inverse = jnp.where(lanes == 2 * j + 1, 1.0 / b, inverse)
        else:
            total = jnp.where(low, a, 1.0)
            value = jnp.where(low, pltpu.roll(a, HEAD, 1), 0.0)
        inverse = jnp.where(lanes == 2 * j, 1.0 / a, inverse)
        o_out[:, 128 * j : 128 * (j + 1)] = (value / total).astype(BF16)
    inv_out[...] = inverse


def attend_back_kernel(
    place, d0, d1, w0, w1, w2, w3, q_cols, o, inv, blocks,
    dq_out, grads, q, dq, do_ext, both_t, pos_ref, start_ref,
):
    query_places(place, pos_ref, start_ref)
    dq[...] = jnp.zeros_like(dq)
    rows = jnp.concatenate([d0()[...], d1()[...]], axis=0)
    w = jnp.concatenate([w0()[...], w1()[...], w2()[...], w3()[...]], axis=0)
    d_o = dot_right(dot_right(rows, w).astype(BF16), out_order(place))
    low = lane((SPAN, 128)) < HEAD
    lanes = lane((SPAN, 128))
    spread_heads(q_cols(), q)
    o, inv = o(), inv()
    for h in range(GROUP):
        j = h // 2
        cols = slice(128 * j, 128 * (j + 1))
        mine = low if h % 2 == 0 else jnp.logical_not(low)
        scale = inv[:, h : h + 1]
        up = d_o[:, cols] * scale
        delta = jnp.sum(jnp.where(mine, up * o[:, cols].astype(F32), 0.0), axis=1, keepdims=True)
        if h % 2 == 0:
            up = pltpu.roll(up, HEAD, 1)
        high = delta.astype(BF16).astype(F32)
        ext = jnp.where(lanes == 0, -high, jnp.where(lanes == 1, high - delta, jnp.where(low, 0.0, up)))
        do_ext[h] = ext.astype(BF16)
        both_t[:, SPAN * h : SPAN * (h + 1)] = jnp.transpose(jnp.where(low, q[h].astype(F32), up)).astype(BF16)
    blocks = blocks()

    @pl.loop(0, BLOCKS)
    def _(n):
        active, full = block_ranges(place, n)

        def step(masked):
            kv = blocks[n]
            ones_v = jnp.where(low, jnp.ones_like(kv), kv)
            if masked:
                allowed = allowed_keys(place, n, pos_ref, start_ref)
            s = dot_right(q[...].reshape(GROUP * SPAN, 128), kv)
            dp = dot_right(do_ext[...].reshape(GROUP * SPAN, 128), ones_v)
            t = jnp.tanh(s * (1.0 / CAP))
            p = jnp.exp2(t * EXP2)
            if masked:
                p = jnp.where(allowed[None], p.reshape(GROUP, SPAN, SPAN), 0.0).reshape(GROUP * SPAN, SPAN)
            ds = (p * dp * (1.0 - t * t)).astype(BF16)
            dq[...] += dot(ds, kv).reshape(GROUP, SPAN, 128)
            dk = dot(both_t[pl.ds(0, HEAD), :], ds)
            dv = dot(both_t[pl.ds(HEAD, HEAD), :], p.astype(BF16))
            grads[n] = jnp.concatenate([dk, dv], axis=0).astype(BF16)

        pl.when(full)(lambda: step(False))
        pl.when(active & jnp.logical_not(full))(lambda: step(True))

        @pl.when(jnp.logical_not(active))
        def _():
            grads[n] = jnp.zeros((128, SPAN), BF16)

    cos, sin = rotary(place)
    for j in range(4):
        u = dq[2 * j]
        if j < 3:
            u = jnp.where(low, u, pltpu.roll(dq[2 * j + 1], HEAD, 1))
        else:
            u = jnp.where(low, u, 0.0)
        u = u * QSCALE
        dq_out[:, 128 * j : 128 * (j + 1)] = (u * cos - swap_halves(u) * sin).astype(BF16)


def query_grad_kernel(place, dq, o, x0, x1, d0, d1, gain, w_grad, after, left):
    row = lane((1, WIDTH))
    kind = row % 14
    target = 7 * owner_column(place, row // 56, row // 14 % 4) + kind % 7
    after[...] = jnp.zeros_like(after)
    left[pl.ds(0, SPAN), :] = dot(dq()[...], one_hot(jnp.where(kind < 7, target, -1), 0, QCOL)).astype(BF16)
    left[pl.ds(SPAN, SPAN), :] = dot(o()[...], one_hot(jnp.where(kind < 7, -1, target), 0, QCOL)).astype(BF16)
    rows = normed_input(x0, x1, gain[...]).astype(BF16)
    right = jnp.concatenate([rows, d0()[...], d1()[...]], axis=0)
    w_grad[...] = dot_left(left[...], right).astype(BF16)


def project_back_kernel(
    place, dkv_parts, dq, w_q, w_kv, x0, x1, gain, g2, g3, g4, g5, q_grads, after,
    own_out, other_out, w_grad,
):
    cos, sin = rotary(place)
    row = lane((1, SPAN))
    kind = row % 16
    target = kind % 2 * HEAD + owner_column(place, row // 16, kind // 2)
    order = one_hot(jnp.where(kind < 8, target, -1), 0, 128)
    normed = normed_input(x0, x1, 1.0)
    d_a = dot(dq()[...], w_q()[...])
    dkv_parts = dkv_parts()
    dkv = dkv_parts[0].astype(F32)
    for j in range(1, BLOCKS):
        dkv += dkv_parts[j].astype(F32)
    u = jnp.transpose(dkv)
    dkv = jnp.where(lane((SPAN, 128)) < HEAD, u * cos - swap_halves(u) * sin, u).astype(BF16)
    d_a += dot(dkv, w_kv()[...])
    own_out[...] = d_a[:TOK]
    other_out[...] = d_a[TOK:].astype(BF16)
    g1 = jnp.sum(normed * d_a, axis=0, keepdims=True)
    gains = jnp.concatenate([g1, g2[...], g3[...], g4[...], g5[...], jnp.zeros((3, WIDTH), F32)], axis=0)
    part = dot_left(dot(dkv, order).astype(BF16), (normed * gain[...]).astype(BF16))
    part = part.reshape(BLOCKS, 16, WIDTH) + jnp.concatenate([jnp.zeros((8, WIDTH), F32), gains], axis=0)[None]
    w_grad[:, pl.ds(0, 16), :] = part.astype(BF16)
    q_grads = q_grads()
    for n in range(BLOCKS):
        w_grad[n, pl.ds(16, 56), :] = q_grads[pl.ds(56 * n, 56), :]


def attn_norm_kernel(x, own, other, gain_b, gain_c, attn_out, r_out, m_out):
    attn = own[...] + other[...].astype(F32)
    attn_out[...] = attn
    resid = x[...].astype(F32) + norm_rows(attn, gain_b[...])[0]
    r_out[...] = resid
    m_out[...] = norm_rows(resid, gain_c[...])[0].astype(BF16)


def sum_parts(own, b, c, d):
    return (own[...] + b[...].astype(F32)) + (c[...].astype(F32) + d[...].astype(F32))


def ffn_norm_kernel(own, b, c, d, resid, cotangent, gain, out, d_out, gain_out):
    fo = sum_parts(own, b, c, d)
    out[...] = (resid[...] + norm_rows(fo, gain[...])[0]).astype(BF16)
    grad, gain_grad = norm_back(fo, gain[...], cotangent[...].astype(F32))
    d_out[...] = grad.astype(BF16)
    gain_out[...] = gain_grad


def ffn_back_norm_kernel(own, b, c, d, resid, attn, cotangent, gain_c, gain_b, r_out, d_out, gain_c_out, gain_b_out):
    d_m = sum_parts(own, b, c, d)
    grad, gain_grad = norm_back(resid[...], gain_c[...], d_m)
    gain_c_out[...] = gain_grad
    d_resid = cotangent[...].astype(F32) + grad
    r_out[...] = d_resid
    grad, gain_grad = norm_back(attn[...], gain_b[...], d_resid)
    gain_b_out[...] = gain_grad
    d_out[...] = grad.astype(BF16)


def input_norm_kernel(own, other, x, d_resid, gain, out):
    d_a = own[...] + other[...].astype(F32)
    out[...] = d_resid[...] + norm_back(x[...].astype(F32), gain[...], d_a)[0]


def gelu_parts(u):
    t = jnp.tanh(GELU_C * (u + 0.044715 * u * u * u))
    active = 0.5 * u * (1.0 + t)
    slope = 0.5 * (1.0 + t) + 0.5 * u * (1.0 - t * t) * GELU_C * (1.0 + 3.0 * 0.044715 * u * u)
    return active, slope


def weight_runs(which):
    runs, at = [], which * HALF_UNITS
    while at < (which + 1) * HALF_UNITS:
        count = min(TOK - at % TOK, (which + 1) * HALF_UNITS - at)
        runs.append((at // TOK, at % TOK, at - which * HALF_UNITS, count))
        at += count
    return runs


def arrange_kernel(place, pieces, gate, up, down, sems):
    copies = []
    for which, dest in enumerate((gate, up, down)):
        for core in range(2):
            source = place[KV] if core == 0 else 1 - place[KV]
            for quarter, row, unit, count in weight_runs(which):
                copies.append(
                    pltpu.make_async_copy(
                        pieces.at[2 * quarter + source, :, pl.ds(row, count), :],
                        dest.at[pl.ds(core * SIDE, SIDE), pl.ds(unit, count), :],
                        sems.at[len(copies)],
                    )
                )
    for c in copies:
        c.start()
    for c in copies:
        c.wait()


def dequantise_kernel(place, gate, up, down, gate_scale, up_scale, down_scale, more, out, codes, sems):
    out[pl.ds(0, TOK), :] = jnp.zeros((TOK, WIDTH), BF16)
    out[pl.ds(TOK, 32), :] = more[...]

    def fill(core, quarter):
        runs = []
        for which in range(3):
            for part, row, unit, count in weight_runs(which):
                first = core * HALF_UNITS + unit
                count = min(count, UNITS - first)
                if part == quarter:
                    runs.append((which, row, first, count))
        copies = [
            pltpu.make_async_copy(
                (gate, up, down)[which].at[pl.ds(first, count), :], codes.at[pl.ds(row, count), :], sems.at[n]
            )
            for n, (which, row, first, count) in enumerate(runs)
        ]
        for c in copies:
            c.start()
        for c in copies:
            c.wait()
        for which, row, first, count in runs:
            c = codes[pl.ds(row, count), :]
            if which == 0:
                weight = c.astype(F32) * gate_scale[pl.ds(first, count), :]
            elif which == 1:
                weight = ((c & -16) + 8).astype(F32) * up_scale[pl.ds(first, count), :]
            else:
                weight = ((c & -64) + 32).astype(F32) * down_scale[...]
            out[pl.ds(row, count), :] = weight.astype(BF16)

    for core in range(2):
        for quarter in range(SIDE):
            pl.when((place[KV] == core) & (place[DP] == quarter))(lambda c=core, q=quarter: fill(c, q))


def ffn_kernel(m0, m1, m2, m3, gate_w, up_w, down_w, f0, f1, f2, f3, gate_out, up_out, m, acc):
    for j, part in enumerate((m0, m1, m2, m3)):
        m[pl.ds(TOK * j, TOK), :] = part[...]
    for n in range(HID // 256):
        units = pl.ds(256 * n, 256)
        gate = dot_right(m[...], gate_w[units, :])
        up = dot_right(m[...], up_w[units, :])
        gate_out[:, 256 * n : 256 * (n + 1)] = gate.astype(BF16)
        up_out[:, 256 * n : 256 * (n + 1)] = up.astype(BF16)
        hidden = (gelu_parts(gate)[0] * up).astype(BF16)
        part = dot(hidden, down_w[units, :])
        if n == 0:
            acc[...] = part
        else:
            acc[...] += part
    f0[...] = acc[pl.ds(0, TOK), :]
    for j, out in enumerate((f1, f2, f3)):
        out[...] = acc[pl.ds(TOK * (j + 1), TOK), :].astype(BF16)


def ffn_back_kernel(
    e0, e1, e2, e3, gate_in, up_in, gate_w, up_w, down_w, f0, f1, f2, f3, hidden_out, gate_out, up_out, e, acc
):
    for j, part in enumerate((e0, e1, e2, e3)):
        e[pl.ds(TOK * j, TOK), :] = part[...]
    for n in range(HID // 256):
        units = pl.ds(256 * n, 256)
        cols = slice(256 * n, 256 * (n + 1))
        d_hidden = dot_right(e[...], down_w[units, :])
        active, slope = gelu_parts(gate_in[:, cols].astype(F32))
        up = up_in[:, cols].astype(F32)
        hidden_out[:, cols] = (active * up).astype(BF16)
        d_gate = (d_hidden * up * slope).astype(BF16)
        d_up = (d_hidden * active).astype(BF16)
        gate_out[:, cols] = d_gate
        up_out[:, cols] = d_up
        part = dot(d_gate, gate_w[units, :]) + dot(d_up, up_w[units, :])
        if n == 0:
            acc[...] = part
        else:
            acc[...] += part
    f0[...] = acc[pl.ds(0, TOK), :]
    for j, out in enumerate((f1, f2, f3)):
        out[...] = acc[pl.ds(TOK * (j + 1), TOK), :].astype(BF16)


def ffn_weight_kernel(
    place, m0, m1, m2, m3, e0, e1, e2, e3, hidden, d_gate, d_up, down_w, down_scale, out, scale_out, m, e
):
    for j, (a, b) in enumerate(zip((m0, m1, m2, m3), (e0, e1, e2, e3))):
        m[pl.ds(TOK * j, TOK), :] = a[...]
        e[pl.ds(TOK * j, TOK), :] = b[...]
    empty = SIDE * TOK - 3 * HALF_UNITS
    out[pl.ds(2 * SIDE - 2, 2), :, pl.ds(TOK - empty, empty), :] = jnp.zeros((2, SIDE, empty, WIDTH), BF16)
    per_unit = 1.0 / down_scale[...]
    scale_grad = jnp.zeros((1, WIDTH), F32)
    for which, (left, right) in enumerate(((d_gate, m), (d_up, m), (hidden, e))):
        runs = weight_runs(which)
        for n in range(HID // 256):
            first = 256 * n
            part = dot_left(left[:, first : first + 256], right[...])
            if which == 2:
                level = down_w[pl.ds(first, 256), :].astype(F32) * per_unit
                level = jnp.floor(level * (1.0 / 64.0)) * 64.0 + 32.0
                scale_grad += jnp.sum(part * level, axis=0, keepdims=True)
            part = part.astype(BF16)
            for piece in range(2 * SIDE):
                core = place[KV] if piece < SIDE else 1 - place[KV]
                for quarter, row, unit, count in runs:
                    low = max(piece * HALF_UNITS + unit, first)
                    high = min(piece * HALF_UNITS + unit + count, first + 256)
                    if low < high:
                        at = row + low - piece * HALF_UNITS - unit
                        out[2 * quarter + core, piece % SIDE, pl.ds(at, high - low), :] = part[low - first : high - first]
    scale_out[...] = scale_grad


def finish_kernel(parts, gate, up, gate_scale, up_scale, down_scale, g_gate, g_up, g_down, s_gate, s_up, sums):
    sums[...] = jnp.zeros_like(sums)
    for core in range(2):
        for which in range(3):
            for quarter, row, unit, count in weight_runs(which):
                first = core * HALF_UNITS + unit
                count = min(count, UNITS - first)
                rows = pl.ds(first, count)
                total = parts[2 * quarter + core, pl.ds(row, count), :].astype(F32)
                if which == 0:
                    g_gate[rows, :] = total * gate_scale[rows, :]
                    part = jnp.sum(total * gate[rows, :].astype(F32), axis=1, keepdims=True)
                    sums[0, rows, :] = jnp.broadcast_to(part, (count, 128))
                elif which == 1:
                    g_up[rows, :] = total * up_scale[rows, :]
                    part = jnp.sum(total * ((up[rows, :] & -16) + 8).astype(F32), axis=1, keepdims=True)
                    sums[1, rows, :] = jnp.broadcast_to(part, (count, 128))
                else:
                    g_down[rows, :] = total * down_scale[...]
    s_gate[...] = jnp.transpose(sums[0])[:1, :UNITS]
    s_up[...] = jnp.transpose(sums[1])[:1, :UNITS]


def shards(
    layer_input, cotangent, doc_bounds, w_query, key_weight, value_weight, w_out,
    gain_attn_in, gain_attn_out, gain_ffn_in, gain_ffn_out,
    code_gate, code_up, code_down, scale_gate, scale_up, scale_down,
):
    ctx, kv, dp = lax.axis_index("ctx"), lax.axis_index("kv"), lax.axis_index("dp")
    place = jnp.concatenate([jnp.stack([ctx, dp, kv]).astype(jnp.int32), doc_bounds[0]])
    x = layer_input.reshape(TOK, WIDTH)
    cot = cotangent.reshape(TOK, WIDTH)
    gain_1, gain_2, gain_3, gain_4 = (
        g.reshape(1, WIDTH) for g in (gain_attn_in, gain_attn_out, gain_ffn_in, gain_ffn_out)
    )
    gate_col, up_col, down_row = scale_gate[:, None], scale_up[:, None], scale_down[None, :]
    rows_f32, rows_bf16, row_f32 = ((TOK, WIDTH), F32), ((TOK, WIDTH), BF16), ((1, WIDTH), F32)

    shard = jnp.concatenate([w_query.T, key_weight.T, value_weight.T, w_out.T], axis=0)
    rounds = [group_round(shard, i) for i in range(4)]
    x_other = from_core(x)

    qkv_rows = jnp.concatenate(
        [r[:8] for r in rounds] + [r[8:9] for r in rounds] + [jnp.zeros((4, WIDTH), BF16)], axis=0
    )
    out_rows = jnp.concatenate([r[8:] for r in rounds], axis=0)
    qkv_rows, out_rows, x_other = lax.optimization_barrier((qkv_rows, out_rows, x_other))

    (quarter,) = kernel_call(
        dequantise_kernel,
        "shhhvvvv",
        "v",
        [((TOK + 32, WIDTH), BF16)],
        "dequantise",
        (place, code_gate.T, code_up.T, code_down, gate_col, up_col, down_row, out_rows),
        [pltpu.VMEM((TOK, WIDTH), jnp.int32), pltpu.SemaphoreType.DMA((2,))],
        vmem=58,
    )
    quarters = ring(back_y, quarter)
    quarters = ring(back_y, quarter)

    def gathered(rows):
        copies = jnp.broadcast_to(rows[None], (BLOCKS,) + rows.shape)
        return all_to_all(copies).reshape(-1, WIDTH)

    qkv_rows = gathered(qkv_rows)

    keys, w_kv = kernel_call(
        kv_kernel,
        "sffvv",
        "ff",
        [((BLOCKS, SPAN, 128), BF16), ((128, WIDTH), BF16)],
        "keys",
        (place, x, x_other, gain_1, qkv_rows),
        us=4,
        vmem=20,
    )
    quarters, after = lax.optimization_barrier((quarters, w_kv))
    ffn_w = lax.all_gather(jnp.stack([p[:TOK] for p in quarters]), ("dp", "kv"))
    out_rows = ring(back_z, jnp.concatenate([p[TOK:] for p in quarters], axis=0))
    keys = all_to_all(keys)
    q, w_q = kernel_call(
        query_kernel,
        "sffvfh",
        "ff",
        [((SPAN, QCOL), BF16), ((QCOL, WIDTH), BF16)],
        "queries",
        (place, x, x_other, gain_1, qkv_rows, after),
        us=4,
        vmem=58,
    )
    o, inv = kernel_call(
        attend_kernel,
        "sfv",
        "ff",
        [((SPAN, QCOL), BF16), ((SPAN, 128), F32)],
        "attend",
        (place, q, keys),
        [
            pltpu.VMEM((GROUP, SPAN, 128), BF16),
            pltpu.VMEM((GROUP, SPAN, 128), F32),
            pltpu.VMEM((SPAN, SPAN), jnp.int32),
            pltpu.VMEM((SPAN, SPAN), jnp.int32),
        ],
        us=16,
        vmem=24,
    )
    attn_own, attn_other = kernel_call(
        attn_project_kernel,
        "sfffff",
        "vv",
        [rows_f32, rows_bf16],
        "attn_project",
        (place, *out_rows, o),
        vmem=16,
    )
    attn_other = from_core(attn_other)
    attn, resid, m_own = kernel_call(
        attn_norm_kernel,
        "vvvvv",
        "vvv",
        [rows_f32, rows_f32, rows_bf16],
        "attn_norm",
        (x, attn_own, attn_other, gain_2, gain_3),
    )

    m_parts = ring(back_z, m_own)
    m_parts[1], ffn_w = lax.optimization_barrier((m_parts[1], ffn_w))
    wide = ((SIDE * TOK, HID), BF16)
    unit_rows = ((2 * SIDE, HALF_UNITS, WIDTH), BF16)
    ffn_w = kernel_call(
        arrange_kernel,
        "sh",
        "vvv",
        [unit_rows] * 3,
        "arrange",
        (place, ffn_w),
        [pltpu.SemaphoreType.DMA((12,))],
        us=4,
    )
    gate_w, up_w, down_w = (w.reshape(HID, WIDTH) for w in ffn_w)
    ffn_scratch = [pltpu.VMEM((SIDE * TOK, WIDTH), BF16), pltpu.VMEM((SIDE * TOK, WIDTH), F32)]
    *fo_parts, gate, up = kernel_call(
        ffn_kernel,
        "vvvvvvv",
        "vvvvvv",
        [rows_f32] + [rows_bf16] * 3 + [wide, wide],
        "ffn",
        (*m_parts, gate_w, up_w, down_w),
        ffn_scratch,
        us=6,
        vmem=16,
    )
    fo_parts = ring_back(back_z, fo_parts)
    block_out, d_fo, g_gain_4 = kernel_call(
        ffn_norm_kernel, "vvvvvvv", "vvv", [rows_bf16, rows_bf16, row_f32], "ffn_norm", (*fo_parts, resid, cot, gain_4)
    )

    d_parts = ring(back_z, d_fo)
    *dm_parts, hidden, d_gate, d_up = kernel_call(
        ffn_back_kernel,
        "vvvvvvvvv",
        "vvvvvvv",
        [rows_f32] + [rows_bf16] * 3 + [wide] * 3,
        "ffn_back",
        (*d_parts, gate, up, gate_w, up_w, down_w),
        ffn_scratch,
        us=10,
        vmem=20,
    )
    dm_parts = ring_back(back_z, dm_parts)
    weight_grads, g_down = kernel_call(
        ffn_weight_kernel,
        "s" + "v" * 13,
        "fv",
        [((2 * SIDE, SIDE, TOK, WIDTH), BF16), row_f32],
        "ffn_weight",
        (place, *m_parts, *d_parts, hidden, d_gate, d_up, down_w, down_row),
        [
            pltpu.VMEM((SIDE * TOK, WIDTH), BF16),
            pltpu.VMEM((SIDE * TOK, WIDTH), BF16),
        ],
        us=8,
        vmem=20,
    )
    dm_parts, weight_grads = lax.optimization_barrier((dm_parts, weight_grads))
    weight_grads = lax.psum_scatter(weight_grads, ("dp", "kv"), scatter_dimension=0)
    d_resid, d_attn, g_gain_3, g_gain_2 = kernel_call(
        ffn_back_norm_kernel,
        "vvvvvvvvv",
        "vvvv",
        [rows_f32, rows_bf16, row_f32, row_f32],
        "ffn_back_norm",
        (*dm_parts, resid, attn, cot, gain_3, gain_2),
    )
    d_attn_other = from_core(d_attn)

    dq, key_grads = kernel_call(
        attend_back_kernel,
        "sffffffffff",
        "ff",
        [((SPAN, QCOL), BF16), ((BLOCKS, 128, SPAN), BF16)],
        "attend_back",
        (place, d_attn, d_attn_other, *out_rows, q, o, inv, keys),
        [
            pltpu.VMEM((GROUP, SPAN, 128), BF16),
            pltpu.VMEM((GROUP, SPAN, 128), F32),
            pltpu.VMEM((GROUP, SPAN, 128), BF16),
            pltpu.VMEM((128, GROUP * SPAN), BF16),
            pltpu.VMEM((SPAN, SPAN), jnp.int32),
            pltpu.VMEM((SPAN, SPAN), jnp.int32),
        ],
        us=26,
        vmem=58,
    )
    key_grads = all_to_all(key_grads)
    q_grads, after = kernel_call(
        query_grad_kernel,
        "sffffffv",
        "fv",
        [((WIDTH, WIDTH), BF16), ((8, 128), F32)],
        "query_grad",
        (place, dq, o, x, x_other, d_attn, d_attn_other, gain_1),
        [pltpu.VMEM((2 * SPAN, WIDTH), BF16)],
        us=5,
        vmem=58,
    )

    def total(parts):
        a, b, c, d = (p.astype(F32) for p in parts)
        return (a + b) + (c + d)

    da_own, da_other, w_grads = kernel_call(
        project_back_kernel,
        "sffffffvvvvvfv",
        "vvv",
        [rows_f32, rows_bf16, ((BLOCKS, 72, WIDTH), BF16)],
        "project_back",
        (place, key_grads, dq, w_q, w_kv, x, x_other, gain_1, g_gain_2, g_gain_3, g_gain_4, g_down, q_grads, after),
        us=4,
        vmem=58,
    )
    weight_grads, da_other = lax.optimization_barrier((weight_grads, da_other))
    weight_grads = weight_grads.reshape(SIDE, TOK, WIDTH)
    eighth = total(ring_back(back_y, [weight_grads[k] for k in range(SIDE)])).astype(BF16)
    eighths = lax.all_gather(eighth, ("dp", "kv"))

    (grad_input,) = kernel_call(
        input_norm_kernel, "vvvvv", "v", [rows_f32], "input_norm", (da_own, from_core(da_other), x, d_resid, gain_1)
    )

    w_grads = all_to_all(w_grads)
    grad_code_gate, grad_code_up, grad_code_down, grad_scale_gate, grad_scale_up = kernel_call(
        finish_kernel,
        "vvvvvv",
        "vvvvv",
        [((UNITS, WIDTH), F32)] * 3 + [((1, UNITS), F32)] * 2,
        "finish",
        (eighths, code_gate.T, code_up.T, gate_col, up_col, down_row),
        [pltpu.VMEM((2, 384, 128), F32)],
        us=3,
    )
    grads = (grad_code_gate, grad_code_up, grad_code_down, grad_scale_gate[0], grad_scale_up[0])
    w_grads, grad_input = lax.optimization_barrier((w_grads, grad_input))


    w_grads = jnp.sum(w_grads.astype(F32), axis=0)
    kv_grads, q_grads = w_grads[:16], w_grads[16:]
    gains = kv_grads[8:] + from_core(kv_grads[8:])
    sums = [jnp.concatenate([q_grads[14 * i : 14 * i + 14], kv_grads[2 * i : 2 * i + 2], gains], axis=0) for i in range(4)]
    sums = [group_round(part.astype(BF16), i, back=True).astype(F32) for i, part in enumerate(sums)]
    grad_w = (sums[0] + sums[1]) + (sums[2] + sums[3])
    gains = grad_w[16:]

    return (
        block_out.reshape(layer_input.shape),
        grad_input.reshape(layer_input.shape),
        grad_w[:7].T,
        grad_w[14:15].T,
        grad_w[15:16].T,
        grad_w[7:14].T,
        gains[0],
        gains[1],
        gains[2],
        gains[3],
        grads[0].T,
        grads[1].T,
        *grads[2:],
        gains[4],
    )


def solution(mesh):
    tokens = P("dp", "ctx", "kv", None, None)
    columns = P(None, ("dp", "kv", "ctx"))
    hidden = (P(None, "ctx"), P(None, "ctx"), P("ctx", None), P("ctx"), P("ctx"), P())
    return jax.shard_map(
        shards,
        mesh=mesh,
        in_specs=(tokens, tokens, P("dp", None)) + (columns,) * 4 + (P(),) * 4 + hidden,
        out_specs=(tokens, tokens) + (columns,) * 4 + (P(),) * 4 + hidden,
        check_vma=False,
    )
```

```python
import math

import jax
import jax.numpy as jnp
from jax import lax
from jax.experimental import pallas as pl
from jax.experimental.pallas import tpu as pltpu
from jax.sharding import PartitionSpec as P

EPS = 1e-06
CAP = 50.0
QSCALE = 0.125
GELU_C = math.sqrt(2.0 / math.pi)
EXP2 = CAP * math.log2(math.e)

TOK = 128
SPAN = 256
WIDTH = 896
HEAD = 64
GROUP = 7
QCOL = 512
SIDE = 4
UNITS = 304
UPAD = 320
HALF_UNITS = 160
HID = 1280
HALF_ROWS = 512
BLOCKS = 16
F32 = jnp.float32
BF16 = jnp.bfloat16
VMEM = pl.BlockSpec(memory_space=pltpu.VMEM)
SMEM = pl.BlockSpec(memory_space=pltpu.SMEM)
HBM = pl.BlockSpec(memory_space=pltpu.HBM)


class Fetched:
    def __init__(self, copy, buffer):
        self.copy, self.buffer = copy, buffer

    def __call__(self):
        if self.copy is not None:
            self.copy.wait()
            self.copy = None
        return self.buffer


def kernel_call(body, ins, outs, out, name, args, scratch=(), us=2.0, vmem=16):
    fetched = [i for i, kind in enumerate(ins) if kind == "f"]
    stored = [i for i, kind in enumerate(outs) if kind == "f"]
    count = len(fetched) + len(stored)

    def whole(*refs):
        if not count:
            return body(*refs)
        sems, buffers = refs[-1], refs[len(refs) - 1 - count : -1]
        refs = list(refs[: len(refs) - 1 - count])
        copies = [pltpu.make_async_copy(refs[i], buffers[n], sems.at[n]) for n, i in enumerate(fetched)]
        for c in copies:
            c.start()
        for n, i in enumerate(fetched):
            refs[i] = Fetched(copies[n], buffers[n])
        back = []
        for n, i in enumerate(stored, len(fetched)):
            back.append(pltpu.make_async_copy(buffers[n], refs[len(ins) + i], sems.at[n]))
            refs[len(ins) + i] = buffers[n]
        body(*refs)
        for c in back:
            c.start()
        for c in back:
            c.wait()

    scratch = list(scratch)
    if count:
        scratch += [pltpu.VMEM(args[i].shape, args[i].dtype) for i in fetched]
        scratch += [pltpu.VMEM(*out[i]) for i in stored]
        scratch.append(pltpu.SemaphoreType.DMA((count,)))
    spec = {"s": SMEM, "v": VMEM, "h": HBM, "f": HBM}
    return pl.pallas_call(
        whole,
        out_shape=[jax.ShapeDtypeStruct(shape, dtype) for shape, dtype in out],
        in_specs=[spec[kind] for kind in ins],
        out_specs=[spec[kind] for kind in outs],
        scratch_shapes=scratch,
        compiler_params=pltpu.CompilerParams(vmem_limit_bytes=vmem * 1024 * 1024),
        cost_estimate=pl.CostEstimate(flops=int(us * 1e9), bytes_accessed=0, transcendentals=0),
        name=name,
    )(*args)


def dot(left, right):
    return lax.dot_general(left, right, (((1,), (0,)), ((), ())), preferred_element_type=F32)


def dot_right(left, right):
    return lax.dot_general(left, right, (((1,), (1,)), ((), ())), preferred_element_type=F32)


def dot_left(left, right):
    return lax.dot_general(left, right, (((0,), (0,)), ((), ())), preferred_element_type=F32)


def from_core(x):
    return lax.ppermute(x, "kv", [(0, 1), (1, 0)])


def back_x(x, k):
    return lax.ppermute(x, "dp", [(i, (i + k) % SIDE) for i in range(SIDE)])


def back_y(x, k):
    pairs = [(z * SIDE + y, z * SIDE + (y + k) % SIDE) for z in range(SIDE) for y in range(SIDE)]
    return lax.ppermute(x, "ctx", pairs)


def back_z(x, k):
    pairs = [(z * SIDE + y, (z + k) % SIDE * SIDE + y) for z in range(SIDE) for y in range(SIDE)]
    return lax.ppermute(x, "ctx", pairs)


def group_round(x, i, back=False):
    pairs = [(n, 2 * ((n % 4 + i) % SIDE) + n // 4) for n in range(8)]
    if back:
        pairs = [(b, a) for a, b in pairs]
    return lax.ppermute(x, ("dp", "kv"), pairs)


def all_to_all(x):
    return lax.all_to_all(x, "ctx", split_axis=0, concat_axis=0, tiled=True)


def ring(send, x):
    got = {k: send(x, k) for k in (1, 3, 2)}
    return [x, got[1], got[2], got[3]]


def ring_back(send, parts):
    got = {k: send(parts[k], SIDE - k) for k in (1, 3, 2)}
    return [parts[0], got[1], got[2], got[3]]


def norm_rows(rows, gain):
    inverse = lax.rsqrt(jnp.mean(rows * rows, axis=-1, keepdims=True) + EPS)
    return rows * inverse * gain, inverse


def norm_back(rows, gain, incoming):
    inverse = lax.rsqrt(jnp.mean(rows * rows, axis=-1, keepdims=True) + EPS)
    normed = rows * inverse
    scaled = incoming * gain
    grad = inverse * (scaled - normed * jnp.mean(scaled * normed, axis=-1, keepdims=True))
    return grad, jnp.sum(incoming * normed, axis=0, keepdims=True)


def lane(shape):
    return lax.broadcasted_iota(jnp.int32, shape, len(shape) - 1)


def swap_halves(x):
    return jnp.where(lane(x.shape) % HEAD < HEAD // 2, pltpu.roll(x, 96, 1), pltpu.roll(x, 32, 1))


CTX, DP, KV, STARTS = 0, 1, 2, 3


def doc_start(place, p):
    start = jnp.zeros_like(p)
    for i in range(8):
        b = place[STARTS + i]
        start = jnp.where(p >= b, jnp.maximum(start, b), start)
    return start


def span_places(shape, dim, chip, kv):
    i = lax.broadcasted_iota(jnp.int32, shape, dim)
    half = jnp.where(i < TOK, kv, 1 - kv)
    return chip * SPAN + half * TOK + i % TOK


def rotary(place):
    spot = span_places((SPAN, 128), 0, place[CTX], place[KV])
    index = lane((SPAN, 128)) % HEAD
    freq = jnp.exp((index % (HEAD // 2)).astype(F32) * (-2.0 * math.log(10000.0) / HEAD))
    angle = (spot - doc_start(place, spot)).astype(F32) * freq
    return jnp.cos(angle), jnp.where(index < HEAD // 2, -1.0, 1.0) * jnp.sin(angle)


def one_hot(target, first, count):
    rows = lax.broadcasted_iota(jnp.int32, (count, target.shape[1]), 0) + first
    return jnp.where(rows == target, 1.0, 0.0).astype(BF16)


def owner_column(place, ctx, turn):
    return ((place[DP] - turn) & 3) * 16 + ctx


def qkv_target(place):
    row = lane((1, 640))
    ctx, inner = row // 40, row % 40
    value = inner >= 32
    turn = jnp.where(value, inner % 8, inner // 8)
    col = owner_column(place, ctx, turn)
    target = jnp.where(inner % 8 < 7, 7 * col + inner % 8, QCOL + col)
    return jnp.where(value, jnp.where(turn < 4, QCOL + HEAD + col, -1), target)


def shifted_ctx(place, z_shift, y_shift):
    z, y = place[CTX] // SIDE, place[CTX] % SIDE
    return ((z - z_shift) & 3) * SIDE + ((y - y_shift) & 3)


def out_order(place):
    row = lane((1, QCOL))
    kind = row % 8 - 1
    ctx = shifted_ctx(place, row // 128, row // 32 % 4)
    target = 7 * owner_column(place, ctx, row // 8 % 4) + kind
    return one_hot(jnp.where(kind >= 0, target, -1), 0, QCOL)


def normed_input(x0, x1, gain):
    rows = jnp.concatenate([x0()[...], x1()[...]], axis=0).astype(F32)
    return norm_rows(rows, gain)[0]


def kv_kernel(place, x0, x1, gain, w, kv_out, w_out):
    cos, sin = rotary(place)
    order = one_hot(qkv_target(place), QCOL, 128)
    rows = normed_input(x0, x1, gain[...]).astype(BF16)
    w_cols = dot(order, w[...]).astype(BF16)
    w_out[...] = w_cols
    u = dot_right(rows, w_cols)
    kv = jnp.where(lane((SPAN, 128)) < HEAD, u * cos + swap_halves(u) * sin, u).astype(BF16)
    for j in range(BLOCKS):
        kv_out[j] = kv


def query_kernel(place, x0, x1, gain, w, after, q_out, w_out):
    cos, sin = rotary(place)
    order = one_hot(qkv_target(place), 0, QCOL)
    rows = normed_input(x0, x1, gain[...]).astype(BF16)
    w_cols = dot(order, w()[...]).astype(BF16)
    w_out[...] = w_cols
    raw = dot_right(rows, w_cols)
    for j in range(4):
        u = raw[:, 128 * j : 128 * (j + 1)]
        q_out[:, 128 * j : 128 * (j + 1)] = ((u * cos + swap_halves(u) * sin) * QSCALE).astype(BF16)


def spread_heads(q, out):
    low = lane((SPAN, 128)) < HEAD
    for j in range(4):
        u = q[:, 128 * j : 128 * (j + 1)].astype(F32)
        out[2 * j] = jnp.where(low, u, 0.0).astype(BF16)
        if j < 3:
            out[2 * j + 1] = jnp.where(low, pltpu.roll(u, HEAD, 1), 0.0).astype(BF16)


def attn_project_kernel(place, w0, w1, w2, w3, o, own_out, other_out):
    rows = jnp.concatenate([w0()[...], w1()[...], w2()[...], w3()[...]], axis=0)
    attn = dot(dot(o()[...], out_order(place)).astype(BF16), rows)
    own_out[...] = attn[:TOK]
    other_out[...] = attn[TOK:].astype(BF16)


def block_ranges(place, n):
    first = place[CTX] * SPAN
    low_start, high_start = doc_start(place, first), doc_start(place, first + SPAN - 1)
    active = (n <= place[CTX]) & (n * SPAN + SPAN - 1 >= low_start)
    full = (n < place[CTX]) & (n * SPAN >= high_start)
    return active, full


def query_places(place, pos_ref, start_ref):
    pos = span_places((SPAN, SPAN), 0, place[CTX], place[KV])
    pos_ref[...] = pos
    start_ref[...] = doc_start(place, pos)


def allowed_keys(place, source, pos_ref, start_ref):
    keys = span_places((SPAN, SPAN), 1, source, place[KV])
    return (keys <= pos_ref[...]) & (keys >= start_ref[...])


def attend_kernel(place, q_cols, blocks, o_out, inv_out, q, acc, pos_ref, start_ref):
    query_places(place, pos_ref, start_ref)
    acc[...] = jnp.zeros_like(acc)
    spread_heads(q_cols(), q)
    low = lane((SPAN, 128)) < HEAD

    @pl.loop(0, BLOCKS)
    def _(n):
        active, full = block_ranges(place, n)

        def step(masked):
            kv = blocks[n]
            ones_v = jnp.where(low, jnp.ones_like(kv), kv)
            if masked:
                allowed = allowed_keys(place, n, pos_ref, start_ref)
            s = dot_right(q[...].reshape(GROUP * SPAN, 128), kv)
            p = jnp.exp2(jnp.tanh(s * (1.0 / CAP)) * EXP2)
            if masked:
                p = jnp.where(allowed[None], p.reshape(GROUP, SPAN, SPAN), 0.0).reshape(GROUP * SPAN, SPAN)
            acc[...] += dot(p.astype(BF16), ones_v).reshape(GROUP, SPAN, 128)

        pl.when(full)(lambda: step(False))
        pl.when(active & jnp.logical_not(full))(lambda: step(True))

    lanes = lane((SPAN, 128))
    inverse = jnp.ones((SPAN, 128), F32)
    for j in range(4):
        a = acc[2 * j]
        if j < 3:
            b = acc[2 * j + 1]
            total = jnp.where(low, a, pltpu.roll(b, HEAD, 1))
            value = jnp.where(low, pltpu.roll(a, HEAD, 1), b)
            inverse = jnp.where(lanes == 2 * j + 1, 1.0 / b, inverse)
        else:
            total = jnp.where(low, a, 1.0)
            value = jnp.where(low, pltpu.roll(a, HEAD, 1), 0.0)
        inverse = jnp.where(lanes == 2 * j, 1.0 / a, inverse)
        o_out[:, 128 * j : 128 * (j + 1)] = (value / total).astype(BF16)
    inv_out[...] = inverse


def attend_back_kernel(
    place, d0, d1, w0, w1, w2, w3, q_cols, o, inv, blocks,
    dq_out, grads, q, dq, do_ext, both_t, pos_ref, start_ref,
):
    query_places(place, pos_ref, start_ref)
    dq[...] = jnp.zeros_like(dq)
    rows = jnp.concatenate([d0()[...], d1()[...]], axis=0)
    w = jnp.concatenate([w0()[...], w1()[...], w2()[...], w3()[...]], axis=0)
    d_o = dot_right(dot_right(rows, w).astype(BF16), out_order(place))
    low = lane((SPAN, 128)) < HEAD
    lanes = lane((SPAN, 128))
    spread_heads(q_cols(), q)
    o, inv = o(), inv()
    for h in range(GROUP):
        j = h // 2
        cols = slice(128 * j, 128 * (j + 1))
        mine = low if h % 2 == 0 else jnp.logical_not(low)
        scale = inv[:, h : h + 1]
        up = d_o[:, cols] * scale
        delta = jnp.sum(jnp.where(mine, up * o[:, cols].astype(F32), 0.0), axis=1, keepdims=True)
        if h % 2 == 0:
            up = pltpu.roll(up, HEAD, 1)
        high = delta.astype(BF16).astype(F32)
        ext = jnp.where(lanes == 0, -high, jnp.where(lanes == 1, high - delta, jnp.where(low, 0.0, up)))
        do_ext[h] = ext.astype(BF16)
        both_t[:, SPAN * h : SPAN * (h + 1)] = jnp.transpose(jnp.where(low, q[h].astype(F32), up)).astype(BF16)
    blocks = blocks()

    @pl.loop(0, BLOCKS)
    def _(n):
        active, full = block_ranges(place, n)

        def step(masked):
            kv = blocks[n]
            ones_v = jnp.where(low, jnp.ones_like(kv), kv)
            if masked:
                allowed = allowed_keys(place, n, pos_ref, start_ref)
            s = dot_right(q[...].reshape(GROUP * SPAN, 128), kv)
            dp = dot_right(do_ext[...].reshape(GROUP * SPAN, 128), ones_v)
            t = jnp.tanh(s * (1.0 / CAP))
            p = jnp.exp2(t * EXP2)
            if masked:
                p = jnp.where(allowed[None], p.reshape(GROUP, SPAN, SPAN), 0.0).reshape(GROUP * SPAN, SPAN)
            ds = (p * dp * (1.0 - t * t)).astype(BF16)
            dq[...] += dot(ds, kv).reshape(GROUP, SPAN, 128)
            dk = dot(both_t[pl.ds(0, HEAD), :], ds)
            dv = dot(both_t[pl.ds(HEAD, HEAD), :], p.astype(BF16))
            grads[n] = jnp.concatenate([dk, dv], axis=0).astype(BF16)

        pl.when(full)(lambda: step(False))
        pl.when(active & jnp.logical_not(full))(lambda: step(True))

        @pl.when(jnp.logical_not(active))
        def _():
            grads[n] = jnp.zeros((128, SPAN), BF16)

    cos, sin = rotary(place)
    for j in range(4):
        u = dq[2 * j]
        if j < 3:
            u = jnp.where(low, u, pltpu.roll(dq[2 * j + 1], HEAD, 1))
        else:
            u = jnp.where(low, u, 0.0)
        u = u * QSCALE
        dq_out[:, 128 * j : 128 * (j + 1)] = (u * cos - swap_halves(u) * sin).astype(BF16)


def query_grad_kernel(place, dq, o, x0, x1, d0, d1, gain, w_grad, after, left):
    row = lane((1, WIDTH))
    kind = row % 14
    target = 7 * (row // 14) + kind % 7
    after[...] = jnp.zeros_like(after)
    left[pl.ds(0, SPAN), :] = dot(dq()[...], one_hot(jnp.where(kind < 7, target, -1), 0, QCOL)).astype(BF16)
    left[pl.ds(SPAN, SPAN), :] = dot(o()[...], one_hot(jnp.where(kind < 7, -1, target), 0, QCOL)).astype(BF16)
    rows = normed_input(x0, x1, gain[...]).astype(BF16)
    right = jnp.concatenate([rows, d0()[...], d1()[...]], axis=0)
    w_grad[...] = dot_left(left[...], right).astype(BF16)


def project_back_kernel(
    place, dkv_parts, dq, w_q, w_kv, x0, x1, gain, g2, g3, g4, g5, after,
    own_out, other_out, w_grad, gains_out,
):
    cos, sin = rotary(place)
    row = lane((1, 128))
    order = one_hot(row % 2 * HEAD + owner_column(place, row // 2 % 16, row // 32), 0, 128)
    normed = normed_input(x0, x1, 1.0)
    d_a = dot(dq()[...], w_q()[...])
    dkv_parts = dkv_parts()
    dkv = dkv_parts[0].astype(F32)
    for j in range(1, BLOCKS):
        dkv += dkv_parts[j].astype(F32)
    u = jnp.transpose(dkv)
    dkv = jnp.where(lane((SPAN, 128)) < HEAD, u * cos - swap_halves(u) * sin, u).astype(BF16)
    d_a += dot(dkv, w_kv()[...])
    own_out[...] = d_a[:TOK]
    other_out[...] = d_a[TOK:].astype(BF16)
    g1 = jnp.sum(normed * d_a, axis=0, keepdims=True)
    gains_out[...] = jnp.concatenate([g1, g2[...], g3[...], g4[...], g5[...], jnp.zeros((3, WIDTH), F32)], axis=0)
    w_grad[...] = dot_left(dot(dkv, order).astype(BF16), (normed * gain[...]).astype(BF16)).astype(BF16)


def attn_norm_kernel(x, own, other, gain_b, gain_c, attn_out, r_out, m_out):
    attn = own[...] + other[...].astype(F32)
    attn_out[...] = attn
    resid = x[...].astype(F32) + norm_rows(attn, gain_b[...])[0]
    r_out[...] = resid
    m_out[...] = norm_rows(resid, gain_c[...])[0].astype(BF16)


def sum_parts(own, b, c, d):
    return (own[...] + b[...].astype(F32)) + (c[...].astype(F32) + d[...].astype(F32))


def ffn_norm_kernel(own, b, c, d, resid, cotangent, gain, out, d_out, gain_out):
    fo = sum_parts(own, b, c, d)
    out[...] = (resid[...] + norm_rows(fo, gain[...])[0]).astype(BF16)
    grad, gain_grad = norm_back(fo, gain[...], cotangent[...].astype(F32))
    d_out[...] = grad.astype(BF16)
    gain_out[...] = gain_grad


def ffn_back_norm_kernel(own, b, c, d, resid, attn, cotangent, gain_c, gain_b, r_out, d_out, gain_c_out, gain_b_out):
    d_m = sum_parts(own, b, c, d)
    grad, gain_grad = norm_back(resid[...], gain_c[...], d_m)
    gain_c_out[...] = gain_grad
    d_resid = cotangent[...].astype(F32) + grad
    r_out[...] = d_resid
    grad, gain_grad = norm_back(attn[...], gain_b[...], d_resid)
    gain_b_out[...] = gain_grad
    d_out[...] = grad.astype(BF16)


def input_norm_kernel(own, other, x, d_resid, gain, out):
    d_a = own[...] + other[...].astype(F32)
    out[...] = d_resid[...] + norm_back(x[...].astype(F32), gain[...], d_a)[0]


def gelu_parts(u):
    t = jnp.tanh(GELU_C * (u + 0.044715 * u * u * u))
    active = 0.5 * u * (1.0 + t)
    slope = 0.5 * (1.0 + t) + 0.5 * u * (1.0 - t * t) * GELU_C * (1.0 + 3.0 * 0.044715 * u * u)
    return active, slope


def weight_runs(which):
    runs, at = [], which * HALF_UNITS
    while at < (which + 1) * HALF_UNITS:
        count = min(TOK - at % TOK, (which + 1) * HALF_UNITS - at)
        runs.append((at // TOK, at % TOK, at - which * HALF_UNITS, count))
        at += count
    return runs


def arrange_kernel(place, pieces, gate, up, down, sems):
    copies = []
    for which, dest in enumerate((gate, up, down)):
        for core in range(2):
            source = place[KV] if core == 0 else 1 - place[KV]
            for quarter, row, unit, count in weight_runs(which):
                copies.append(
                    pltpu.make_async_copy(
                        pieces.at[2 * quarter + source, :, pl.ds(row, count), :],
                        dest.at[pl.ds(core * SIDE, SIDE), pl.ds(unit, count), :],
                        sems.at[len(copies)],
                    )
                )
    for c in copies:
        c.start()
    for c in copies:
        c.wait()


def dequantise_kernel(place, gate, up, down, gate_scale, up_scale, down_scale, more, out, codes, sems):
    out[pl.ds(0, TOK), :] = jnp.zeros((TOK, WIDTH), BF16)
    out[pl.ds(TOK, 32), :] = more[...]

    def fill(core, quarter):
        runs = []
        for which in range(3):
            for part, row, unit, count in weight_runs(which):
                first = core * HALF_UNITS + unit
                count = min(count, UNITS - first)
                if part == quarter:
                    runs.append((which, row, first, count))
        copies = [
            pltpu.make_async_copy(
                (gate, up, down)[which].at[pl.ds(first, count), :], codes.at[pl.ds(row, count), :], sems.at[n]
            )
            for n, (which, row, first, count) in enumerate(runs)
        ]
        for c in copies:
            c.start()
        for c in copies:
            c.wait()
        for which, row, first, count in runs:
            c = codes[pl.ds(row, count), :]
            if which == 0:
                weight = c.astype(F32) * gate_scale[pl.ds(first, count), :]
            elif which == 1:
                weight = ((c & -16) + 8).astype(F32) * up_scale[pl.ds(first, count), :]
            else:
                weight = ((c & -64) + 32).astype(F32) * down_scale[...]
            out[pl.ds(row, count), :] = weight.astype(BF16)

    for core in range(2):
        for quarter in range(SIDE):
            pl.when((place[KV] == core) & (place[DP] == quarter))(lambda c=core, q=quarter: fill(c, q))


def ffn_kernel(m0, m1, m2, m3, gate_w, up_w, down_w, f0, f1, f2, f3, gate_out, up_out, m, acc):
    for j, part in enumerate((m0, m1, m2, m3)):
        m[pl.ds(TOK * j, TOK), :] = part[...]
    for n in range(HID // 256):
        units = pl.ds(256 * n, 256)
        gate = dot_right(m[...], gate_w[units, :])
        up = dot_right(m[...], up_w[units, :])
        gate_out[:, 256 * n : 256 * (n + 1)] = gate.astype(BF16)
        up_out[:, 256 * n : 256 * (n + 1)] = up.astype(BF16)
        hidden = (gelu_parts(gate)[0] * up).astype(BF16)
        part = dot(hidden, down_w[units, :])
        if n == 0:
            acc[...] = part
        else:
            acc[...] += part
    f0[...] = acc[pl.ds(0, TOK), :]
    for j, out in enumerate((f1, f2, f3)):
        out[...] = acc[pl.ds(TOK * (j + 1), TOK), :].astype(BF16)


def ffn_back_kernel(
    e0, e1, e2, e3, gate_in, up_in, gate_w, up_w, down_w, f0, f1, f2, f3, hidden_out, gate_out, up_out, e, acc
):
    for j, part in enumerate((e0, e1, e2, e3)):
        e[pl.ds(TOK * j, TOK), :] = part[...]
    for n in range(HID // 256):
        units = pl.ds(256 * n, 256)
        cols = slice(256 * n, 256 * (n + 1))
        d_hidden = dot_right(e[...], down_w[units, :])
        active, slope = gelu_parts(gate_in[:, cols].astype(F32))
        up = up_in[:, cols].astype(F32)
        hidden_out[:, cols] = (active * up).astype(BF16)
        d_gate = (d_hidden * up * slope).astype(BF16)
        d_up = (d_hidden * active).astype(BF16)
        gate_out[:, cols] = d_gate
        up_out[:, cols] = d_up
        part = dot(d_gate, gate_w[units, :]) + dot(d_up, up_w[units, :])
        if n == 0:
            acc[...] = part
        else:
            acc[...] += part
    f0[...] = acc[pl.ds(0, TOK), :]
    for j, out in enumerate((f1, f2, f3)):
        out[...] = acc[pl.ds(TOK * (j + 1), TOK), :].astype(BF16)


def ffn_weight_kernel(
    place, m0, m1, m2, m3, e0, e1, e2, e3, hidden, d_gate, d_up, down_w, down_scale, out, scale_out, m, e
):
    for j, (a, b) in enumerate(zip((m0, m1, m2, m3), (e0, e1, e2, e3))):
        m[pl.ds(TOK * j, TOK), :] = a[...]
        e[pl.ds(TOK * j, TOK), :] = b[...]
    empty = SIDE * TOK - 3 * HALF_UNITS
    out[pl.ds(2 * SIDE - 2, 2), :, pl.ds(TOK - empty, empty), :] = jnp.zeros((2, SIDE, empty, WIDTH), BF16)
    per_unit = 1.0 / down_scale[...]
    scale_grad = jnp.zeros((1, WIDTH), F32)
    for which, (left, right) in enumerate(((d_gate, m), (d_up, m), (hidden, e))):
        runs = weight_runs(which)
        for n in range(HID // 256):
            first = 256 * n
            part = dot_left(left[:, first : first + 256], right[...])
            if which == 2:
                level = down_w[pl.ds(first, 256), :].astype(F32) * per_unit
                level = jnp.floor(level * (1.0 / 64.0)) * 64.0 + 32.0
                scale_grad += jnp.sum(part * level, axis=0, keepdims=True)
            part = part.astype(BF16)
            for piece in range(2 * SIDE):
                core = place[KV] if piece < SIDE else 1 - place[KV]
                for quarter, row, unit, count in runs:
                    low = max(piece * HALF_UNITS + unit, first)
                    high = min(piece * HALF_UNITS + unit + count, first + 256)
                    if low < high:
                        at = row + low - piece * HALF_UNITS - unit
                        out[2 * quarter + core, piece % SIDE, pl.ds(at, high - low), :] = part[low - first : high - first]
    scale_out[...] = scale_grad


def finish_kernel(
    place, own, other, gate, up, gate_scale, up_scale, down_scale, g_gate, g_up, g_down, s_gate, s_up, sums, parts
):
    for k in range(SIDE):
        quarter = (place[DP] - k) & 3
        parts[2 * quarter + place[KV]] = own[pl.ds(TOK * k, TOK), :]
        parts[2 * quarter + 1 - place[KV]] = other[pl.ds(TOK * k, TOK), :]
    sums[...] = jnp.zeros_like(sums)
    for core in range(2):
        for which in range(3):
            for quarter, row, unit, count in weight_runs(which):
                first = core * HALF_UNITS + unit
                count = min(count, UNITS - first)
                rows = pl.ds(first, count)
                total = parts[2 * quarter + core, pl.ds(row, count), :].astype(F32)
                if which == 0:
                    g_gate[rows, :] = total * gate_scale[rows, :]
                    part = jnp.sum(total * gate[rows, :].astype(F32), axis=1, keepdims=True)
                    sums[0, rows, :] = jnp.broadcast_to(part, (count, 128))
                elif which == 1:
                    g_up[rows, :] = total * up_scale[rows, :]
                    part = jnp.sum(total * ((up[rows, :] & -16) + 8).astype(F32), axis=1, keepdims=True)
                    sums[1, rows, :] = jnp.broadcast_to(part, (count, 128))
                else:
                    g_down[rows, :] = total * down_scale[...]
    s_gate[...] = jnp.transpose(sums[0])[:1, :UNITS]
    s_up[...] = jnp.transpose(sums[1])[:1, :UNITS]


def shards(
    layer_input, cotangent, doc_bounds, w_query, key_weight, value_weight, w_out,
    gain_attn_in, gain_attn_out, gain_ffn_in, gain_ffn_out,
    code_gate, code_up, code_down, scale_gate, scale_up, scale_down,
):
    ctx, kv, dp = lax.axis_index("ctx"), lax.axis_index("kv"), lax.axis_index("dp")
    place = jnp.concatenate([jnp.stack([ctx, dp, kv]).astype(jnp.int32), doc_bounds[0]])
    x = layer_input.reshape(TOK, WIDTH)
    cot = cotangent.reshape(TOK, WIDTH)
    gain_1, gain_2, gain_3, gain_4 = (
        g.reshape(1, WIDTH) for g in (gain_attn_in, gain_attn_out, gain_ffn_in, gain_ffn_out)
    )
    gate_col, up_col, down_row = scale_gate[:, None], scale_up[:, None], scale_down[None, :]
    rows_f32, rows_bf16, row_f32 = ((TOK, WIDTH), F32), ((TOK, WIDTH), BF16), ((1, WIDTH), F32)

    shard = jnp.concatenate([w_query.T, key_weight.T, value_weight.T, w_out.T], axis=0)
    rounds = [group_round(shard, i) for i in range(4)]
    x_other = from_core(x)

    qkv_rows = jnp.concatenate(
        [r[:8] for r in rounds] + [r[8:9] for r in rounds] + [jnp.zeros((4, WIDTH), BF16)], axis=0
    )
    out_rows = jnp.concatenate([r[8:] for r in rounds], axis=0)
    qkv_rows, out_rows = lax.optimization_barrier((qkv_rows, out_rows))

    (quarter,) = kernel_call(
        dequantise_kernel,
        "shhhvvvv",
        "v",
        [((TOK + 32, WIDTH), BF16)],
        "dequantise",
        (place, code_gate.T, code_up.T, code_down, gate_col, up_col, down_row, out_rows),
        [pltpu.VMEM((TOK, WIDTH), jnp.int32), pltpu.SemaphoreType.DMA((2,))],
        vmem=58,
    )
    quarter, x_other = lax.optimization_barrier((quarter, x_other))
    quarters = ring(back_y, quarter)

    def gathered(rows):
        copies = jnp.broadcast_to(rows[None], (BLOCKS,) + rows.shape)
        return all_to_all(copies).reshape(-1, WIDTH)

    qkv_rows = gathered(qkv_rows)

    keys, w_kv = kernel_call(
        kv_kernel,
        "sffvv",
        "ff",
        [((BLOCKS, SPAN, 128), BF16), ((128, WIDTH), BF16)],
        "keys",
        (place, x, x_other, gain_1, qkv_rows),
        us=4,
        vmem=20,
    )
    quarters, after = lax.optimization_barrier((quarters, w_kv))
    ffn_w = lax.all_gather(jnp.stack([p[:TOK] for p in quarters]), ("dp", "kv"))
    out_rows = ring(back_z, jnp.concatenate([p[TOK:] for p in quarters], axis=0))
    keys = all_to_all(keys)
    q, w_q = kernel_call(
        query_kernel,
        "sffvfh",
        "ff",
        [((SPAN, QCOL), BF16), ((QCOL, WIDTH), BF16)],
        "queries",
        (place, x, x_other, gain_1, qkv_rows, after),
        us=4,
        vmem=58,
    )
    o, inv = kernel_call(
        attend_kernel,
        "sfv",
        "ff",
        [((SPAN, QCOL), BF16), ((SPAN, 128), F32)],
        "attend",
        (place, q, keys),
        [
            pltpu.VMEM((GROUP, SPAN, 128), BF16),
            pltpu.VMEM((GROUP, SPAN, 128), F32),
            pltpu.VMEM((SPAN, SPAN), jnp.int32),
            pltpu.VMEM((SPAN, SPAN), jnp.int32),
        ],
        us=16,
        vmem=24,
    )
    attn_own, attn_other = kernel_call(
        attn_project_kernel,
        "sfffff",
        "vv",
        [rows_f32, rows_bf16],
        "attn_project",
        (place, *out_rows, o),
        vmem=16,
    )
    attn_other = from_core(attn_other)
    attn, resid, m_own = kernel_call(
        attn_norm_kernel,
        "vvvvv",
        "vvv",
        [rows_f32, rows_f32, rows_bf16],
        "attn_norm",
        (x, attn_own, attn_other, gain_2, gain_3),
    )

    m_parts = ring(back_z, m_own)
    m_parts[1], ffn_w = lax.optimization_barrier((m_parts[1], ffn_w))
    wide = ((SIDE * TOK, HID), BF16)
    unit_rows = ((2 * SIDE, HALF_UNITS, WIDTH), BF16)
    ffn_w = kernel_call(
        arrange_kernel,
        "sh",
        "vvv",
        [unit_rows] * 3,
        "arrange",
        (place, ffn_w),
        [pltpu.SemaphoreType.DMA((12,))],
        us=4,
    )
    gate_w, up_w, down_w = (w.reshape(HID, WIDTH) for w in ffn_w)
    ffn_scratch = [pltpu.VMEM((SIDE * TOK, WIDTH), BF16), pltpu.VMEM((SIDE * TOK, WIDTH), F32)]
    *fo_parts, gate, up = kernel_call(
        ffn_kernel,
        "vvvvvvv",
        "vvvvvv",
        [rows_f32] + [rows_bf16] * 3 + [wide, wide],
        "ffn",
        (*m_parts, gate_w, up_w, down_w),
        ffn_scratch,
        us=6,
        vmem=16,
    )
    fo_parts = ring_back(back_z, fo_parts)
    block_out, d_fo, g_gain_4 = kernel_call(
        ffn_norm_kernel, "vvvvvvv", "vvv", [rows_bf16, rows_bf16, row_f32], "ffn_norm", (*fo_parts, resid, cot, gain_4)
    )

    d_parts = ring(back_z, d_fo)
    *dm_parts, hidden, d_gate, d_up = kernel_call(
        ffn_back_kernel,
        "vvvvvvvvv",
        "vvvvvvv",
        [rows_f32] + [rows_bf16] * 3 + [wide] * 3,
        "ffn_back",
        (*d_parts, gate, up, gate_w, up_w, down_w),
        ffn_scratch,
        us=10,
        vmem=20,
    )
    dm_parts = ring_back(back_z, dm_parts)
    weight_grads, g_down = kernel_call(
        ffn_weight_kernel,
        "s" + "v" * 13,
        "fv",
        [((2 * SIDE, SIDE, TOK, WIDTH), BF16), row_f32],
        "ffn_weight",
        (place, *m_parts, *d_parts, hidden, d_gate, d_up, down_w, down_row),
        [
            pltpu.VMEM((SIDE * TOK, WIDTH), BF16),
            pltpu.VMEM((SIDE * TOK, WIDTH), BF16),
        ],
        us=8,
        vmem=20,
    )
    dm_parts, weight_grads = lax.optimization_barrier((dm_parts, weight_grads))
    weight_grads = lax.psum_scatter(weight_grads, ("dp", "kv"), scatter_dimension=0)
    d_resid, d_attn, g_gain_3, g_gain_2 = kernel_call(
        ffn_back_norm_kernel,
        "vvvvvvvvv",
        "vvvv",
        [rows_f32, rows_bf16, row_f32, row_f32],
        "ffn_back_norm",
        (*dm_parts, resid, attn, cot, gain_3, gain_2),
    )
    d_attn_other = from_core(d_attn)

    dq, key_grads = kernel_call(
        attend_back_kernel,
        "sffffffffff",
        "ff",
        [((SPAN, QCOL), BF16), ((BLOCKS, 128, SPAN), BF16)],
        "attend_back",
        (place, d_attn, d_attn_other, *out_rows, q, o, inv, keys),
        [
            pltpu.VMEM((GROUP, SPAN, 128), BF16),
            pltpu.VMEM((GROUP, SPAN, 128), F32),
            pltpu.VMEM((GROUP, SPAN, 128), BF16),
            pltpu.VMEM((128, GROUP * SPAN), BF16),
            pltpu.VMEM((SPAN, SPAN), jnp.int32),
            pltpu.VMEM((SPAN, SPAN), jnp.int32),
        ],
        us=26,
        vmem=58,
    )
    key_grads = all_to_all(key_grads)
    q_grads, after = kernel_call(
        query_grad_kernel,
        "sffffffv",
        "fv",
        [((WIDTH, WIDTH), BF16), ((8, 128), F32)],
        "query_grad",
        (place, dq, o, x, x_other, d_attn, d_attn_other, gain_1),
        [pltpu.VMEM((2 * SPAN, WIDTH), BF16)],
        us=5,
        vmem=58,
    )

    def total(parts):
        a, b, c, d = (p.astype(F32) for p in parts)
        return (a + b) + (c + d)

    q_grads = lax.psum_scatter(q_grads.reshape(SIDE, 224, WIDTH), "dp", scatter_dimension=0)
    da_own, da_other, kv_grads, gains = kernel_call(
        project_back_kernel,
        "sffffffvvvvvv",
        "vvvv",
        [rows_f32, rows_bf16, ((128, WIDTH), BF16), ((8, WIDTH), F32)],
        "project_back",
        (place, key_grads, dq, w_q, w_kv, x, x_other, gain_1, g_gain_2, g_gain_3, g_gain_4, g_down, after),
        us=4,
        vmem=58,
    )
    weight_grads, da_other = lax.optimization_barrier((weight_grads, da_other))
    weight_grads = weight_grads.reshape(SIDE, TOK, WIDTH)
    eighth = total(ring_back(back_y, [weight_grads[k] for k in range(SIDE)])).astype(BF16)
    eighths = jnp.concatenate(ring(back_x, eighth), axis=0)

    (grad_input,) = kernel_call(
        input_norm_kernel, "vvvvv", "v", [rows_f32], "input_norm", (da_own, from_core(da_other), x, d_resid, gain_1)
    )

    gains = (gains + from_core(gains)).astype(BF16)
    kv_grads = [jnp.concatenate([kv_grads[32 * k : 32 * (k + 1)], gains], axis=0) for k in range(SIDE)]
    kv_grads = total(ring_back(back_x, kv_grads)).astype(BF16)
    gains = jnp.broadcast_to(kv_grads[None, 32:], (BLOCKS, 8, WIDTH))
    w_grads = [q_grads.reshape(BLOCKS, 14, WIDTH), kv_grads[:32].reshape(BLOCKS, 2, WIDTH), gains]
    w_grads = all_to_all(jnp.concatenate(w_grads, axis=1))
    w_grads, grad_input = lax.optimization_barrier((w_grads, grad_input))
    w_grads = jnp.sum(w_grads.astype(F32), axis=0)
    gains = w_grads[16:]
    pairs = [(2 * n + k, 2 * (2 * k + n // 2) + n % 2) for n in range(SIDE) for k in range(2)]
    grad_w = lax.ppermute(w_grads[:16], ("dp", "kv"), pairs)

    grad_code_gate, grad_code_up, grad_code_down, grad_scale_gate, grad_scale_up = kernel_call(
        finish_kernel,
        "svvvvvvv",
        "vvvvv",
        [((UNITS, WIDTH), F32)] * 3 + [((1, UNITS), F32)] * 2,
        "finish",
        (place, eighths, from_core(eighths), code_gate.T, code_up.T, gate_col, up_col, down_row),
        [pltpu.VMEM((2, 384, 128), F32), pltpu.VMEM((2 * SIDE, TOK, WIDTH), BF16)],
        us=3,
    )
    grads = (grad_code_gate, grad_code_up, grad_code_down, grad_scale_gate[0], grad_scale_up[0])

    return (
        block_out.reshape(layer_input.shape),
        grad_input.reshape(layer_input.shape),
        grad_w[:7].T,
        grad_w[14:15].T,
        grad_w[15:16].T,
        grad_w[7:14].T,
        gains[0],
        gains[1],
        gains[2],
        gains[3],
        grads[0].T,
        grads[1].T,
        *grads[2:],
        gains[4],
    )


def solution(mesh):
    tokens = P("dp", "ctx", "kv", None, None)
    columns = P(None, ("dp", "kv", "ctx"))
    hidden = (P(None, "ctx"), P(None, "ctx"), P("ctx", None), P("ctx"), P("ctx"), P())
    return jax.shard_map(
        shards,
        mesh=mesh,
        in_specs=(tokens, tokens, P("dp", None)) + (columns,) * 4 + (P(),) * 4 + hidden,
        out_specs=(tokens, tokens) + (columns,) * 4 + (P(),) * 4 + hidden,
        check_vma=False,
    )
```

```python
import math

import jax
import jax.numpy as jnp
from jax import lax
from jax.experimental import pallas as pl
from jax.experimental.pallas import tpu as pltpu
from jax.sharding import PartitionSpec as P

EPS = 1e-06
CAP = 50.0
QSCALE = 0.125
GELU_C = math.sqrt(2.0 / math.pi)
EXP2 = CAP * math.log2(math.e)

TOK = 128
SPAN = 256
WIDTH = 896
HEAD = 64
GROUP = 7
QCOL = 512
SIDE = 4
UNITS = 304
UPAD = 320
HALF_UNITS = 160
HID = 1280
HALF_ROWS = 512
BLOCKS = 16
F32 = jnp.float32
BF16 = jnp.bfloat16
VMEM = pl.BlockSpec(memory_space=pltpu.VMEM)
SMEM = pl.BlockSpec(memory_space=pltpu.SMEM)
HBM = pl.BlockSpec(memory_space=pltpu.HBM)


class Fetched:
    def __init__(self, copy, buffer):
        self.copy, self.buffer = copy, buffer

    def __call__(self):
        if self.copy is not None:
            self.copy.wait()
            self.copy = None
        return self.buffer


def kernel_call(body, ins, outs, out, name, args, scratch=(), us=2.0, vmem=16):
    fetched = [i for i, kind in enumerate(ins) if kind == "f"]
    stored = [i for i, kind in enumerate(outs) if kind == "f"]
    count = len(fetched) + len(stored)

    def whole(*refs):
        if not count:
            return body(*refs)
        sems, buffers = refs[-1], refs[len(refs) - 1 - count : -1]
        refs = list(refs[: len(refs) - 1 - count])
        copies = [pltpu.make_async_copy(refs[i], buffers[n], sems.at[n]) for n, i in enumerate(fetched)]
        for c in copies:
            c.start()
        for n, i in enumerate(fetched):
            refs[i] = Fetched(copies[n], buffers[n])
        back = []
        for n, i in enumerate(stored, len(fetched)):
            back.append(pltpu.make_async_copy(buffers[n], refs[len(ins) + i], sems.at[n]))
            refs[len(ins) + i] = buffers[n]
        body(*refs)
        for c in back:
            c.start()
        for c in back:
            c.wait()

    scratch = list(scratch)
    if count:
        scratch += [pltpu.VMEM(args[i].shape, args[i].dtype) for i in fetched]
        scratch += [pltpu.VMEM(*out[i]) for i in stored]
        scratch.append(pltpu.SemaphoreType.DMA((count,)))
    spec = {"s": SMEM, "v": VMEM, "h": HBM, "f": HBM}
    return pl.pallas_call(
        whole,
        out_shape=[jax.ShapeDtypeStruct(shape, dtype) for shape, dtype in out],
        in_specs=[spec[kind] for kind in ins],
        out_specs=[spec[kind] for kind in outs],
        scratch_shapes=scratch,
        compiler_params=pltpu.CompilerParams(vmem_limit_bytes=vmem * 1024 * 1024),
        cost_estimate=pl.CostEstimate(flops=int(us * 1e9), bytes_accessed=0, transcendentals=0),
        name=name,
    )(*args)


def dot(left, right):
    return lax.dot_general(left, right, (((1,), (0,)), ((), ())), preferred_element_type=F32)


def dot_right(left, right):
    return lax.dot_general(left, right, (((1,), (1,)), ((), ())), preferred_element_type=F32)


def dot_left(left, right):
    return lax.dot_general(left, right, (((0,), (0,)), ((), ())), preferred_element_type=F32)


def from_core(x):
    return lax.ppermute(x, "kv", [(0, 1), (1, 0)])


def back_x(x, k):
    return lax.ppermute(x, "dp", [(i, (i + k) % SIDE) for i in range(SIDE)])


def back_y(x, k):
    pairs = [(z * SIDE + y, z * SIDE + (y + k) % SIDE) for z in range(SIDE) for y in range(SIDE)]
    return lax.ppermute(x, "ctx", pairs)


def back_z(x, k):
    pairs = [(z * SIDE + y, (z + k) % SIDE * SIDE + y) for z in range(SIDE) for y in range(SIDE)]
    return lax.ppermute(x, "ctx", pairs)


def group_round(x, i, back=False):
    pairs = [(n, 2 * ((n % 4 + i) % SIDE) + n // 4) for n in range(8)]
    if back:
        pairs = [(b, a) for a, b in pairs]
    return lax.ppermute(x, ("dp", "kv"), pairs)


def all_to_all(x):
    return lax.all_to_all(x, "ctx", split_axis=0, concat_axis=0, tiled=True)


def ring(send, x):
    got = {k: send(x, k) for k in (1, 3, 2)}
    return [x, got[1], got[2], got[3]]


def ring_back(send, parts):
    got = {k: send(parts[k], SIDE - k) for k in (1, 3, 2)}
    return [parts[0], got[1], got[2], got[3]]


def norm_rows(rows, gain):
    inverse = lax.rsqrt(jnp.mean(rows * rows, axis=-1, keepdims=True) + EPS)
    return rows * inverse * gain, inverse


def norm_back(rows, gain, incoming):
    inverse = lax.rsqrt(jnp.mean(rows * rows, axis=-1, keepdims=True) + EPS)
    normed = rows * inverse
    scaled = incoming * gain
    grad = inverse * (scaled - normed * jnp.mean(scaled * normed, axis=-1, keepdims=True))
    return grad, jnp.sum(incoming * normed, axis=0, keepdims=True)


def lane(shape):
    return lax.broadcasted_iota(jnp.int32, shape, len(shape) - 1)


def swap_halves(x):
    return jnp.where(lane(x.shape) % HEAD < HEAD // 2, pltpu.roll(x, 96, 1), pltpu.roll(x, 32, 1))


CTX, DP, KV, STARTS = 0, 1, 2, 3


def doc_start(place, p):
    start = jnp.zeros_like(p)
    for i in range(8):
        b = place[STARTS + i]
        start = jnp.where(p >= b, jnp.maximum(start, b), start)
    return start


def span_places(shape, dim, chip, kv):
    i = lax.broadcasted_iota(jnp.int32, shape, dim)
    half = jnp.where(i < TOK, kv, 1 - kv)
    return chip * SPAN + half * TOK + i % TOK


def rotary(place):
    spot = span_places((SPAN, 128), 0, place[CTX], place[KV])
    index = lane((SPAN, 128)) % HEAD
    freq = jnp.exp((index % (HEAD // 2)).astype(F32) * (-2.0 * math.log(10000.0) / HEAD))
    angle = (spot - doc_start(place, spot)).astype(F32) * freq
    return jnp.cos(angle), jnp.where(index < HEAD // 2, -1.0, 1.0) * jnp.sin(angle)


def one_hot(target, first, count):
    rows = lax.broadcasted_iota(jnp.int32, (count, target.shape[1]), 0) + first
    return jnp.where(rows == target, 1.0, 0.0).astype(BF16)


def owner_column(place, ctx, turn):
    return ((place[DP] - turn) & 3) * 16 + ctx


def qkv_target(place):
    row = lane((1, 576))
    turn, inner = row // 144, row % 144
    value = inner >= 128
    col = owner_column(place, jnp.where(value, inner - 128, inner // 8), turn)
    target = jnp.where(inner % 8 < 7, 7 * col + inner % 8, QCOL + col)
    return jnp.where(value, QCOL + HEAD + col, target)


def out_order(place):
    row = lane((1, QCOL))
    kind = row % 8 - 1
    target = 7 * owner_column(place, row // 8 % 16, row // 128) + kind
    return one_hot(jnp.where(kind >= 0, target, -1), 0, QCOL)


def normed_input(x0, x1, gain):
    rows = jnp.concatenate([x0()[...], x1()[...]], axis=0).astype(F32)
    return norm_rows(rows, gain)[0]


def kv_kernel(place, x0, x1, gain, w0, w1, w2, w3, kv_out, w_out):
    cos, sin = rotary(place)
    order = one_hot(qkv_target(place), QCOL, 128)
    rows = normed_input(x0, x1, gain[...]).astype(BF16)
    w_cols = dot(order, jnp.concatenate([w0[...], w1[...], w2[...], w3[...]], axis=0)).astype(BF16)
    w_out[...] = w_cols
    u = dot_right(rows, w_cols)
    kv = jnp.where(lane((SPAN, 128)) < HEAD, u * cos + swap_halves(u) * sin, u).astype(BF16)
    for j in range(BLOCKS):
        kv_out[j] = kv


def query_kernel(place, x0, x1, gain, w0, w1, w2, w3, after, q_out, w_out):
    cos, sin = rotary(place)
    order = one_hot(qkv_target(place), 0, QCOL)
    rows = normed_input(x0, x1, gain[...]).astype(BF16)
    w_cols = dot(order, jnp.concatenate([w0()[...], w1()[...], w2()[...], w3()[...]], axis=0)).astype(BF16)
    w_out[...] = w_cols
    raw = dot_right(rows, w_cols)
    for j in range(4):
        u = raw[:, 128 * j : 128 * (j + 1)]
        q_out[:, 128 * j : 128 * (j + 1)] = ((u * cos + swap_halves(u) * sin) * QSCALE).astype(BF16)


def spread_heads(q, out):
    low = lane((SPAN, 128)) < HEAD
    for j in range(4):
        u = q[:, 128 * j : 128 * (j + 1)].astype(F32)
        out[2 * j] = jnp.where(low, u, 0.0).astype(BF16)
        if j < 3:
            out[2 * j + 1] = jnp.where(low, pltpu.roll(u, HEAD, 1), 0.0).astype(BF16)


def attn_project_kernel(place, w0, w1, w2, w3, o, own_out, other_out):
    rows = jnp.concatenate([w0()[...], w1()[...], w2()[...], w3()[...]], axis=0)
    attn = dot(dot(o()[...], out_order(place)).astype(BF16), rows)
    own_out[...] = attn[:TOK]
    other_out[...] = attn[TOK:].astype(BF16)


def block_ranges(place, n):
    first = place[CTX] * SPAN
    low_start, high_start = doc_start(place, first), doc_start(place, first + SPAN - 1)
    active = (n <= place[CTX]) & (n * SPAN + SPAN - 1 >= low_start)
    full = (n < place[CTX]) & (n * SPAN >= high_start)
    return active, full


def query_places(place, pos_ref, start_ref):
    pos = span_places((SPAN, SPAN), 0, place[CTX], place[KV])
    pos_ref[...] = pos
    start_ref[...] = doc_start(place, pos)


def allowed_keys(place, source, pos_ref, start_ref):
    keys = span_places((SPAN, SPAN), 1, source, place[KV])
    return (keys <= pos_ref[...]) & (keys >= start_ref[...])


def attend_kernel(place, q_cols, blocks, o_out, inv_out, q, acc, pos_ref, start_ref):
    query_places(place, pos_ref, start_ref)
    acc[...] = jnp.zeros_like(acc)
    spread_heads(q_cols(), q)
    low = lane((SPAN, 128)) < HEAD

    @pl.loop(0, BLOCKS)
    def _(n):
        active, full = block_ranges(place, n)

        def step(masked):
            kv = blocks[n]
            ones_v = jnp.where(low, jnp.ones_like(kv), kv)
            if masked:
                allowed = allowed_keys(place, n, pos_ref, start_ref)
            s = dot_right(q[...].reshape(GROUP * SPAN, 128), kv)
            p = jnp.exp2(jnp.tanh(s * (1.0 / CAP)) * EXP2)
            if masked:
                p = jnp.where(allowed[None], p.reshape(GROUP, SPAN, SPAN), 0.0).reshape(GROUP * SPAN, SPAN)
            acc[...] += dot(p.astype(BF16), ones_v).reshape(GROUP, SPAN, 128)

        pl.when(full)(lambda: step(False))
        pl.when(active & jnp.logical_not(full))(lambda: step(True))

    lanes = lane((SPAN, 128))
    inverse = jnp.ones((SPAN, 128), F32)
    for j in range(4):
        a = acc[2 * j]
        if j < 3:
            b = acc[2 * j + 1]
            total = jnp.where(low, a, pltpu.roll(b, HEAD, 1))
            value = jnp.where(low, pltpu.roll(a, HEAD, 1), b)
            inverse = jnp.where(lanes == 2 * j + 1, 1.0 / b, inverse)
        else:
            total = jnp.where(low, a, 1.0)
            value = jnp.where(low, pltpu.roll(a, HEAD, 1), 0.0)
        inverse = jnp.where(lanes == 2 * j, 1.0 / a, inverse)
        o_out[:, 128 * j : 128 * (j + 1)] = (value / total).astype(BF16)
    inv_out[...] = inverse


def attend_back_kernel(
    place, d0, d1, w0, w1, w2, w3, q_cols, o, inv, blocks,
    dq_out, grads, q, dq, do_ext, both_t, pos_ref, start_ref,
):
    query_places(place, pos_ref, start_ref)
    dq[...] = jnp.zeros_like(dq)
    rows = jnp.concatenate([d0()[...], d1()[...]], axis=0)
    w = jnp.concatenate([w0()[...], w1()[...], w2()[...], w3()[...]], axis=0)
    d_o = dot_right(dot_right(rows, w).astype(BF16), out_order(place))
    low = lane((SPAN, 128)) < HEAD
    lanes = lane((SPAN, 128))
    spread_heads(q_cols(), q)
    o, inv = o(), inv()
    for h in range(GROUP):
        j = h // 2
        cols = slice(128 * j, 128 * (j + 1))
        mine = low if h % 2 == 0 else jnp.logical_not(low)
        scale = inv[:, h : h + 1]
        up = d_o[:, cols] * scale
        delta = jnp.sum(jnp.where(mine, up * o[:, cols].astype(F32), 0.0), axis=1, keepdims=True)
        if h % 2 == 0:
            up = pltpu.roll(up, HEAD, 1)
        high = delta.astype(BF16).astype(F32)
        ext = jnp.where(lanes == 0, -high, jnp.where(lanes == 1, high - delta, jnp.where(low, 0.0, up)))
        do_ext[h] = ext.astype(BF16)
        both_t[:, SPAN * h : SPAN * (h + 1)] = jnp.transpose(jnp.where(low, q[h].astype(F32), up)).astype(BF16)
    blocks = blocks()

    @pl.loop(0, BLOCKS)
    def _(n):
        active, full = block_ranges(place, n)

        def step(masked):
            kv = blocks[n]
            ones_v = jnp.where(low, jnp.ones_like(kv), kv)
            if masked:
                allowed = allowed_keys(place, n, pos_ref, start_ref)
            s = dot_right(q[...].reshape(GROUP * SPAN, 128), kv)
            dp = dot_right(do_ext[...].reshape(GROUP * SPAN, 128), ones_v)
            t = jnp.tanh(s * (1.0 / CAP))
            p = jnp.exp2(t * EXP2)
            if masked:
                p = jnp.where(allowed[None], p.reshape(GROUP, SPAN, SPAN), 0.0).reshape(GROUP * SPAN, SPAN)
            ds = (p * dp * (1.0 - t * t)).astype(BF16)
            dq[...] += dot(ds, kv).reshape(GROUP, SPAN, 128)
            dk = dot(both_t[pl.ds(0, HEAD), :], ds)
            dv = dot(both_t[pl.ds(HEAD, HEAD), :], p.astype(BF16))
            grads[n] = jnp.concatenate([dk, dv], axis=0).astype(BF16)

        pl.when(full)(lambda: step(False))
        pl.when(active & jnp.logical_not(full))(lambda: step(True))

        @pl.when(jnp.logical_not(active))
        def _():
            grads[n] = jnp.zeros((128, SPAN), BF16)

    cos, sin = rotary(place)
    for j in range(4):
        u = dq[2 * j]
        if j < 3:
            u = jnp.where(low, u, pltpu.roll(dq[2 * j + 1], HEAD, 1))
        else:
            u = jnp.where(low, u, 0.0)
        u = u * QSCALE
        dq_out[:, 128 * j : 128 * (j + 1)] = (u * cos - swap_halves(u) * sin).astype(BF16)


def query_grad_kernel(place, dq, o, x0, x1, d0, d1, gain, w_grad, after, left):
    row = lane((1, WIDTH))
    kind = row % 14
    target = 7 * (row // 14) + kind % 7
    after[...] = jnp.zeros_like(after)
    left[pl.ds(0, SPAN), :] = dot(dq()[...], one_hot(jnp.where(kind < 7, target, -1), 0, QCOL)).astype(BF16)
    left[pl.ds(SPAN, SPAN), :] = dot(o()[...], one_hot(jnp.where(kind < 7, -1, target), 0, QCOL)).astype(BF16)
    rows = normed_input(x0, x1, gain[...]).astype(BF16)
    right = jnp.concatenate([rows, d0()[...], d1()[...]], axis=0)
    w_grad[...] = dot_left(left[...], right).astype(BF16)


def project_back_kernel(
    place, dkv_parts, dq, w_q, w_kv, x0, x1, gain, g2, g3, g4, g5, after,
    own_out, other_out, w_grad, gains_out,
):
    cos, sin = rotary(place)
    row = lane((1, 128))
    order = one_hot(row % 2 * HEAD + owner_column(place, row // 2 % 16, row // 32), 0, 128)
    normed = normed_input(x0, x1, 1.0)
    d_a = dot(dq()[...], w_q()[...])
    dkv_parts = dkv_parts()
    dkv = dkv_parts[0].astype(F32)
    for j in range(1, BLOCKS):
        dkv += dkv_parts[j].astype(F32)
    u = jnp.transpose(dkv)
    dkv = jnp.where(lane((SPAN, 128)) < HEAD, u * cos - swap_halves(u) * sin, u).astype(BF16)
    d_a += dot(dkv, w_kv()[...])
    own_out[...] = d_a[:TOK]
    other_out[...] = d_a[TOK:].astype(BF16)
    g1 = jnp.sum(normed * d_a, axis=0, keepdims=True)
    gains_out[...] = jnp.concatenate([g1, g2[...], g3[...], g4[...], g5[...], jnp.zeros((3, WIDTH), F32)], axis=0)
    w_grad[...] = dot_left(dot(dkv, order).astype(BF16), (normed * gain[...]).astype(BF16)).astype(BF16)


def attn_norm_kernel(x, own, other, gain_b, gain_c, attn_out, r_out, m_out):
    attn = own[...] + other[...].astype(F32)
    attn_out[...] = attn
    resid = x[...].astype(F32) + norm_rows(attn, gain_b[...])[0]
    r_out[...] = resid
    m_out[...] = norm_rows(resid, gain_c[...])[0].astype(BF16)


def sum_parts(own, b, c, d):
    return (own[...] + b[...].astype(F32)) + (c[...].astype(F32) + d[...].astype(F32))


def ffn_norm_kernel(own, b, c, d, resid, cotangent, gain, out, d_out, gain_out):
    fo = sum_parts(own, b, c, d)
    out[...] = (resid[...] + norm_rows(fo, gain[...])[0]).astype(BF16)
    grad, gain_grad = norm_back(fo, gain[...], cotangent[...].astype(F32))
    d_out[...] = grad.astype(BF16)
    gain_out[...] = gain_grad


def ffn_back_norm_kernel(own, b, c, d, resid, attn, cotangent, gain_c, gain_b, r_out, d_out, gain_c_out, gain_b_out):
    d_m = sum_parts(own, b, c, d)
    grad, gain_grad = norm_back(resid[...], gain_c[...], d_m)
    gain_c_out[...] = gain_grad
    d_resid = cotangent[...].astype(F32) + grad
    r_out[...] = d_resid
    grad, gain_grad = norm_back(attn[...], gain_b[...], d_resid)
    gain_b_out[...] = gain_grad
    d_out[...] = grad.astype(BF16)


def input_norm_kernel(own, other, x, d_resid, gain, out):
    d_a = own[...] + other[...].astype(F32)
    out[...] = d_resid[...] + norm_back(x[...].astype(F32), gain[...], d_a)[0]


def gelu_parts(u):
    t = jnp.tanh(GELU_C * (u + 0.044715 * u * u * u))
    active = 0.5 * u * (1.0 + t)
    slope = 0.5 * (1.0 + t) + 0.5 * u * (1.0 - t * t) * GELU_C * (1.0 + 3.0 * 0.044715 * u * u)
    return active, slope


def weight_runs(which):
    runs, at = [], which * HALF_UNITS
    while at < (which + 1) * HALF_UNITS:
        count = min(TOK - at % TOK, (which + 1) * HALF_UNITS - at)
        runs.append((at // TOK, at % TOK, at - which * HALF_UNITS, count))
        at += count
    return runs


def arrange_kernel(place, pieces, gate, up, down, sems):
    copies = []
    for which, dest in enumerate((gate, up, down)):
        for core in range(2):
            source = place[KV] if core == 0 else 1 - place[KV]
            for quarter, row, unit, count in weight_runs(which):
                copies.append(
                    pltpu.make_async_copy(
                        pieces.at[2 * quarter + source, :, pl.ds(row, count), :],
                        dest.at[pl.ds(core * SIDE, SIDE), pl.ds(unit, count), :],
                        sems.at[len(copies)],
                    )
                )
    for c in copies:
        c.start()
    for c in copies:
        c.wait()


def dequantise_kernel(place, gate, up, down, gate_scale, up_scale, down_scale, out, codes, sems):
    out[...] = jnp.zeros((TOK, WIDTH), BF16)

    def fill(core, quarter):
        runs = []
        for which in range(3):
            for part, row, unit, count in weight_runs(which):
                first = core * HALF_UNITS + unit
                count = min(count, UNITS - first)
                if part == quarter:
                    runs.append((which, row, first, count))
        copies = [
            pltpu.make_async_copy(
                (gate, up, down)[which].at[pl.ds(first, count), :], codes.at[pl.ds(row, count), :], sems.at[n]
            )
            for n, (which, row, first, count) in enumerate(runs)
        ]
        for c in copies:
            c.start()
        for c in copies:
            c.wait()
        for which, row, first, count in runs:
            c = codes[pl.ds(row, count), :]
            if which == 0:
                weight = c.astype(F32) * gate_scale[pl.ds(first, count), :]
            elif which == 1:
                weight = ((c & -16) + 8).astype(F32) * up_scale[pl.ds(first, count), :]
            else:
                weight = ((c & -64) + 32).astype(F32) * down_scale[...]
            out[pl.ds(row, count), :] = weight.astype(BF16)

    for core in range(2):
        for quarter in range(SIDE):
            pl.when((place[KV] == core) & (place[DP] == quarter))(lambda c=core, q=quarter: fill(c, q))


def ffn_kernel(m0, m1, m2, m3, gate_w, up_w, down_w, f0, f1, f2, f3, gate_out, up_out, m, acc):
    for j, part in enumerate((m0, m1, m2, m3)):
        m[pl.ds(TOK * j, TOK), :] = part[...]
    for n in range(HID // 256):
        units = pl.ds(256 * n, 256)
        gate = dot_right(m[...], gate_w[units, :])
        up = dot_right(m[...], up_w[units, :])
        gate_out[:, 256 * n : 256 * (n + 1)] = gate.astype(BF16)
        up_out[:, 256 * n : 256 * (n + 1)] = up.astype(BF16)
        hidden = (gelu_parts(gate)[0] * up).astype(BF16)
        part = dot(hidden, down_w[units, :])
        if n == 0:
            acc[...] = part
        else:
            acc[...] += part
    f0[...] = acc[pl.ds(0, TOK), :]
    for j, out in enumerate((f1, f2, f3)):
        out[...] = acc[pl.ds(TOK * (j + 1), TOK), :].astype(BF16)


def ffn_back_kernel(
    e0, e1, e2, e3, gate_in, up_in, gate_w, up_w, down_w, f0, f1, f2, f3, hidden_out, gate_out, up_out, e, acc
):
    for j, part in enumerate((e0, e1, e2, e3)):
        e[pl.ds(TOK * j, TOK), :] = part[...]
    for n in range(HID // 256):
        units = pl.ds(256 * n, 256)
        cols = slice(256 * n, 256 * (n + 1))
        d_hidden = dot_right(e[...], down_w[units, :])
        active, slope = gelu_parts(gate_in[:, cols].astype(F32))
        up = up_in[:, cols].astype(F32)
        hidden_out[:, cols] = (active * up).astype(BF16)
        d_gate = (d_hidden * up * slope).astype(BF16)
        d_up = (d_hidden * active).astype(BF16)
        gate_out[:, cols] = d_gate
        up_out[:, cols] = d_up
        part = dot(d_gate, gate_w[units, :]) + dot(d_up, up_w[units, :])
        if n == 0:
            acc[...] = part
        else:
            acc[...] += part
    f0[...] = acc[pl.ds(0, TOK), :]
    for j, out in enumerate((f1, f2, f3)):
        out[...] = acc[pl.ds(TOK * (j + 1), TOK), :].astype(BF16)


def ffn_weight_kernel(
    place, m0, m1, m2, m3, e0, e1, e2, e3, hidden, d_gate, d_up, down_w, down_scale, out, scale_out, m, e
):
    for j, (a, b) in enumerate(zip((m0, m1, m2, m3), (e0, e1, e2, e3))):
        m[pl.ds(TOK * j, TOK), :] = a[...]
        e[pl.ds(TOK * j, TOK), :] = b[...]
    empty = SIDE * TOK - 3 * HALF_UNITS
    out[pl.ds(2 * SIDE - 2, 2), :, pl.ds(TOK - empty, empty), :] = jnp.zeros((2, SIDE, empty, WIDTH), BF16)
    per_unit = 1.0 / down_scale[...]
    scale_grad = jnp.zeros((1, WIDTH), F32)
    for which, (left, right) in enumerate(((d_gate, m), (d_up, m), (hidden, e))):
        runs = weight_runs(which)
        for n in range(HID // 256):
            first = 256 * n
            part = dot_left(left[:, first : first + 256], right[...])
            if which == 2:
                level = down_w[pl.ds(first, 256), :].astype(F32) * per_unit
                level = jnp.floor(level * (1.0 / 64.0)) * 64.0 + 32.0
                scale_grad += jnp.sum(part * level, axis=0, keepdims=True)
            part = part.astype(BF16)
            for piece in range(2 * SIDE):
                core = place[KV] if piece < SIDE else 1 - place[KV]
                for quarter, row, unit, count in runs:
                    low = max(piece * HALF_UNITS + unit, first)
                    high = min(piece * HALF_UNITS + unit + count, first + 256)
                    if low < high:
                        at = row + low - piece * HALF_UNITS - unit
                        out[2 * quarter + core, piece % SIDE, pl.ds(at, high - low), :] = part[low - first : high - first]
    scale_out[...] = scale_grad


def finish_kernel(
    place, own, other, gate, up, gate_scale, up_scale, down_scale, g_gate, g_up, g_down, s_gate, s_up, sums, parts
):
    for k in range(SIDE):
        quarter = (place[DP] - k) & 3
        parts[2 * quarter + place[KV]] = own[pl.ds(TOK * k, TOK), :]
        parts[2 * quarter + 1 - place[KV]] = other[pl.ds(TOK * k, TOK), :]
    sums[...] = jnp.zeros_like(sums)
    for core in range(2):
        for which in range(3):
            for quarter, row, unit, count in weight_runs(which):
                first = core * HALF_UNITS + unit
                count = min(count, UNITS - first)
                rows = pl.ds(first, count)
                total = parts[2 * quarter + core, pl.ds(row, count), :].astype(F32)
                if which == 0:
                    g_gate[rows, :] = total * gate_scale[rows, :]
                    part = jnp.sum(total * gate[rows, :].astype(F32), axis=1, keepdims=True)
                    sums[0, rows, :] = jnp.broadcast_to(part, (count, 128))
                elif which == 1:
                    g_up[rows, :] = total * up_scale[rows, :]
                    part = jnp.sum(total * ((up[rows, :] & -16) + 8).astype(F32), axis=1, keepdims=True)
                    sums[1, rows, :] = jnp.broadcast_to(part, (count, 128))
                else:
                    g_down[rows, :] = total * down_scale[...]
    s_gate[...] = jnp.transpose(sums[0])[:1, :UNITS]
    s_up[...] = jnp.transpose(sums[1])[:1, :UNITS]


def shards(
    layer_input, cotangent, doc_bounds, w_query, key_weight, value_weight, w_out,
    gain_attn_in, gain_attn_out, gain_ffn_in, gain_ffn_out,
    code_gate, code_up, code_down, scale_gate, scale_up, scale_down,
):
    ctx, kv, dp = lax.axis_index("ctx"), lax.axis_index("kv"), lax.axis_index("dp")
    place = jnp.concatenate([jnp.stack([ctx, dp, kv]).astype(jnp.int32), doc_bounds[0]])
    x = layer_input.reshape(TOK, WIDTH)
    cot = cotangent.reshape(TOK, WIDTH)
    gain_1, gain_2, gain_3, gain_4 = (
        g.reshape(1, WIDTH) for g in (gain_attn_in, gain_attn_out, gain_ffn_in, gain_ffn_out)
    )
    gate_col, up_col, down_row = scale_gate[:, None], scale_up[:, None], scale_down[None, :]
    rows_f32, rows_bf16, row_f32 = ((TOK, WIDTH), F32), ((TOK, WIDTH), BF16), ((1, WIDTH), F32)

    shard = jnp.concatenate([w_query.T, key_weight.T, value_weight.T, w_out.T], axis=0)
    rows = all_to_all(jnp.broadcast_to(shard[None], (BLOCKS, 16, WIDTH)))
    x_other = from_core(x)

    (quarter,) = kernel_call(
        dequantise_kernel,
        "shhhvvv",
        "v",
        [rows_bf16],
        "dequantise",
        (place, code_gate.T, code_up.T, code_down, gate_col, up_col, down_row),
        [pltpu.VMEM((TOK, WIDTH), jnp.int32), pltpu.SemaphoreType.DMA((2,))],
        vmem=58,
    )
    quarter, rows = lax.optimization_barrier((quarter, rows))
    quarters = ring(back_y, quarter)
    qkv_rows = jnp.concatenate([rows[:, :8].reshape(128, WIDTH), rows[:, 8]], axis=0)
    out_rows = rows[:, 8:].reshape(128, WIDTH)
    qkv_rows = [group_round(qkv_rows, i) for i in range(4)]

    quarters, qkv_rows = lax.optimization_barrier((quarters, qkv_rows))
    ffn_w = lax.all_gather(jnp.stack(quarters), ("dp", "kv"))

    keys, w_kv = kernel_call(
        kv_kernel,
        "sffvvvvv",
        "ff",
        [((BLOCKS, SPAN, 128), BF16), ((128, WIDTH), BF16)],
        "keys",
        (place, x, x_other, gain_1, *qkv_rows),
        us=4,
        vmem=20,
    )
    out_rows, after = lax.optimization_barrier((out_rows, w_kv))
    out_rows = [group_round(out_rows, i) for i in range(4)]
    keys = all_to_all(keys)
    q, w_q = kernel_call(
        query_kernel,
        "sffvffffh",
        "ff",
        [((SPAN, QCOL), BF16), ((QCOL, WIDTH), BF16)],
        "queries",
        (place, x, x_other, gain_1, *qkv_rows, after),
        us=4,
        vmem=58,
    )
    o, inv = kernel_call(
        attend_kernel,
        "sfv",
        "ff",
        [((SPAN, QCOL), BF16), ((SPAN, 128), F32)],
        "attend",
        (place, q, keys),
        [
            pltpu.VMEM((GROUP, SPAN, 128), BF16),
            pltpu.VMEM((GROUP, SPAN, 128), F32),
            pltpu.VMEM((SPAN, SPAN), jnp.int32),
            pltpu.VMEM((SPAN, SPAN), jnp.int32),
        ],
        us=16,
        vmem=24,
    )
    attn_own, attn_other = kernel_call(
        attn_project_kernel,
        "sfffff",
        "vv",
        [rows_f32, rows_bf16],
        "attn_project",
        (place, *out_rows, o),
        vmem=16,
    )
    attn_other = from_core(attn_other)
    attn, resid, m_own = kernel_call(
        attn_norm_kernel,
        "vvvvv",
        "vvv",
        [rows_f32, rows_f32, rows_bf16],
        "attn_norm",
        (x, attn_own, attn_other, gain_2, gain_3),
    )

    m_parts = ring(back_z, m_own)
    m_parts[1], ffn_w = lax.optimization_barrier((m_parts[1], ffn_w))
    wide = ((SIDE * TOK, HID), BF16)
    unit_rows = ((2 * SIDE, HALF_UNITS, WIDTH), BF16)
    ffn_w = kernel_call(
        arrange_kernel,
        "sh",
        "vvv",
        [unit_rows] * 3,
        "arrange",
        (place, ffn_w),
        [pltpu.SemaphoreType.DMA((12,))],
        us=4,
    )
    gate_w, up_w, down_w = (w.reshape(HID, WIDTH) for w in ffn_w)
    ffn_scratch = [pltpu.VMEM((SIDE * TOK, WIDTH), BF16), pltpu.VMEM((SIDE * TOK, WIDTH), F32)]
    *fo_parts, gate, up = kernel_call(
        ffn_kernel,
        "vvvvvvv",
        "vvvvvv",
        [rows_f32] + [rows_bf16] * 3 + [wide, wide],
        "ffn",
        (*m_parts, gate_w, up_w, down_w),
        ffn_scratch,
        us=6,
        vmem=16,
    )
    fo_parts = ring_back(back_z, fo_parts)
    block_out, d_fo, g_gain_4 = kernel_call(
        ffn_norm_kernel, "vvvvvvv", "vvv", [rows_bf16, rows_bf16, row_f32], "ffn_norm", (*fo_parts, resid, cot, gain_4)
    )

    d_parts = ring(back_z, d_fo)
    *dm_parts, hidden, d_gate, d_up = kernel_call(
        ffn_back_kernel,
        "vvvvvvvvv",
        "vvvvvvv",
        [rows_f32] + [rows_bf16] * 3 + [wide] * 3,
        "ffn_back",
        (*d_parts, gate, up, gate_w, up_w, down_w),
        ffn_scratch,
        us=10,
        vmem=20,
    )
    dm_parts = ring_back(back_z, dm_parts)
    weight_grads, g_down = kernel_call(
        ffn_weight_kernel,
        "s" + "v" * 13,
        "fv",
        [((2 * SIDE, SIDE, TOK, WIDTH), BF16), row_f32],
        "ffn_weight",
        (place, *m_parts, *d_parts, hidden, d_gate, d_up, down_w, down_row),
        [
            pltpu.VMEM((SIDE * TOK, WIDTH), BF16),
            pltpu.VMEM((SIDE * TOK, WIDTH), BF16),
        ],
        us=8,
        vmem=20,
    )
    dm_parts, weight_grads = lax.optimization_barrier((dm_parts, weight_grads))
    weight_grads = lax.psum_scatter(weight_grads, ("dp", "kv"), scatter_dimension=0)
    d_resid, d_attn, g_gain_3, g_gain_2 = kernel_call(
        ffn_back_norm_kernel,
        "vvvvvvvvv",
        "vvvv",
        [rows_f32, rows_bf16, row_f32, row_f32],
        "ffn_back_norm",
        (*dm_parts, resid, attn, cot, gain_3, gain_2),
    )
    d_attn_other = from_core(d_attn)

    dq, key_grads = kernel_call(
        attend_back_kernel,
        "sffffffffff",
        "ff",
        [((SPAN, QCOL), BF16), ((BLOCKS, 128, SPAN), BF16)],
        "attend_back",
        (place, d_attn, d_attn_other, *out_rows, q, o, inv, keys),
        [
            pltpu.VMEM((GROUP, SPAN, 128), BF16),
            pltpu.VMEM((GROUP, SPAN, 128), F32),
            pltpu.VMEM((GROUP, SPAN, 128), BF16),
            pltpu.VMEM((128, GROUP * SPAN), BF16),
            pltpu.VMEM((SPAN, SPAN), jnp.int32),
            pltpu.VMEM((SPAN, SPAN), jnp.int32),
        ],
        us=26,
        vmem=58,
    )
    key_grads = all_to_all(key_grads)
    q_grads, after = kernel_call(
        query_grad_kernel,
        "sffffffv",
        "fv",
        [((WIDTH, WIDTH), BF16), ((8, 128), F32)],
        "query_grad",
        (place, dq, o, x, x_other, d_attn, d_attn_other, gain_1),
        [pltpu.VMEM((2 * SPAN, WIDTH), BF16)],
        us=5,
        vmem=58,
    )

    def total(parts):
        a, b, c, d = (p.astype(F32) for p in parts)
        return (a + b) + (c + d)

    q_grads = lax.psum_scatter(q_grads.reshape(SIDE, 224, WIDTH), "dp", scatter_dimension=0)
    da_own, da_other, kv_grads, gains = kernel_call(
        project_back_kernel,
        "sffffffvvvvvv",
        "vvvv",
        [rows_f32, rows_bf16, ((128, WIDTH), BF16), ((8, WIDTH), F32)],
        "project_back",
        (place, key_grads, dq, w_q, w_kv, x, x_other, gain_1, g_gain_2, g_gain_3, g_gain_4, g_down, after),
        us=4,
        vmem=58,
    )
    weight_grads, da_other = lax.optimization_barrier((weight_grads, da_other))
    weight_grads = weight_grads.reshape(SIDE, TOK, WIDTH)
    eighth = total(ring_back(back_y, [weight_grads[k] for k in range(SIDE)])).astype(BF16)
    eighths = jnp.concatenate(ring(back_x, eighth), axis=0)

    (grad_input,) = kernel_call(
        input_norm_kernel, "vvvvv", "v", [rows_f32], "input_norm", (da_own, from_core(da_other), x, d_resid, gain_1)
    )

    gains = (gains + from_core(gains)).astype(BF16)
    kv_grads = [jnp.concatenate([kv_grads[32 * k : 32 * (k + 1)], gains], axis=0) for k in range(SIDE)]
    kv_grads = total(ring_back(back_x, kv_grads)).astype(BF16)
    gains = jnp.broadcast_to(kv_grads[None, 32:], (BLOCKS, 8, WIDTH))
    w_grads = [q_grads.reshape(BLOCKS, 14, WIDTH), kv_grads[:32].reshape(BLOCKS, 2, WIDTH), gains]
    w_grads = all_to_all(jnp.concatenate(w_grads, axis=1))
    w_grads, grad_input = lax.optimization_barrier((w_grads, grad_input))
    w_grads = jnp.sum(w_grads.astype(F32), axis=0)
    gains = w_grads[16:]
    pairs = [(2 * n + k, 2 * (2 * k + n // 2) + n % 2) for n in range(SIDE) for k in range(2)]
    grad_w = lax.ppermute(w_grads[:16], ("dp", "kv"), pairs)

    grad_code_gate, grad_code_up, grad_code_down, grad_scale_gate, grad_scale_up = kernel_call(
        finish_kernel,
        "svvvvvvv",
        "vvvvv",
        [((UNITS, WIDTH), F32)] * 3 + [((1, UNITS), F32)] * 2,
        "finish",
        (place, eighths, from_core(eighths), code_gate.T, code_up.T, gate_col, up_col, down_row),
        [pltpu.VMEM((2, 384, 128), F32), pltpu.VMEM((2 * SIDE, TOK, WIDTH), BF16)],
        us=3,
    )
    grads = (grad_code_gate, grad_code_up, grad_code_down, grad_scale_gate[0], grad_scale_up[0])

    return (
        block_out.reshape(layer_input.shape),
        grad_input.reshape(layer_input.shape),
        grad_w[:7].T,
        grad_w[14:15].T,
        grad_w[15:16].T,
        grad_w[7:14].T,
        gains[0],
        gains[1],
        gains[2],
        gains[3],
        grads[0].T,
        grads[1].T,
        *grads[2:],
        gains[4],
    )


def solution(mesh):
    tokens = P("dp", "ctx", "kv", None, None)
    columns = P(None, ("dp", "kv", "ctx"))
    hidden = (P(None, "ctx"), P(None, "ctx"), P("ctx", None), P("ctx"), P("ctx"), P())
    return jax.shard_map(
        shards,
        mesh=mesh,
        in_specs=(tokens, tokens, P("dp", None)) + (columns,) * 4 + (P(),) * 4 + hidden,
        out_specs=(tokens, tokens) + (columns,) * 4 + (P(),) * 4 + hidden,
        check_vma=False,
    )
```

```python
import math

import jax
import jax.numpy as jnp
from jax import lax
from jax.experimental import pallas as pl
from jax.experimental.pallas import tpu as pltpu
from jax.sharding import PartitionSpec as P

EPS = 1e-06
CAP = 50.0
QSCALE = 0.125
GELU_C = math.sqrt(2.0 / math.pi)
EXP2 = CAP * math.log2(math.e)

TOK = 128
SPAN = 256
WIDTH = 896
HEAD = 64
GROUP = 7
QCOL = 512
SIDE = 4
UNITS = 304
UPAD = 320
HALF_UNITS = 160
HID = 1280
HALF_ROWS = 512
BLOCKS = 16
F32 = jnp.float32
BF16 = jnp.bfloat16
VMEM = pl.BlockSpec(memory_space=pltpu.VMEM)
SMEM = pl.BlockSpec(memory_space=pltpu.SMEM)
HBM = pl.BlockSpec(memory_space=pltpu.HBM)


class Fetched:
    def __init__(self, copy, buffer):
        self.copy, self.buffer = copy, buffer

    def __call__(self):
        if self.copy is not None:
            self.copy.wait()
            self.copy = None
        return self.buffer


def kernel_call(body, ins, outs, out, name, args, scratch=(), us=2.0, vmem=16):
    fetched = [i for i, kind in enumerate(ins) if kind == "f"]
    stored = [i for i, kind in enumerate(outs) if kind == "f"]
    count = len(fetched) + len(stored)

    def whole(*refs):
        if not count:
            return body(*refs)
        sems, buffers = refs[-1], refs[len(refs) - 1 - count : -1]
        refs = list(refs[: len(refs) - 1 - count])
        copies = [pltpu.make_async_copy(refs[i], buffers[n], sems.at[n]) for n, i in enumerate(fetched)]
        for c in copies:
            c.start()
        for n, i in enumerate(fetched):
            refs[i] = Fetched(copies[n], buffers[n])
        back = []
        for n, i in enumerate(stored, len(fetched)):
            back.append(pltpu.make_async_copy(buffers[n], refs[len(ins) + i], sems.at[n]))
            refs[len(ins) + i] = buffers[n]
        body(*refs)
        for c in back:
            c.start()
        for c in back:
            c.wait()

    scratch = list(scratch)
    if count:
        scratch += [pltpu.VMEM(args[i].shape, args[i].dtype) for i in fetched]
        scratch += [pltpu.VMEM(*out[i]) for i in stored]
        scratch.append(pltpu.SemaphoreType.DMA((count,)))
    spec = {"s": SMEM, "v": VMEM, "h": HBM, "f": HBM}
    return pl.pallas_call(
        whole,
        out_shape=[jax.ShapeDtypeStruct(shape, dtype) for shape, dtype in out],
        in_specs=[spec[kind] for kind in ins],
        out_specs=[spec[kind] for kind in outs],
        scratch_shapes=scratch,
        compiler_params=pltpu.CompilerParams(vmem_limit_bytes=vmem * 1024 * 1024),
        cost_estimate=pl.CostEstimate(flops=int(us * 1e9), bytes_accessed=0, transcendentals=0),
        name=name,
    )(*args)


def dot(left, right):
    return lax.dot_general(left, right, (((1,), (0,)), ((), ())), preferred_element_type=F32)


def dot_right(left, right):
    return lax.dot_general(left, right, (((1,), (1,)), ((), ())), preferred_element_type=F32)


def dot_left(left, right):
    return lax.dot_general(left, right, (((0,), (0,)), ((), ())), preferred_element_type=F32)


def from_core(x):
    return lax.ppermute(x, "kv", [(0, 1), (1, 0)])


def back_x(x, k):
    return lax.ppermute(x, "dp", [(i, (i + k) % SIDE) for i in range(SIDE)])


def back_y(x, k):
    pairs = [(z * SIDE + y, z * SIDE + (y + k) % SIDE) for z in range(SIDE) for y in range(SIDE)]
    return lax.ppermute(x, "ctx", pairs)


def back_z(x, k):
    pairs = [(z * SIDE + y, (z + k) % SIDE * SIDE + y) for z in range(SIDE) for y in range(SIDE)]
    return lax.ppermute(x, "ctx", pairs)


def group_round(x, i, back=False):
    pairs = [(n, 2 * ((n % 4 + i) % SIDE) + n // 4) for n in range(8)]
    if back:
        pairs = [(b, a) for a, b in pairs]
    return lax.ppermute(x, ("dp", "kv"), pairs)


def all_to_all(x):
    return lax.all_to_all(x, "ctx", split_axis=0, concat_axis=0, tiled=True)


def ring(send, x):
    got = {k: send(x, k) for k in (1, 3, 2)}
    return [x, got[1], got[2], got[3]]


def ring_back(send, parts):
    got = {k: send(parts[k], SIDE - k) for k in (1, 3, 2)}
    return [parts[0], got[1], got[2], got[3]]


def norm_rows(rows, gain):
    inverse = lax.rsqrt(jnp.mean(rows * rows, axis=-1, keepdims=True) + EPS)
    return rows * inverse * gain, inverse


def norm_back(rows, gain, incoming):
    inverse = lax.rsqrt(jnp.mean(rows * rows, axis=-1, keepdims=True) + EPS)
    normed = rows * inverse
    scaled = incoming * gain
    grad = inverse * (scaled - normed * jnp.mean(scaled * normed, axis=-1, keepdims=True))
    return grad, jnp.sum(incoming * normed, axis=0, keepdims=True)


def lane(shape):
    return lax.broadcasted_iota(jnp.int32, shape, len(shape) - 1)


def swap_halves(x):
    return jnp.where(lane(x.shape) % HEAD < HEAD // 2, pltpu.roll(x, 96, 1), pltpu.roll(x, 32, 1))


CTX, DP, KV, STARTS = 0, 1, 2, 3


def doc_start(place, p):
    start = jnp.zeros_like(p)
    for i in range(8):
        b = place[STARTS + i]
        start = jnp.where(p >= b, jnp.maximum(start, b), start)
    return start


def span_places(shape, dim, chip, kv):
    i = lax.broadcasted_iota(jnp.int32, shape, dim)
    half = jnp.where(i < TOK, kv, 1 - kv)
    return chip * SPAN + half * TOK + i % TOK


def rotary(place):
    spot = span_places((SPAN, 128), 0, place[CTX], place[KV])
    index = lane((SPAN, 128)) % HEAD
    freq = jnp.exp((index % (HEAD // 2)).astype(F32) * (-2.0 * math.log(10000.0) / HEAD))
    angle = (spot - doc_start(place, spot)).astype(F32) * freq
    return jnp.cos(angle), jnp.where(index < HEAD // 2, -1.0, 1.0) * jnp.sin(angle)


def one_hot(target, first, count):
    rows = lax.broadcasted_iota(jnp.int32, (count, target.shape[1]), 0) + first
    return jnp.where(rows == target, 1.0, 0.0).astype(BF16)


def owner_column(place, ctx, turn):
    return ((place[DP] - turn) & 3) * 16 + ctx


def qkv_target(place):
    row = lane((1, 576))
    turn, inner = row // 144, row % 144
    value = inner >= 128
    col = owner_column(place, jnp.where(value, inner - 128, inner // 8), turn)
    target = jnp.where(inner % 8 < 7, 7 * col + inner % 8, QCOL + col)
    return jnp.where(value, QCOL + HEAD + col, target)


def out_order(place):
    row = lane((1, QCOL))
    kind = row % 8 - 1
    target = 7 * owner_column(place, row // 8 % 16, row // 128) + kind
    return one_hot(jnp.where(kind >= 0, target, -1), 0, QCOL)


def normed_input(x0, x1, gain):
    rows = jnp.concatenate([x0()[...], x1()[...]], axis=0).astype(F32)
    return norm_rows(rows, gain)[0]


def kv_kernel(place, x0, x1, gain, w0, w1, w2, w3, kv_out, w_out):
    cos, sin = rotary(place)
    order = one_hot(qkv_target(place), QCOL, 128)
    rows = normed_input(x0, x1, gain[...]).astype(BF16)
    w_cols = dot(order, jnp.concatenate([w0[...], w1[...], w2[...], w3[...]], axis=0)).astype(BF16)
    w_out[...] = w_cols
    u = dot_right(rows, w_cols)
    kv = jnp.where(lane((SPAN, 128)) < HEAD, u * cos + swap_halves(u) * sin, u).astype(BF16)
    for j in range(BLOCKS):
        kv_out[j] = kv


def query_kernel(place, x0, x1, gain, w0, w1, w2, w3, after, q_out, w_out):
    cos, sin = rotary(place)
    order = one_hot(qkv_target(place), 0, QCOL)
    rows = normed_input(x0, x1, gain[...]).astype(BF16)
    w_cols = dot(order, jnp.concatenate([w0()[...], w1()[...], w2()[...], w3()[...]], axis=0)).astype(BF16)
    w_out[...] = w_cols
    raw = dot_right(rows, w_cols)
    for j in range(4):
        u = raw[:, 128 * j : 128 * (j + 1)]
        q_out[:, 128 * j : 128 * (j + 1)] = ((u * cos + swap_halves(u) * sin) * QSCALE).astype(BF16)


def spread_heads(q, out):
    low = lane((SPAN, 128)) < HEAD
    for j in range(4):
        u = q[:, 128 * j : 128 * (j + 1)].astype(F32)
        out[2 * j] = jnp.where(low, u, 0.0).astype(BF16)
        if j < 3:
            out[2 * j + 1] = jnp.where(low, pltpu.roll(u, HEAD, 1), 0.0).astype(BF16)


def attn_project_kernel(place, w0, w1, w2, w3, o, own_out, other_out):
    rows = jnp.concatenate([w0()[...], w1()[...], w2()[...], w3()[...]], axis=0)
    attn = dot(dot(o()[...], out_order(place)).astype(BF16), rows)
    own_out[...] = attn[:TOK]
    other_out[...] = attn[TOK:].astype(BF16)


def block_ranges(place, n):
    first = place[CTX] * SPAN
    low_start, high_start = doc_start(place, first), doc_start(place, first + SPAN - 1)
    active = (n <= place[CTX]) & (n * SPAN + SPAN - 1 >= low_start)
    full = (n < place[CTX]) & (n * SPAN >= high_start)
    return active, full


def query_places(place, pos_ref, start_ref):
    pos = span_places((SPAN, SPAN), 0, place[CTX], place[KV])
    pos_ref[...] = pos
    start_ref[...] = doc_start(place, pos)


def allowed_keys(place, source, pos_ref, start_ref):
    keys = span_places((SPAN, SPAN), 1, source, place[KV])
    return (keys <= pos_ref[...]) & (keys >= start_ref[...])


def attend_kernel(place, q_cols, blocks, o_out, inv_out, q, acc, pos_ref, start_ref):
    query_places(place, pos_ref, start_ref)
    acc[...] = jnp.zeros_like(acc)
    spread_heads(q_cols(), q)
    low = lane((SPAN, 128)) < HEAD

    @pl.loop(0, BLOCKS)
    def _(n):
        active, full = block_ranges(place, n)

        def step(masked):
            kv = blocks[n]
            ones_v = jnp.where(low, jnp.ones_like(kv), kv)
            if masked:
                allowed = allowed_keys(place, n, pos_ref, start_ref)
            s = dot_right(q[...].reshape(GROUP * SPAN, 128), kv)
            p = jnp.exp2(jnp.tanh(s * (1.0 / CAP)) * EXP2)
            if masked:
                p = jnp.where(allowed[None], p.reshape(GROUP, SPAN, SPAN), 0.0).reshape(GROUP * SPAN, SPAN)
            acc[...] += dot(p.astype(BF16), ones_v).reshape(GROUP, SPAN, 128)

        pl.when(full)(lambda: step(False))
        pl.when(active & jnp.logical_not(full))(lambda: step(True))

    lanes = lane((SPAN, 128))
    inverse = jnp.ones((SPAN, 128), F32)
    for j in range(4):
        a = acc[2 * j]
        if j < 3:
            b = acc[2 * j + 1]
            total = jnp.where(low, a, pltpu.roll(b, HEAD, 1))
            value = jnp.where(low, pltpu.roll(a, HEAD, 1), b)
            inverse = jnp.where(lanes == 2 * j + 1, 1.0 / b, inverse)
        else:
            total = jnp.where(low, a, 1.0)
            value = jnp.where(low, pltpu.roll(a, HEAD, 1), 0.0)
        inverse = jnp.where(lanes == 2 * j, 1.0 / a, inverse)
        o_out[:, 128 * j : 128 * (j + 1)] = (value / total).astype(BF16)
    inv_out[...] = inverse


def attend_back_kernel(
    place, d0, d1, w0, w1, w2, w3, q_cols, o, inv, blocks,
    dq_out, grads, q, dq, do_ext, both_t, pos_ref, start_ref,
):
    query_places(place, pos_ref, start_ref)
    dq[...] = jnp.zeros_like(dq)
    rows = jnp.concatenate([d0()[...], d1()[...]], axis=0)
    w = jnp.concatenate([w0()[...], w1()[...], w2()[...], w3()[...]], axis=0)
    d_o = dot_right(dot_right(rows, w).astype(BF16), out_order(place))
    low = lane((SPAN, 128)) < HEAD
    lanes = lane((SPAN, 128))
    spread_heads(q_cols(), q)
    o, inv = o(), inv()
    for h in range(GROUP):
        j = h // 2
        cols = slice(128 * j, 128 * (j + 1))
        mine = low if h % 2 == 0 else jnp.logical_not(low)
        scale = inv[:, h : h + 1]
        up = d_o[:, cols] * scale
        delta = jnp.sum(jnp.where(mine, up * o[:, cols].astype(F32), 0.0), axis=1, keepdims=True)
        if h % 2 == 0:
            up = pltpu.roll(up, HEAD, 1)
        high = delta.astype(BF16).astype(F32)
        ext = jnp.where(lanes == 0, -high, jnp.where(lanes == 1, high - delta, jnp.where(low, 0.0, up)))
        do_ext[h] = ext.astype(BF16)
        both_t[:, SPAN * h : SPAN * (h + 1)] = jnp.transpose(jnp.where(low, q[h].astype(F32), up)).astype(BF16)
    blocks = blocks()

    @pl.loop(0, BLOCKS)
    def _(n):
        active, full = block_ranges(place, n)

        def step(masked):
            kv = blocks[n]
            ones_v = jnp.where(low, jnp.ones_like(kv), kv)
            if masked:
                allowed = allowed_keys(place, n, pos_ref, start_ref)
            s = dot_right(q[...].reshape(GROUP * SPAN, 128), kv)
            dp = dot_right(do_ext[...].reshape(GROUP * SPAN, 128), ones_v)
            t = jnp.tanh(s * (1.0 / CAP))
            p = jnp.exp2(t * EXP2)
            if masked:
                p = jnp.where(allowed[None], p.reshape(GROUP, SPAN, SPAN), 0.0).reshape(GROUP * SPAN, SPAN)
            ds = (p * dp * (1.0 - t * t)).astype(BF16)
            dq[...] += dot(ds, kv).reshape(GROUP, SPAN, 128)
            dk = dot(both_t[pl.ds(0, HEAD), :], ds)
            dv = dot(both_t[pl.ds(HEAD, HEAD), :], p.astype(BF16))
            grads[n] = jnp.concatenate([dk, dv], axis=0).astype(BF16)

        pl.when(full)(lambda: step(False))
        pl.when(active & jnp.logical_not(full))(lambda: step(True))

        @pl.when(jnp.logical_not(active))
        def _():
            grads[n] = jnp.zeros((128, SPAN), BF16)

    cos, sin = rotary(place)
    for j in range(4):
        u = dq[2 * j]
        if j < 3:
            u = jnp.where(low, u, pltpu.roll(dq[2 * j + 1], HEAD, 1))
        else:
            u = jnp.where(low, u, 0.0)
        u = u * QSCALE
        dq_out[:, 128 * j : 128 * (j + 1)] = (u * cos - swap_halves(u) * sin).astype(BF16)


def query_grad_kernel(place, dq, o, x0, x1, d0, d1, gain, w_grad, after, left):
    row = lane((1, WIDTH))
    kind = row % 14
    target = 7 * (row // 14) + kind % 7
    after[...] = jnp.zeros_like(after)
    left[pl.ds(0, SPAN), :] = dot(dq()[...], one_hot(jnp.where(kind < 7, target, -1), 0, QCOL)).astype(BF16)
    left[pl.ds(SPAN, SPAN), :] = dot(o()[...], one_hot(jnp.where(kind < 7, -1, target), 0, QCOL)).astype(BF16)
    rows = normed_input(x0, x1, gain[...]).astype(BF16)
    right = jnp.concatenate([rows, d0()[...], d1()[...]], axis=0)
    w_grad[...] = dot_left(left[...], right).astype(BF16)


def project_back_kernel(
    place, dkv_parts, dq, w_q, w_kv, x0, x1, gain, g2, g3, g4, g5, after,
    own_out, other_out, w_grad, gains_out,
):
    cos, sin = rotary(place)
    row = lane((1, 128))
    order = one_hot(row % 2 * HEAD + owner_column(place, row // 2 % 16, row // 32), 0, 128)
    normed = normed_input(x0, x1, 1.0)
    d_a = dot(dq()[...], w_q()[...])
    dkv_parts = dkv_parts()
    dkv = dkv_parts[0].astype(F32)
    for j in range(1, BLOCKS):
        dkv += dkv_parts[j].astype(F32)
    u = jnp.transpose(dkv)
    dkv = jnp.where(lane((SPAN, 128)) < HEAD, u * cos - swap_halves(u) * sin, u).astype(BF16)
    d_a += dot(dkv, w_kv()[...])
    own_out[...] = d_a[:TOK]
    other_out[...] = d_a[TOK:].astype(BF16)
    g1 = jnp.sum(normed * d_a, axis=0, keepdims=True)
    gains_out[...] = jnp.concatenate([g1, g2[...], g3[...], g4[...], g5[...], jnp.zeros((3, WIDTH), F32)], axis=0)
    w_grad[...] = dot_left(dot(dkv, order).astype(BF16), (normed * gain[...]).astype(BF16)).astype(BF16)


def attn_norm_kernel(x, own, other, gain_b, gain_c, attn_out, r_out, m_out):
    attn = own[...] + other[...].astype(F32)
    attn_out[...] = attn
    resid = x[...].astype(F32) + norm_rows(attn, gain_b[...])[0]
    r_out[...] = resid
    m_out[...] = norm_rows(resid, gain_c[...])[0].astype(BF16)


def sum_parts(own, b, c, d):
    return (own[...] + b[...].astype(F32)) + (c[...].astype(F32) + d[...].astype(F32))


def ffn_norm_kernel(own, b, c, d, resid, cotangent, gain, out, d_out, gain_out):
    fo = sum_parts(own, b, c, d)
    out[...] = (resid[...] + norm_rows(fo, gain[...])[0]).astype(BF16)
    grad, gain_grad = norm_back(fo, gain[...], cotangent[...].astype(F32))
    d_out[...] = grad.astype(BF16)
    gain_out[...] = gain_grad


def ffn_back_norm_kernel(own, b, c, d, resid, attn, cotangent, gain_c, gain_b, r_out, d_out, gain_c_out, gain_b_out):
    d_m = sum_parts(own, b, c, d)
    grad, gain_grad = norm_back(resid[...], gain_c[...], d_m)
    gain_c_out[...] = gain_grad
    d_resid = cotangent[...].astype(F32) + grad
    r_out[...] = d_resid
    grad, gain_grad = norm_back(attn[...], gain_b[...], d_resid)
    gain_b_out[...] = gain_grad
    d_out[...] = grad.astype(BF16)


def input_norm_kernel(own, other, x, d_resid, gain, out):
    d_a = own[...] + other[...].astype(F32)
    out[...] = d_resid[...] + norm_back(x[...].astype(F32), gain[...], d_a)[0]


def gelu_parts(u):
    t = jnp.tanh(GELU_C * (u + 0.044715 * u * u * u))
    active = 0.5 * u * (1.0 + t)
    slope = 0.5 * (1.0 + t) + 0.5 * u * (1.0 - t * t) * GELU_C * (1.0 + 3.0 * 0.044715 * u * u)
    return active, slope


def weight_runs(which):
    runs, at = [], which * HALF_UNITS
    while at < (which + 1) * HALF_UNITS:
        count = min(TOK - at % TOK, (which + 1) * HALF_UNITS - at)
        runs.append((at // TOK, at % TOK, at - which * HALF_UNITS, count))
        at += count
    return runs


def arrange_kernel(place, pieces, gate, up, down, sems):
    copies = []
    for which, dest in enumerate((gate, up, down)):
        for core in range(2):
            source = place[KV] if core == 0 else 1 - place[KV]
            for quarter, row, unit, count in weight_runs(which):
                copies.append(
                    pltpu.make_async_copy(
                        pieces.at[2 * quarter + source, :, pl.ds(row, count), :],
                        dest.at[pl.ds(core * SIDE, SIDE), pl.ds(unit, count), :],
                        sems.at[len(copies)],
                    )
                )
    for c in copies:
        c.start()
    for c in copies:
        c.wait()


def dequantise_kernel(place, gate, up, down, gate_scale, up_scale, down_scale, out, codes, sems):
    out[...] = jnp.zeros((TOK, WIDTH), BF16)

    def fill(core, quarter):
        runs = []
        for which in range(3):
            for part, row, unit, count in weight_runs(which):
                first = core * HALF_UNITS + unit
                count = min(count, UNITS - first)
                if part == quarter:
                    runs.append((which, row, first, count))
        copies = [
            pltpu.make_async_copy(
                (gate, up, down)[which].at[pl.ds(first, count), :], codes.at[pl.ds(row, count), :], sems.at[n]
            )
            for n, (which, row, first, count) in enumerate(runs)
        ]
        for c in copies:
            c.start()
        for c in copies:
            c.wait()
        for which, row, first, count in runs:
            c = codes[pl.ds(row, count), :]
            if which == 0:
                weight = c.astype(F32) * gate_scale[pl.ds(first, count), :]
            elif which == 1:
                weight = ((c & -16) + 8).astype(F32) * up_scale[pl.ds(first, count), :]
            else:
                weight = ((c & -64) + 32).astype(F32) * down_scale[...]
            out[pl.ds(row, count), :] = weight.astype(BF16)

    for core in range(2):
        for quarter in range(SIDE):
            pl.when((place[KV] == core) & (place[DP] == quarter))(lambda c=core, q=quarter: fill(c, q))


def ffn_kernel(m0, m1, m2, m3, gate_w, up_w, down_w, f0, f1, f2, f3, gate_out, up_out, m, acc):
    for j, part in enumerate((m0, m1, m2, m3)):
        m[pl.ds(TOK * j, TOK), :] = part[...]
    for n in range(HID // 256):
        units = pl.ds(256 * n, 256)
        gate = dot_right(m[...], gate_w[units, :])
        up = dot_right(m[...], up_w[units, :])
        gate_out[:, 256 * n : 256 * (n + 1)] = gate.astype(BF16)
        up_out[:, 256 * n : 256 * (n + 1)] = up.astype(BF16)
        hidden = (gelu_parts(gate)[0] * up).astype(BF16)
        part = dot(hidden, down_w[units, :])
        if n == 0:
            acc[...] = part
        else:
            acc[...] += part
    f0[...] = acc[pl.ds(0, TOK), :]
    for j, out in enumerate((f1, f2, f3)):
        out[...] = acc[pl.ds(TOK * (j + 1), TOK), :].astype(BF16)


def ffn_back_kernel(
    e0, e1, e2, e3, gate_in, up_in, gate_w, up_w, down_w, f0, f1, f2, f3, hidden_out, gate_out, up_out, e, acc
):
    for j, part in enumerate((e0, e1, e2, e3)):
        e[pl.ds(TOK * j, TOK), :] = part[...]
    for n in range(HID // 256):
        units = pl.ds(256 * n, 256)
        cols = slice(256 * n, 256 * (n + 1))
        d_hidden = dot_right(e[...], down_w[units, :])
        active, slope = gelu_parts(gate_in[:, cols].astype(F32))
        up = up_in[:, cols].astype(F32)
        hidden_out[:, cols] = (active * up).astype(BF16)
        d_gate = (d_hidden * up * slope).astype(BF16)
        d_up = (d_hidden * active).astype(BF16)
        gate_out[:, cols] = d_gate
        up_out[:, cols] = d_up
        part = dot(d_gate, gate_w[units, :]) + dot(d_up, up_w[units, :])
        if n == 0:
            acc[...] = part
        else:
            acc[...] += part
    f0[...] = acc[pl.ds(0, TOK), :]
    for j, out in enumerate((f1, f2, f3)):
        out[...] = acc[pl.ds(TOK * (j + 1), TOK), :].astype(BF16)


def ffn_weight_kernel(
    place, m0, m1, m2, m3, e0, e1, e2, e3, hidden, d_gate, d_up, down_w, down_scale, out, scale_out, m, e
):
    for j, (a, b) in enumerate(zip((m0, m1, m2, m3), (e0, e1, e2, e3))):
        m[pl.ds(TOK * j, TOK), :] = a[...]
        e[pl.ds(TOK * j, TOK), :] = b[...]
    empty = SIDE * TOK - 3 * HALF_UNITS
    out[pl.ds(2 * SIDE - 2, 2), :, pl.ds(TOK - empty, empty), :] = jnp.zeros((2, SIDE, empty, WIDTH), BF16)
    per_unit = 1.0 / down_scale[...]
    scale_grad = jnp.zeros((1, WIDTH), F32)
    for which, (left, right) in enumerate(((d_gate, m), (d_up, m), (hidden, e))):
        runs = weight_runs(which)
        for n in range(HID // 256):
            first = 256 * n
            part = dot_left(left[:, first : first + 256], right[...])
            if which == 2:
                level = down_w[pl.ds(first, 256), :].astype(F32) * per_unit
                level = jnp.floor(level * (1.0 / 64.0)) * 64.0 + 32.0
                scale_grad += jnp.sum(part * level, axis=0, keepdims=True)
            part = part.astype(BF16)
            for piece in range(2 * SIDE):
                core = place[KV] if piece < SIDE else 1 - place[KV]
                for quarter, row, unit, count in runs:
                    low = max(piece * HALF_UNITS + unit, first)
                    high = min(piece * HALF_UNITS + unit + count, first + 256)
                    if low < high:
                        at = row + low - piece * HALF_UNITS - unit
                        out[2 * quarter + core, piece % SIDE, pl.ds(at, high - low), :] = part[low - first : high - first]
    scale_out[...] = scale_grad


def finish_kernel(
    place, own, other, gate, up, gate_scale, up_scale, down_scale, g_gate, g_up, g_down, s_gate, s_up, sums, parts
):
    for k in range(SIDE):
        quarter = (place[DP] - k) & 3
        parts[2 * quarter + place[KV]] = own[pl.ds(TOK * k, TOK), :]
        parts[2 * quarter + 1 - place[KV]] = other[pl.ds(TOK * k, TOK), :]
    sums[...] = jnp.zeros_like(sums)
    for core in range(2):
        for which in range(3):
            for quarter, row, unit, count in weight_runs(which):
                first = core * HALF_UNITS + unit
                count = min(count, UNITS - first)
                rows = pl.ds(first, count)
                total = parts[2 * quarter + core, pl.ds(row, count), :].astype(F32)
                if which == 0:
                    g_gate[rows, :] = total * gate_scale[rows, :]
                    part = jnp.sum(total * gate[rows, :].astype(F32), axis=1, keepdims=True)
                    sums[0, rows, :] = jnp.broadcast_to(part, (count, 128))
                elif which == 1:
                    g_up[rows, :] = total * up_scale[rows, :]
                    part = jnp.sum(total * ((up[rows, :] & -16) + 8).astype(F32), axis=1, keepdims=True)
                    sums[1, rows, :] = jnp.broadcast_to(part, (count, 128))
                else:
                    g_down[rows, :] = total * down_scale[...]
    s_gate[...] = jnp.transpose(sums[0])[:1, :UNITS]
    s_up[...] = jnp.transpose(sums[1])[:1, :UNITS]


def shards(
    layer_input, cotangent, doc_bounds, w_query, key_weight, value_weight, w_out,
    gain_attn_in, gain_attn_out, gain_ffn_in, gain_ffn_out,
    code_gate, code_up, code_down, scale_gate, scale_up, scale_down,
):
    ctx, kv, dp = lax.axis_index("ctx"), lax.axis_index("kv"), lax.axis_index("dp")
    place = jnp.concatenate([jnp.stack([ctx, dp, kv]).astype(jnp.int32), doc_bounds[0]])
    x = layer_input.reshape(TOK, WIDTH)
    cot = cotangent.reshape(TOK, WIDTH)
    gain_1, gain_2, gain_3, gain_4 = (
        g.reshape(1, WIDTH) for g in (gain_attn_in, gain_attn_out, gain_ffn_in, gain_ffn_out)
    )
    gate_col, up_col, down_row = scale_gate[:, None], scale_up[:, None], scale_down[None, :]
    rows_f32, rows_bf16, row_f32 = ((TOK, WIDTH), F32), ((TOK, WIDTH), BF16), ((1, WIDTH), F32)

    shard = jnp.concatenate([w_query.T, key_weight.T, value_weight.T, w_out.T], axis=0)
    rows = all_to_all(jnp.broadcast_to(shard[None], (BLOCKS, 16, WIDTH)))
    x_other = from_core(x)

    (quarter,) = kernel_call(
        dequantise_kernel,
        "shhhvvv",
        "v",
        [rows_bf16],
        "dequantise",
        (place, code_gate.T, code_up.T, code_down, gate_col, up_col, down_row),
        [pltpu.VMEM((TOK, WIDTH), jnp.int32), pltpu.SemaphoreType.DMA((2,))],
        vmem=58,
    )
    quarter, rows = lax.optimization_barrier((quarter, rows))
    quarters = ring(back_y, quarter)
    qkv_rows = jnp.concatenate([rows[:, :8].reshape(128, WIDTH), rows[:, 8]], axis=0)
    out_rows = rows[:, 8:].reshape(128, WIDTH)
    qkv_rows = [group_round(qkv_rows, i) for i in range(4)]

    quarters, qkv_rows = lax.optimization_barrier((quarters, qkv_rows))
    ffn_w = lax.all_gather(jnp.stack(quarters), ("dp", "kv"))

    keys, w_kv = kernel_call(
        kv_kernel,
        "sffvvvvv",
        "ff",
        [((BLOCKS, SPAN, 128), BF16), ((128, WIDTH), BF16)],
        "keys",
        (place, x, x_other, gain_1, *qkv_rows),
        us=4,
        vmem=20,
    )
    out_rows, after = lax.optimization_barrier((out_rows, w_kv))
    out_rows = [group_round(out_rows, i) for i in range(4)]
    keys = all_to_all(keys)
    q, w_q = kernel_call(
        query_kernel,
        "sffvffffh",
        "ff",
        [((SPAN, QCOL), BF16), ((QCOL, WIDTH), BF16)],
        "queries",
        (place, x, x_other, gain_1, *qkv_rows, after),
        us=4,
        vmem=58,
    )
    o, inv = kernel_call(
        attend_kernel,
        "sfv",
        "ff",
        [((SPAN, QCOL), BF16), ((SPAN, 128), F32)],
        "attend",
        (place, q, keys),
        [
            pltpu.VMEM((GROUP, SPAN, 128), BF16),
            pltpu.VMEM((GROUP, SPAN, 128), F32),
            pltpu.VMEM((SPAN, SPAN), jnp.int32),
            pltpu.VMEM((SPAN, SPAN), jnp.int32),
        ],
        us=16,
        vmem=24,
    )
    attn_own, attn_other = kernel_call(
        attn_project_kernel,
        "sfffff",
        "vv",
        [rows_f32, rows_bf16],
        "attn_project",
        (place, *out_rows, o),
        vmem=16,
    )
    attn_other = from_core(attn_other)
    attn, resid, m_own = kernel_call(
        attn_norm_kernel,
        "vvvvv",
        "vvv",
        [rows_f32, rows_f32, rows_bf16],
        "attn_norm",
        (x, attn_own, attn_other, gain_2, gain_3),
    )

    m_parts = ring(back_z, m_own)
    m_parts[1], ffn_w = lax.optimization_barrier((m_parts[1], ffn_w))
    wide = ((SIDE * TOK, HID), BF16)
    unit_rows = ((2 * SIDE, HALF_UNITS, WIDTH), BF16)
    ffn_w = kernel_call(
        arrange_kernel,
        "sh",
        "vvv",
        [unit_rows] * 3,
        "arrange",
        (place, ffn_w),
        [pltpu.SemaphoreType.DMA((12,))],
        us=4,
    )
    gate_w, up_w, down_w = (w.reshape(HID, WIDTH) for w in ffn_w)
    ffn_scratch = [pltpu.VMEM((SIDE * TOK, WIDTH), BF16), pltpu.VMEM((SIDE * TOK, WIDTH), F32)]
    *fo_parts, gate, up = kernel_call(
        ffn_kernel,
        "vvvvvvv",
        "vvvvvv",
        [rows_f32] + [rows_bf16] * 3 + [wide, wide],
        "ffn",
        (*m_parts, gate_w, up_w, down_w),
        ffn_scratch,
        us=6,
        vmem=16,
    )
    fo_parts = ring_back(back_z, fo_parts)
    block_out, d_fo, g_gain_4 = kernel_call(
        ffn_norm_kernel, "vvvvvvv", "vvv", [rows_bf16, rows_bf16, row_f32], "ffn_norm", (*fo_parts, resid, cot, gain_4)
    )

    d_parts = ring(back_z, d_fo)
    *dm_parts, hidden, d_gate, d_up = kernel_call(
        ffn_back_kernel,
        "vvvvvvvvv",
        "vvvvvvv",
        [rows_f32] + [rows_bf16] * 3 + [wide] * 3,
        "ffn_back",
        (*d_parts, gate, up, gate_w, up_w, down_w),
        ffn_scratch,
        us=10,
        vmem=20,
    )
    dm_parts = ring_back(back_z, dm_parts)
    weight_grads, g_down = kernel_call(
        ffn_weight_kernel,
        "s" + "v" * 13,
        "fv",
        [((2 * SIDE, SIDE, TOK, WIDTH), BF16), row_f32],
        "ffn_weight",
        (place, *m_parts, *d_parts, hidden, d_gate, d_up, down_w, down_row),
        [
            pltpu.VMEM((SIDE * TOK, WIDTH), BF16),
            pltpu.VMEM((SIDE * TOK, WIDTH), BF16),
        ],
        us=8,
        vmem=20,
    )
    dm_parts, weight_grads = lax.optimization_barrier((dm_parts, weight_grads))
    weight_grads = lax.psum_scatter(weight_grads, ("dp", "kv"), scatter_dimension=0)
    d_resid, d_attn, g_gain_3, g_gain_2 = kernel_call(
        ffn_back_norm_kernel,
        "vvvvvvvvv",
        "vvvv",
        [rows_f32, rows_bf16, row_f32, row_f32],
        "ffn_back_norm",
        (*dm_parts, resid, attn, cot, gain_3, gain_2),
    )
    d_attn_other = from_core(d_attn)

    dq, key_grads = kernel_call(
        attend_back_kernel,
        "sffffffffff",
        "ff",
        [((SPAN, QCOL), BF16), ((BLOCKS, 128, SPAN), BF16)],
        "attend_back",
        (place, d_attn, d_attn_other, *out_rows, q, o, inv, keys),
        [
            pltpu.VMEM((GROUP, SPAN, 128), BF16),
            pltpu.VMEM((GROUP, SPAN, 128), F32),
            pltpu.VMEM((GROUP, SPAN, 128), BF16),
            pltpu.VMEM((128, GROUP * SPAN), BF16),
            pltpu.VMEM((SPAN, SPAN), jnp.int32),
            pltpu.VMEM((SPAN, SPAN), jnp.int32),
        ],
        us=26,
        vmem=58,
    )
    key_grads = all_to_all(key_grads)
    q_grads, after = kernel_call(
        query_grad_kernel,
        "sffffffv",
        "fv",
        [((WIDTH, WIDTH), BF16), ((8, 128), F32)],
        "query_grad",
        (place, dq, o, x, x_other, d_attn, d_attn_other, gain_1),
        [pltpu.VMEM((2 * SPAN, WIDTH), BF16)],
        us=5,
        vmem=58,
    )

    def total(parts):
        a, b, c, d = (p.astype(F32) for p in parts)
        return (a + b) + (c + d)

    q_grads, key_grads = lax.optimization_barrier((q_grads, key_grads))
    q_grads = lax.psum_scatter(q_grads.reshape(SIDE, 224, WIDTH), "dp", scatter_dimension=0)
    da_own, da_other, kv_grads, gains = kernel_call(
        project_back_kernel,
        "sffffffvvvvvv",
        "vvvv",
        [rows_f32, rows_bf16, ((128, WIDTH), BF16), ((8, WIDTH), F32)],
        "project_back",
        (place, key_grads, dq, w_q, w_kv, x, x_other, gain_1, g_gain_2, g_gain_3, g_gain_4, g_down, after),
        us=4,
        vmem=58,
    )
    weight_grads, da_other = lax.optimization_barrier((weight_grads, da_other))
    weight_grads = weight_grads.reshape(SIDE, TOK, WIDTH)
    eighth = total(ring_back(back_y, [weight_grads[k] for k in range(SIDE)])).astype(BF16)
    eighths = jnp.concatenate(ring(back_x, eighth), axis=0)

    (grad_input,) = kernel_call(
        input_norm_kernel, "vvvvv", "v", [rows_f32], "input_norm", (da_own, from_core(da_other), x, d_resid, gain_1)
    )

    gains = (gains + from_core(gains)).astype(BF16)
    kv_grads = [jnp.concatenate([kv_grads[32 * k : 32 * (k + 1)], gains], axis=0) for k in range(SIDE)]
    kv_grads = total(ring_back(back_x, kv_grads)).astype(BF16)
    gains = jnp.broadcast_to(kv_grads[None, 32:], (BLOCKS, 8, WIDTH))
    w_grads = [q_grads.reshape(BLOCKS, 14, WIDTH), kv_grads[:32].reshape(BLOCKS, 2, WIDTH), gains]
    w_grads = all_to_all(jnp.concatenate(w_grads, axis=1))
    w_grads, grad_input = lax.optimization_barrier((w_grads, grad_input))
    w_grads = jnp.sum(w_grads.astype(F32), axis=0)
    gains = w_grads[16:]
    pairs = [(2 * n + k, 2 * (2 * k + n // 2) + n % 2) for n in range(SIDE) for k in range(2)]
    grad_w = lax.ppermute(w_grads[:16], ("dp", "kv"), pairs)

    grad_code_gate, grad_code_up, grad_code_down, grad_scale_gate, grad_scale_up = kernel_call(
        finish_kernel,
        "svvvvvvv",
        "vvvvv",
        [((UNITS, WIDTH), F32)] * 3 + [((1, UNITS), F32)] * 2,
        "finish",
        (place, eighths, from_core(eighths), code_gate.T, code_up.T, gate_col, up_col, down_row),
        [pltpu.VMEM((2, 384, 128), F32), pltpu.VMEM((2 * SIDE, TOK, WIDTH), BF16)],
        us=3,
    )
    grads = (grad_code_gate, grad_code_up, grad_code_down, grad_scale_gate[0], grad_scale_up[0])

    return (
        block_out.reshape(layer_input.shape),
        grad_input.reshape(layer_input.shape),
        grad_w[:7].T,
        grad_w[14:15].T,
        grad_w[15:16].T,
        grad_w[7:14].T,
        gains[0],
        gains[1],
        gains[2],
        gains[3],
        grads[0].T,
        grads[1].T,
        *grads[2:],
        gains[4],
    )


def solution(mesh):
    tokens = P("dp", "ctx", "kv", None, None)
    columns = P(None, ("dp", "kv", "ctx"))
    hidden = (P(None, "ctx"), P(None, "ctx"), P("ctx", None), P("ctx"), P("ctx"), P())
    return jax.shard_map(
        shards,
        mesh=mesh,
        in_specs=(tokens, tokens, P("dp", None)) + (columns,) * 4 + (P(),) * 4 + hidden,
        out_specs=(tokens, tokens) + (columns,) * 4 + (P(),) * 4 + hidden,
        check_vma=False,
    )
```
